32 devices in a mesh: ex: 16 (over z, y, x), tp: 2 (over core).
Axes of the slice: x: 2, y: 2, z: 4, core: 2. Of those that a mesh axis runs over, the one named last changes fastest.
Arguments:
- tokens: bfloat16 [8192, 1024], P('ex'), may hold values from -6 to 6
- cotangent: bfloat16 [8192, 1024], P('ex'), may hold values from -6 to 6
- gain_one: float32 [1024], replicated, may hold values from 0.5 to 1.5
- w_query: bfloat16 [1024, 1024], P(None, 'tp'), may hold values from -0.1875 to 0.1875
- key_weight: bfloat16 [1024, 512], P(None, 'tp'), may hold values from -0.1875 to 0.1875
- value_weight: bfloat16 [1024, 512], P(None, 'tp'), may hold values from -0.1875 to 0.1875
- w_out: bfloat16 [1024, 1024], P('tp'), may hold values from -1.5 to 1.5
- gain_two: float32 [1024], replicated, may hold values from 0.5 to 1.5
- router: float32 [1024, 16], replicated, may hold values from -0.09375 to 0.09375
- w_gate: bfloat16 [16, 1024, 512], P('ex', None, 'tp'), may hold values from -0.1875 to 0.1875
- w_up: bfloat16 [16, 1024, 512], P('ex', None, 'tp'), may hold values from -0.1875 to 0.1875
- w_down: bfloat16 [16, 512, 1024], P('ex', 'tp'), may hold values from -1.5 to 1.5
- expert_ids: int32 [8192, 8], P('ex'), may hold values from 0 to 15, all different within a row; in each aligned block of 512 rows (0 to 511, 512 to 1023, ...) at most 512 rows name the same one
- leading_sequence_length: int32 [16], P('ex'), may hold values from 128 to 512, as said below
Outputs:
- output: bfloat16 [8192, 1024], P('ex')
- grad_tokens: bfloat16 [8192, 1024], P('ex')
- grad_gain_one: float32 [1024], replicated
- grad_query: float32 [1024, 1024], P(None, 'tp')
- grad_key: float32 [1024, 512], P(None, 'tp')
- grad_value: float32 [1024, 512], P(None, 'tp')
- grad_out_proj: float32 [1024, 1024], P('tp')
- grad_gain_two: float32 [1024], replicated
- grad_router: float32 [1024, 16], replicated
- grad_gate: float32 [16, 1024, 512], P('ex', None, 'tp')
- grad_up: float32 [16, 1024, 512], P('ex', None, 'tp')
- grad_down: float32 [16, 512, 1024], P('ex', 'tp')
The draws below stay inside these ranges and needn't reach their ends.
Inputs may be any that keep to these rules, and one draw needn't show every extreme that they name: `expert_ids`: among the 512 rows of one block of tokens, each row names 8 different experts and no expert is named by more than 512 rows. `leading_sequence_length`: the second sequence of a block holds the remaining tokens and may be empty.
All inputs are finite; a program needn't handle non-finite values.
Results may differ from the reference program's by a relative error of at most 0.024.
Values may be sent and summed in bfloat16 or wider, within the bound.
No kernel may reach another device: no remote copies, remote signals or barrier semaphores. Data moves between devices by JAX's collectives and lax.ppermute only.
A program may use at most 256 MiB of HBM per device.

```python
import math
import jax
import jax.numpy as jnp
import numpy as np
from jax import lax

MODEL_WIDTH = 1024
QUERY_HEADS = 16
KEY_VALUE_HEADS = 8
HEAD_SIZE = 64
FF = 512
TOPK = 8
TOKENS_PER_SHARD = 512
EXPERTS = 16
TOKENS = 8192
CAP = 512
N_EX = 16


def draw_leading_sequence_length(key, part):
    key = jax.random.fold_in(key, 7)
    key_length, key_spot = jax.random.split(key)
    lengths = jax.random.randint(key_length, (N_EX,), TOKENS_PER_SHARD // 4, TOKENS_PER_SHARD + 1)
    spot = jax.random.randint(key_spot, (), 0, N_EX)
    places = jnp.arange(N_EX)
    lengths = jnp.where(places == spot, TOKENS_PER_SHARD, lengths)
    lengths = jnp.where(places == (spot + 1) % N_EX, TOKENS_PER_SHARD // 4, lengths)
    return lengths.astype(jnp.int32)


def block_scale(rng, dims, cuts, smallest, largest):
    def one(position, blocks):
        draws = jax.random.uniform(jax.random.fold_in(jax.random.fold_in(rng, 6), position), (blocks,), jnp.float32, smallest / len(cuts), largest / len(cuts))
        return jnp.repeat(jnp.exp(draws), dims[position] // blocks).reshape((-1,) + (1,) * (len(dims) - position - 1))

    level = one(*cuts[0])
    for cut in cuts[1:]:
        level = level * one(*cut)
    return level


def routed_block(key, own, number, rows, amount, top, reach, lean):
    ranking = jax.random.permutation(key, amount)
    heavy_load, ordinary = shares(amount, rows * top, reach, lean, True), shares(amount, rows * top, reach, lean, False)
    places = jnp.arange(amount)

    def named(sizes, turn):
        used = int((sizes > 0).sum())
        fixed = max(1, used // 4)
        shifted = fixed + (places - fixed + turn * (used - fixed)) % max(1, amount - fixed)
        return jnp.zeros((amount,), jnp.int32).at[ranking[jnp.where(places < fixed, places, shifted)]].set(jnp.asarray(sizes, jnp.int32))

    sizes = jnp.where(number % 4 == 0, named(heavy_load, number // 4), named(ordinary, number - number // 4 - 1))
    mixed = jax.random.permutation(jax.random.fold_in(own, 3), amount)
    giver, taker = mixed[0:amount // 2 * 2:2], mixed[1:amount // 2 * 2:2]
    margin = jnp.minimum(sizes[giver] - 1, reach - sizes[taker]) // 2
    margin = jnp.where((giver == ranking[0]) | (taker == ranking[0]) | (sizes[taker] == 0), 0, jnp.maximum(margin, 0))
    shifted = jax.random.randint(jax.random.fold_in(own, 4), (amount // 2,), 0, 1 << 20) % (margin + 1)
    sizes = sizes.at[giver].add(-shifted).at[taker].add(shifted)
    members = jnp.searchsorted(jnp.cumsum(sizes), jnp.arange(rows * top), side="right").astype(jnp.int32)
    table = members.reshape(top, rows).T
    table = table[jax.random.permutation(jax.random.fold_in(own, 1), rows)]
    turn = jax.random.randint(jax.random.fold_in(own, 2), (rows, 1), 0, top)
    return jnp.take_along_axis(table, (jnp.arange(top)[None, :] + turn) % top, axis=1)


def shares(number_of, total, limit, slope, full):
    portions = [(1 << 20) // math.isqrt(standing ** slope) + 1 for standing in range(1, number_of + 1)]
    largest = limit if full else min(limit, max(-(-total // number_of), total * portions[0] // sum(portions)))
    least = 1 if total - largest >= number_of - 1 else 0
    holding, rest = [largest] + [least] * (number_of - 1), total - largest - least * (number_of - 1)
    while rest > 0:
        movable = [i for i in range(1, number_of) if holding[i] < largest] or [i for i in range(1, number_of) if holding[i] < limit]
        pool, left = sum([portions[i] for i in movable]), rest
        for i in movable:
            more = min(limit - holding[i], max(1, left * portions[i] // pool), rest)
            holding[i] = holding[i] + more
            rest = rest - more
    return np.array(holding)


def centred(stream_key, dims, deviation, reach, shards=(), kind=jnp.bfloat16):
    values = deviation * jax.random.normal(stream_key, dims, jnp.float32)
    if shards:
        values = values * block_scale(stream_key, dims, shards, -0.22, 0.18)
    return jnp.clip(values, -reach, reach).astype(kind)


def setup_inputs(seed: int = 0) -> dict:
    seeds = jax.random.split(jax.random.key(seed), 15)
    tokens = centred(seeds[0], (TOKENS, MODEL_WIDTH), 1.0, 6.0, ((0, 16),))
    cotangent = centred(seeds[1], (TOKENS, MODEL_WIDTH), 1.0, 6.0, ((0, 16),))
    gain_one = jnp.clip(1.0 + 0.1 * jax.random.normal(seeds[2], (MODEL_WIDTH,), jnp.float32), 0.5, 1.5)
    w_query = centred(seeds[3], (MODEL_WIDTH, QUERY_HEADS * HEAD_SIZE), MODEL_WIDTH ** -0.5, 0.1875, ((1, 2),))
    key_weight = centred(seeds[4], (MODEL_WIDTH, KEY_VALUE_HEADS * HEAD_SIZE), MODEL_WIDTH ** -0.5, 0.1875, ((1, 2),))
    value_weight = centred(seeds[5], (MODEL_WIDTH, KEY_VALUE_HEADS * HEAD_SIZE), MODEL_WIDTH ** -0.5, 0.1875, ((1, 2),))
    w_out = centred(seeds[6], (QUERY_HEADS * HEAD_SIZE, MODEL_WIDTH), 16 ** -0.5, 1.5, ((0, 2),))
    gain_two = jnp.clip(1.0 + 0.1 * jax.random.normal(seeds[7], (MODEL_WIDTH,), jnp.float32), 0.5, 1.5)
    router = centred(seeds[8], (MODEL_WIDTH, EXPERTS), (4 * MODEL_WIDTH) ** -0.5, 0.09375, (), jnp.float32)
    w_gate = centred(seeds[9], (EXPERTS, MODEL_WIDTH, FF), MODEL_WIDTH ** -0.5, 0.1875, ((0, 16), (2, 2)))
    w_up = centred(seeds[10], (EXPERTS, MODEL_WIDTH, FF), MODEL_WIDTH ** -0.5, 0.1875, ((0, 16), (2, 2)))
    w_down = centred(seeds[11], (EXPERTS, FF, MODEL_WIDTH), (FF // 32) ** -0.5, 1.5, ((0, 16), (1, 2)))
    expert_ids_keys = jax.random.split(jax.random.fold_in(seeds[12], 1), TOKENS // TOKENS_PER_SHARD)
    expert_ids_turns = jax.random.permutation(jax.random.fold_in(seeds[12], 3), TOKENS // TOKENS_PER_SHARD)
    expert_ids = jax.vmap(lambda own, number: routed_block(jax.random.fold_in(seeds[12], 2), own, number, TOKENS_PER_SHARD, EXPERTS, TOPK, CAP, 1))(expert_ids_keys, expert_ids_turns).reshape((TOKENS, TOPK))
    leading_sequence_length = draw_leading_sequence_length(jax.random.fold_in(seeds[14], 71), 0)
    return {"tokens": tokens, "cotangent": cotangent, "gain_one": gain_one, "w_query": w_query, "key_weight": key_weight, "value_weight": value_weight, "w_out": w_out, "gain_two": gain_two, "router": router, "w_gate": w_gate, "w_up": w_up, "w_down": w_down, "expert_ids": expert_ids, "leading_sequence_length": leading_sequence_length}


EPS = 1e-06
THETA = 10000.0
NEGATIVE = -1e+30
HIGH = lax.Precision.HIGHEST

@jax.custom_vjp
def lower_precision(v):
    return lax.optimization_barrier(v.astype(jnp.bfloat16)).astype(jnp.float32)

@jax.custom_vjp
def low_back(v):
    return v

def low_keep(v):
    return (lower_precision(v), None)

def low_pass(kept, grad):
    return (grad,)

def back_keep(v):
    return (v, None)

def back_low(kept, grad):
    return (lower_precision(grad),)
lower_precision.defvjp(low_keep, low_pass)
low_back.defvjp(back_keep, back_low)

def rms_norm(value_rows, gain):
    return value_rows * lax.rsqrt(lax.optimization_barrier(jnp.mean(value_rows * value_rows, axis=-1, keepdims=True)) + EPS) * gain

def rope_tables(length, split, width):
    index = jnp.arange(length, dtype=jnp.int32)
    second = index >= split
    place = jnp.where(second, index - split, index).astype(jnp.float32)
    freq = THETA ** (-(jnp.arange(width // 2, dtype=jnp.float32) * 2.0 / width))
    angle = place[:, None] * freq[None, :]
    return (jnp.cos(angle)[:, None, None, :], jnp.sin(angle)[:, None, None, :], second)

def apply_rotary(value_rows, cosine_table, sine_table):
    middle = value_rows.shape[-1] // 2
    front = value_rows[..., :middle]
    back = value_rows[..., middle:]
    return jnp.concatenate([front * cosine_table - back * sine_table, back * cosine_table + front * sine_table], axis=-1)

def attend_group(query_unrotated, key_unrotated, value_projected, split):
    query_group = QUERY_HEADS // KEY_VALUE_HEADS
    cosine_table, sine_table, second = rope_tables(TOKENS_PER_SHARD, split, HEAD_SIZE)
    query_rows = lower_precision(apply_rotary(query_unrotated.reshape(TOKENS_PER_SHARD, KEY_VALUE_HEADS, query_group, HEAD_SIZE), cosine_table, sine_table))
    key_rows = lower_precision(apply_rotary(key_unrotated.reshape(TOKENS_PER_SHARD, KEY_VALUE_HEADS, 1, HEAD_SIZE), cosine_table, sine_table))[:, :, 0, :]
    value_rows = value_projected.reshape(TOKENS_PER_SHARD, KEY_VALUE_HEADS, HEAD_SIZE)
    raw = jnp.einsum('qkgd,skd->kgqs', query_rows, key_rows, precision=HIGH)
    scores = low_back(raw) * float(HEAD_SIZE) ** (-0.5)
    index = jnp.arange(TOKENS_PER_SHARD, dtype=jnp.int32)
    allowed = (index[None, :] <= index[:, None]) & (second[None, :] == second[:, None])
    scores = jnp.where(allowed, scores, NEGATIVE)
    probs = lower_precision(jax.nn.softmax(scores, axis=-1))
    result = jnp.einsum('kgqs,skd->qkgd', probs, value_rows, precision=HIGH)
    return result.reshape(TOKENS_PER_SHARD, QUERY_HEADS * HEAD_SIZE)

def expert_rows(padded, token_index, gate_w, up_w, down_w):
    rows = low_back(padded[token_index])
    pre_gate = low_back(jnp.dot(rows, gate_w, precision=HIGH))
    pre_up = low_back(jnp.dot(rows, up_w, precision=HIGH))
    hidden = lower_precision(jax.nn.silu(pre_gate) * pre_up)
    return low_back(lower_precision(jnp.dot(hidden, down_w, precision=HIGH)))

def slot_tables(expert_ids):
    pairs = TOKENS * TOPK
    flat = expert_ids.reshape(N_EX, TOKENS_PER_SHARD * TOPK)
    hits = (flat[:, :, None] == jnp.arange(EXPERTS, dtype=jnp.int32)[None, None, :]).astype(jnp.int32)
    rank = lax.optimization_barrier(jnp.sum(jnp.cumsum(hits, axis=1) * hits, axis=2)) - 1
    slot_row = (jnp.arange(N_EX, dtype=jnp.int32)[:, None] * CAP + rank).reshape(pairs)
    table = jnp.full((EXPERTS, N_EX * CAP), pairs, jnp.int32)
    table = table.at[expert_ids.reshape(pairs), slot_row].set(jnp.arange(pairs, dtype=jnp.int32))
    return (table, slot_row)

def make_forward(expert_ids, leading_sequence_length):
    table, slot_row = slot_tables(expert_ids)
    token_table = (table // TOPK).astype(jnp.int32)
    flat_ids = expert_ids.reshape(TOKENS * TOPK)

    def forward(x_in, gain_one, w_query, key_weight, value_weight, w_out, gain_two, router, w_gate, w_up, w_down):
        normed = lower_precision(rms_norm(x_in, gain_one))
        query_unrotated = low_back(jnp.dot(normed, w_query, precision=HIGH))
        key_unrotated = low_back(jnp.dot(normed, key_weight, precision=HIGH))
        value_projected = lower_precision(low_back(jnp.dot(normed, value_weight, precision=HIGH)))

        def group_body(carry, pieces):
            return (carry, jax.checkpoint(attend_group)(*pieces))
        zero_start = jnp.zeros((), jnp.float32)
        unused_result, attention_output = lax.scan(group_body, zero_start, (query_unrotated.reshape(N_EX, TOKENS_PER_SHARD, QUERY_HEADS * HEAD_SIZE), key_unrotated.reshape(N_EX, TOKENS_PER_SHARD, KEY_VALUE_HEADS * HEAD_SIZE), value_projected.reshape(N_EX, TOKENS_PER_SHARD, KEY_VALUE_HEADS * HEAD_SIZE), leading_sequence_length))
        heads = low_back(lower_precision(attention_output.reshape(TOKENS, QUERY_HEADS * HEAD_SIZE)))
        mixed = x_in + low_back(jnp.dot(heads, w_out, precision=HIGH))
        normed_two = rms_norm(mixed, gain_two)
        logits = jnp.dot(normed_two, router, precision=HIGH)
        chosen = jnp.take_along_axis(logits, expert_ids, axis=1)
        gates = jax.nn.softmax(chosen, axis=-1)
        padded = jnp.concatenate([lower_precision(normed_two), jnp.zeros((1, MODEL_WIDTH), jnp.float32)], axis=0)

        def expert_step(carry, pieces):
            return (carry, jax.checkpoint(expert_rows)(padded, *pieces))
        unused_result, results = lax.scan(expert_step, zero_start, (token_table, w_gate, w_up, w_down))
        picked = results[flat_ids, slot_row].reshape(TOKENS, TOPK, MODEL_WIDTH)
        return mixed + lax.optimization_barrier(jnp.sum(gates[:, :, None] * picked, axis=1))
    return forward

def reference(tokens, cotangent, gain_one, w_query, key_weight, value_weight, w_out, gain_two, router, w_gate, w_up, w_down, expert_ids, leading_sequence_length):
    forward = make_forward(expert_ids, leading_sequence_length)
    params = (tokens.astype(jnp.float32), gain_one, w_query.astype(jnp.float32), key_weight.astype(jnp.float32), value_weight.astype(jnp.float32), w_out.astype(jnp.float32), gain_two, router, w_gate.astype(jnp.float32), w_up.astype(jnp.float32), w_down.astype(jnp.float32))
    result, pullback = jax.vjp(forward, *params)
    grads = pullback(cotangent.astype(jnp.float32))
    return (result.astype(jnp.bfloat16), grads[0].astype(jnp.bfloat16), grads[1], grads[2], grads[3], grads[4], grads[5], grads[6], grads[7], grads[8], grads[9], grads[10])
```

```python
import jax
import jax.numpy as jnp
from jax import lax
from jax.sharding import PartitionSpec as P

QUERY_HEADS = 16
KEY_VALUE_HEADS = 8
HEAD_SIZE = 64


EPS = 1e-06
THETA = 10000.0
NEGATIVE = -1e30
HIGH = lax.Precision.HIGHEST


def norm_scale(value_rows):
    return lax.rsqrt(jnp.mean(value_rows * value_rows, axis=-1, keepdims=True) + EPS)


def norm_backward(value_rows, scale, gain, grad):
    weighted = grad * gain
    inner = jnp.mean(weighted * value_rows, axis=-1, keepdims=True)
    grad_input = scale * weighted - value_rows * scale * scale * scale * inner
    grad_gain = jnp.sum(grad * value_rows * scale, axis=0)
    return (grad_input, grad_gain)


def rope_tables(length, split, width):
    index = jnp.arange(length, dtype=jnp.int32)
    second = index >= split
    place = jnp.where(second, index - split, index).astype(jnp.float32)
    freq = THETA ** (-(jnp.arange(width // 2, dtype=jnp.float32) * 2.0 / width))
    angle = place[:, None] * freq[None, :]
    return (jnp.cos(angle)[:, None, None, :], jnp.sin(angle)[:, None, None, :], second)


def apply_rotary(value_rows, cosine_table, sine_table):
    middle = value_rows.shape[-1] // 2
    front = value_rows[..., :middle]
    back = value_rows[..., middle:]
    return jnp.concatenate(
        [front * cosine_table - back * sine_table, back * cosine_table + front * sine_table],
        axis=-1,
    )


def rotate_back(grad, cosine_table, sine_table):
    middle = grad.shape[-1] // 2
    front = grad[..., :middle]
    back = grad[..., middle:]
    return jnp.concatenate(
        [front * cosine_table + back * sine_table, back * cosine_table - front * sine_table],
        axis=-1,
    )


def block_scores(query_block, key_rows, offset, second, factor):
    raw = jnp.einsum("qkgd,skd->kgqs", query_block, key_rows, preferred_element_type=jnp.float32)
    height = query_block.shape[0]
    row_index = offset + jnp.arange(height, dtype=jnp.int32)
    col_index = jnp.arange(key_rows.shape[0], dtype=jnp.int32)
    allowed = (col_index[None, :] <= row_index[:, None]) & (second[None, :] == second[:, None])
    return jnp.where(allowed, raw * factor, NEGATIVE)


BITS = (1, 2)


def swap(rows):
    return lax.ppermute(rows, "tp", [(0, 1), (1, 0)])


def tp_sum(part):
    if lax.axis_size("tp") == 2:
        return part + swap(part)
    return lax.psum(part, "tp")


def own_first(rows):
    if lax.axis_size("tp") == 2:
        half = rows.shape[0] // 2
        place = lax.axis_index("tp")
        own = lax.dynamic_slice_in_dim(rows, place * half, half, 0)
        other = lax.dynamic_slice_in_dim(rows, (1 - place) * half, half, 0)
        return (own, jnp.concatenate([own, other], axis=0))
    share = rows.shape[0] // lax.axis_size("tp")
    own = lax.dynamic_slice_in_dim(rows, lax.axis_index("tp") * share, share, 0)
    return (own, rows)


def flip_columns(values):
    if lax.axis_size("tp") == 2:
        half = values.shape[-1] // 2
        turned = jnp.concatenate([values[..., half:], values[..., :half]], axis=-1)
        return jnp.where(lax.axis_index("tp") == 0, values, turned)
    return values


def join_halves(own):
    if lax.axis_size("tp") == 2:
        return jnp.concatenate([own, swap(own)], axis=0)
    return lax.all_gather(own, "tp", axis=0, tiled=True)


def sum_halves(part):
    if lax.axis_size("tp") == 2:
        half = part.shape[0] // 2
        return part[:half] + swap(part[half:])
    return lax.psum_scatter(part, "tp", scatter_dimension=0, tiled=True)


def absolute_rows(own):
    if lax.axis_size("tp") == 2:
        other = swap(own)
        first = lax.axis_index("tp") == 0
        return jnp.concatenate(
            [jnp.where(first, own, other), jnp.where(first, other, own)], axis=0
        )
    return lax.all_gather(own, "tp", axis=0, tiled=True)


def group_pairs(turn):
    ex = lax.axis_size("ex")
    tp = lax.axis_size("tp")
    pairs = []
    for place in range(ex):
        for core in range(tp):
            bit = BITS[(turn + core) % 2]
            pairs.append((place * tp + core, (place ^ bit) * tp + core))
    return pairs


def group_swap(value_rows, turn):
    return lax.ppermute(value_rows, ("ex", "tp"), group_pairs(turn))


def line_shift(value_rows, step):
    ex = lax.axis_size("ex")
    moved = 4 * step
    return lax.ppermute(value_rows, "ex", [(place, (place - moved) % ex) for place in range(ex)])


def group_gather(value_rows):
    for turn in range(2):
        value_rows = jnp.concatenate([value_rows, group_swap(value_rows, turn)], axis=-1)
    return value_rows


def group_scatter(value_rows):
    for turn in (1, 0):
        half = value_rows.shape[-1] // 2
        sent = group_swap(value_rows[..., half:].astype(jnp.bfloat16), turn)
        value_rows = value_rows[..., :half] + sent.astype(jnp.float32)
    return value_rows


def group_bit(turn):
    bit = jnp.where((lax.axis_index("tp") + turn) % 2 == 0, BITS[0], BITS[1])
    return ((lax.axis_index("ex") & bit) != 0).astype(jnp.int32)


def everywhere_sum(value_rows):
    planes = lax.axis_size("ex") // 4
    for turn in (1, 0):
        half = value_rows.shape[0] // 2
        bit = group_bit(turn)
        kept = lax.dynamic_slice_in_dim(value_rows, bit * half, half, 0)
        sent = lax.dynamic_slice_in_dim(value_rows, (1 - bit) * half, half, 0)
        sent = group_swap(sent.astype(jnp.bfloat16), turn)
        value_rows = kept + sent.astype(jnp.float32)
    share = value_rows.shape[0] // planes
    plane = lax.axis_index("ex") // 4
    low = value_rows.astype(jnp.bfloat16)
    total = lax.dynamic_slice_in_dim(value_rows, plane * share, share, 0)
    for step in range(1, planes):
        target = lax.rem(plane + planes - step, planes)
        piece = lax.dynamic_slice_in_dim(low, target * share, share, 0)
        total = total + line_shift(piece, step).astype(jnp.float32)
    total = total.astype(jnp.bfloat16)
    value_rows = lax.dynamic_update_slice_in_dim(low, total, plane * share, 0)
    for step in range(1, planes):
        source = lax.rem(plane + step, planes)
        value_rows = lax.dynamic_update_slice_in_dim(
            value_rows, line_shift(total, step), source * share, 0
        )
    for turn in range(2):
        first = group_bit(turn) == 0
        other = group_swap(value_rows, turn)
        value_rows = jnp.concatenate(
            [jnp.where(first, value_rows, other), jnp.where(first, other, value_rows)], axis=0
        )
    return value_rows


def shards(
    tokens,
    cotangent,
    gain_one,
    w_query,
    key_weight,
    value_weight,
    w_out,
    gain_two,
    router,
    w_gate,
    w_up,
    w_down,
    expert_ids,
    leading_sequence_length,
):
    length = tokens.shape[0]
    width = tokens.shape[1]
    experts = router.shape[1]
    planes = lax.axis_size("ex") // 4
    plane = lax.axis_index("ex") // 4
    member = lax.axis_index("ex") % 4
    odd = lax.axis_index("tp") % 2
    query_group = QUERY_HEADS // KEY_VALUE_HEADS
    kv_local = key_weight.shape[1] // HEAD_SIZE
    q_width = w_query.shape[1]
    units = w_gate.shape[2]
    factor = float(HEAD_SIZE) ** (-0.5)
    low = jnp.bfloat16
    f32 = jnp.float32

    expert_weights = group_gather(jnp.stack([w_gate[0], w_up[0], w_down[0].T], axis=0))
    gate_w = expert_weights[0]
    up_w = expert_weights[1]
    down_w = expert_weights[2]
    grad_held = [own_first(cotangent)]
    for step in range(1, planes):
        arrived = line_shift(grad_held[-1][0], 1)
        grad_held.append((arrived, join_halves(arrived)))

    x_full = tokens.astype(f32)
    scale_one = norm_scale(x_full)
    normed_one = (x_full * scale_one * gain_one).astype(low)
    cosine_table, sine_table, second = rope_tables(length, leading_sequence_length[0], HEAD_SIZE)
    query_pre = jnp.dot(normed_one, w_query, preferred_element_type=f32).reshape(
        length, kv_local, query_group, HEAD_SIZE
    )
    query_rows = apply_rotary(query_pre, cosine_table, sine_table).astype(low)
    key_pre = jnp.dot(normed_one, key_weight, preferred_element_type=f32).reshape(
        length, kv_local, 1, HEAD_SIZE
    )
    key_rows = apply_rotary(key_pre, cosine_table, sine_table).astype(low)[:, :, 0, :]
    value_rows = (
        jnp.dot(normed_one, value_weight, preferred_element_type=f32)
        .astype(low)
        .reshape(length, kv_local, HEAD_SIZE)
    )
    scores = block_scores(query_rows, key_rows, 0, second, factor)
    largest = jnp.max(scores, axis=-1, keepdims=True)
    weights = jnp.exp(scores - largest)
    total = jnp.sum(weights, axis=-1, keepdims=True)
    probs = (weights / total).astype(low)
    log_totals = (largest + jnp.log(total))[..., 0]
    heads = (
        jnp.einsum("kgqs,skd->qkgd", probs, value_rows, preferred_element_type=f32)
        .astype(low)
        .reshape(length, q_width)
    )
    mixed = x_full + tp_sum(jnp.dot(heads, w_out, preferred_element_type=f32))
    scale_two = norm_scale(mixed)
    normed_two = mixed * scale_two * gain_two
    routed = normed_two.astype(low)
    logits = lax.dot_general(router, normed_two, (((0,), (1,)), ((), ())), precision=HIGH)
    expert_iota = jnp.arange(experts, dtype=jnp.int32)
    chosen = jnp.any(expert_ids.T[None, :, :] == expert_iota[:, None, None], axis=1)
    masked = jnp.where(chosen, logits, NEGATIVE)
    gate_weights = jnp.where(chosen, jnp.exp(masked - jnp.max(masked, axis=0, keepdims=True)), 0.0)
    gates = gate_weights / jnp.sum(gate_weights, axis=0, keepdims=True)

    gates_high = gates.astype(low)
    gates_rest = (gates - gates_high.astype(f32)).astype(low)
    extra = jnp.concatenate([gates_high, gates_rest], axis=1)
    extra = jnp.pad(extra, ((0, 0), (0, width - extra.shape[1])))
    own_routed, own_block = own_first(routed)
    payload = jnp.concatenate([own_routed, extra], axis=0)
    share = own_routed.shape[0]
    blocks = [(own_block, gates)]
    for step in range(1, planes):
        payload = line_shift(payload, 1)
        sent_gates = payload[share:].astype(f32)
        blocks.append(
            (
                join_halves(payload[:share]),
                sent_gates[:, :length] + sent_gates[:, length : 2 * length],
            )
        )

    slots = jnp.arange(4, dtype=jnp.int32)
    flipped = (slots % 2) * 2 + slots // 2
    slot_member = jnp.where(odd == 1, flipped, slots) ^ member
    slot_expert = plane * 4 + slot_member
    placed = (expert_iota[:, None] == slot_expert[None, :]).astype(f32)

    def expert_block(rows, grads, block_gates):
        pre_gate = jnp.dot(rows, gate_w, preferred_element_type=f32)
        pre_up = jnp.dot(rows, up_w, preferred_element_type=f32)
        grad_plain = jnp.dot(grads, down_w, preferred_element_type=f32)
        slot_gates = jnp.sum(
            placed[:, :, None] * flip_columns(block_gates)[:, None, :], axis=0
        ).T
        wide_gates = jnp.broadcast_to(slot_gates[:, :, None], (length, 4, units)).reshape(
            length, 4 * units
        )
        sigmoid = jax.nn.sigmoid(pre_gate)
        activated = pre_gate * sigmoid
        hidden = activated * pre_up
        gate_part = jnp.sum((hidden * grad_plain).reshape(length, 4, units), axis=-1).T
        gate_part = flip_columns(jnp.sum(placed[:, :, None] * gate_part[None, :, :], axis=1))
        hidden = (hidden * wide_gates).astype(low)
        grad_hidden = grad_plain * wide_gates
        grad_pre_gate = (
            grad_hidden * pre_up * sigmoid * (1.0 + pre_gate * (1.0 - sigmoid))
        ).astype(low)
        grad_pre_up = (grad_hidden * activated).astype(low)
        back = lax.dot_general(
            grad_pre_gate, gate_w, (((1,), (1,)), ((), ())), preferred_element_type=f32
        ) + lax.dot_general(
            grad_pre_up, up_w, (((1,), (1,)), ((), ())), preferred_element_type=f32
        )
        front = lax.dot_general(
            hidden, down_w, (((1,), (1,)), ((), ())), preferred_element_type=f32
        )
        return (back.astype(low), front.astype(low), gate_part, hidden, grad_pre_gate, grad_pre_up)

    results = [
        expert_block(blocks[step][0], grad_held[step][1], blocks[step][1])
        for step in range(planes)
    ]

    def packed_back(step):
        back, front, gate_part, *unused = results[step]
        part_high = gate_part.astype(low)
        part_rest = (gate_part - part_high.astype(f32)).astype(low)
        rest = jnp.concatenate([part_high, part_rest], axis=1)
        rest = jnp.pad(rest, ((0, 0), (0, width - rest.shape[1])))
        return jnp.concatenate([sum_halves(back), rest], axis=0)

    def line_sum(pieces):
        running = None
        for step in range(1, planes):
            piece = pieces(step)
            running = piece if running is None else running + piece
            running = line_shift(running, 1)
        last = pieces(0)
        return last if running is None else running + last

    back_sum = line_sum(packed_back)
    grad_moe = absolute_rows(back_sum[:share]).astype(f32)
    gate_sum = back_sum[share:].astype(f32)
    gate_grads = tp_sum(gate_sum[:, :length] + gate_sum[:, length : 2 * length])

    grad_out = cotangent.astype(f32)
    grad_logits = gates * (gate_grads - jnp.sum(gates * gate_grads, axis=0, keepdims=True))
    grad_router = lax.dot_general(
        normed_two, grad_logits, (((0,), (1,)), ((), ())), precision=HIGH
    )
    grad_normed_two = grad_moe + lax.dot_general(
        grad_logits, router, (((0,), (1,)), ((), ())), precision=HIGH
    )
    grad_mixed_norm, grad_gain_two = norm_backward(mixed, scale_two, gain_two, grad_normed_two)
    grad_mixed = grad_out + grad_mixed_norm
    grad_attended = grad_mixed.astype(low)

    def packed_front(step):
        return sum_halves(fronts[step])

    fronts = [results[step][1] for step in range(planes)]
    fronts = list(lax.optimization_barrier((*fronts, back_sum))[:planes])
    front_sum = line_sum(packed_front)
    output = (mixed + absolute_rows(front_sum).astype(f32)).astype(low)

    all_rows = jnp.concatenate([block[0] for block in blocks], axis=0)
    all_grads = jnp.concatenate([held[1] for held in grad_held], axis=0)
    all_hidden = jnp.concatenate([result[3] for result in results], axis=0)
    all_gate = jnp.concatenate([result[4] for result in results], axis=0)
    all_up = jnp.concatenate([result[5] for result in results], axis=0)

    def over_rows(left, right):
        return lax.dot_general(left, right, (((0,), (0,)), ((), ())), preferred_element_type=f32)

    expert_grads = group_scatter(
        jnp.stack(
            [
                over_rows(all_rows, all_gate),
                over_rows(all_rows, all_up),
                over_rows(all_grads, all_hidden),
            ],
            axis=0,
        )
    )

    grad_out_proj = over_rows(heads, grad_attended)
    grad_out_proj = everywhere_sum(grad_out_proj).astype(f32)
    grad_heads = jnp.einsum("td,hd->th", grad_attended, w_out, preferred_element_type=f32)
    grad_heads = grad_heads.astype(low).reshape(length, kv_local, query_group, HEAD_SIZE)
    scores = block_scores(query_rows, key_rows, 0, second, factor)
    probs = jnp.exp(scores - log_totals[..., None])
    probs_low = probs.astype(low)
    grad_probs = jnp.einsum("qkgd,skd->kgqs", grad_heads, value_rows, preferred_element_type=f32)
    inner = jnp.sum(probs * grad_probs, axis=-1, keepdims=True)
    grad_scores = (probs * (grad_probs - inner) * factor).astype(low)
    grad_queries = jnp.einsum("kgqs,skd->qkgd", grad_scores, key_rows, preferred_element_type=f32)
    grad_keys = jnp.einsum("kgqs,qkgd->skd", grad_scores, query_rows, preferred_element_type=f32)
    grad_values = jnp.einsum("kgqs,qkgd->skd", probs_low, grad_heads, preferred_element_type=f32)
    grad_queries = rotate_back(grad_queries, cosine_table, sine_table)
    grad_queries = grad_queries.astype(low).reshape(length, q_width)
    grad_keys_pre = (
        rotate_back(grad_keys[:, :, None, :], cosine_table, sine_table)
        .astype(low)
        .reshape(length, kv_local * HEAD_SIZE)
    )
    grad_values_low = grad_values.astype(low).reshape(length, kv_local * HEAD_SIZE)
    grad_three = jnp.concatenate([grad_queries, grad_keys_pre, grad_values_low], axis=1)
    three_weights = jnp.concatenate([w_query, key_weight, value_weight], axis=1)
    grad_normed_one = lax.dot_general(
        grad_three, three_weights, (((1,), (1,)), ((), ())), preferred_element_type=f32
    )
    grad_normed_one = tp_sum(grad_normed_one.astype(low)).astype(f32)
    weight_grads = everywhere_sum(over_rows(normed_one, grad_three)).astype(f32)
    grad_input_norm, grad_gain_one = norm_backward(x_full, scale_one, gain_one, grad_normed_one)
    grad_tokens = (grad_mixed + grad_input_norm).astype(low)
    grad_gain_one, grad_gain_two, grad_router = (
        lax.psum(grad_gain_one, "ex"),
        lax.psum(grad_gain_two, "ex"),
        lax.psum(grad_router, "ex"),
    )
    key_end = q_width + key_weight.shape[1]
    return (
        output,
        grad_tokens,
        grad_gain_one,
        weight_grads[:, :q_width],
        weight_grads[:, q_width:key_end],
        weight_grads[:, key_end:],
        grad_out_proj,
        grad_gain_two,
        grad_router,
        expert_grads[0][None],
        expert_grads[1][None],
        expert_grads[2].T[None],
    )


def solution(mesh):
    placed = (
        P("ex", None),
        P("ex", None),
        P(),
        P(None, "tp"),
        P(None, "tp"),
        P(None, "tp"),
        P("tp", None),
        P(),
        P(),
        P("ex", None, "tp"),
        P("ex", None, "tp"),
        P("ex", "tp", None),
        P("ex", None),
        P("ex"),
    )
    return jax.shard_map(
        shards,
        mesh=mesh,
        in_specs=placed,
        out_specs=(
            P("ex", None),
            P("ex", None),
            P(),
            P(None, "tp"),
            P(None, "tp"),
            P(None, "tp"),
            P("tp", None),
            P(),
            P(),
            P("ex", None, "tp"),
            P("ex", None, "tp"),
            P("ex", "tp", None),
        ),
        check_vma=False,
    )
```

```python
import functools

import jax
import jax.numpy as jnp
from jax import lax
from jax.experimental import pallas as pl
from jax.experimental.pallas import tpu as pltpu
from jax.sharding import PartitionSpec as P

QUERY_HEADS = 16
KEY_VALUE_HEADS = 8
HEAD_SIZE = 64


EPS = 1e-06
THETA = 10000.0
NEGATIVE = -1e30
HIGH = lax.Precision.HIGHEST


def norm_scale(value_rows):
    return lax.rsqrt(jnp.mean(value_rows * value_rows, axis=-1, keepdims=True) + EPS)


def norm_backward(value_rows, scale, gain, grad):
    weighted = grad * gain
    inner = jnp.mean(weighted * value_rows, axis=-1, keepdims=True)
    grad_input = scale * weighted - value_rows * scale * scale * scale * inner
    grad_gain = jnp.sum(grad * value_rows * scale, axis=0)
    return (grad_input, grad_gain)


def rope_tables(length, split, width):
    index = jnp.arange(length, dtype=jnp.int32)
    second = index >= split
    place = jnp.where(second, index - split, index).astype(jnp.float32)
    freq = THETA ** (-(jnp.arange(width // 2, dtype=jnp.float32) * 2.0 / width))
    angle = place[:, None] * freq[None, :]
    return (jnp.cos(angle)[:, None, None, :], jnp.sin(angle)[:, None, None, :], second)


def apply_rotary(value_rows, cosine_table, sine_table):
    middle = value_rows.shape[-1] // 2
    front = value_rows[..., :middle]
    back = value_rows[..., middle:]
    return jnp.concatenate(
        [front * cosine_table - back * sine_table, back * cosine_table + front * sine_table],
        axis=-1,
    )


def rotate_back(grad, cosine_table, sine_table):
    middle = grad.shape[-1] // 2
    front = grad[..., :middle]
    back = grad[..., middle:]
    return jnp.concatenate(
        [front * cosine_table + back * sine_table, back * cosine_table - front * sine_table],
        axis=-1,
    )


def block_scores(query_block, key_rows, offset, second, factor):
    raw = jnp.einsum("qkgd,skd->kgqs", query_block, key_rows, preferred_element_type=jnp.float32)
    height = query_block.shape[0]
    row_index = offset + jnp.arange(height, dtype=jnp.int32)
    col_index = jnp.arange(key_rows.shape[0], dtype=jnp.int32)
    allowed = (col_index[None, :] <= row_index[:, None]) & (second[None, :] == second[:, None])
    return jnp.where(allowed, raw * factor, NEGATIVE)


BITS = (1, 2)


def swap(rows):
    return lax.ppermute(rows, "tp", [(0, 1), (1, 0)])


def tp_sum(part):
    if lax.axis_size("tp") == 2:
        return part + swap(part)
    return lax.psum(part, "tp")


def own_half(rows):
    share = rows.shape[0] // lax.axis_size("tp")
    return lax.dynamic_slice_in_dim(rows, lax.axis_index("tp") * share, share, 0)


def two_halves(own):
    if lax.axis_size("tp") == 2:
        return (own, swap(own))
    whole = lax.all_gather(own, "tp", axis=0, tiled=True)
    half = whole.shape[0] // 2
    return (whole[:half], whole[half:])


def sum_halves(kept, sent):
    if lax.axis_size("tp") == 2:
        return kept + swap(sent)
    whole = jnp.concatenate([kept, sent], axis=0)
    return lax.psum_scatter(whole, "tp", scatter_dimension=0, tiled=True)


def absolute_rows(own):
    if lax.axis_size("tp") == 2:
        other = swap(own)
        first = lax.axis_index("tp") == 0
        return jnp.concatenate(
            [jnp.where(first, own, other), jnp.where(first, other, own)], axis=0
        )
    return lax.all_gather(own, "tp", axis=0, tiled=True)


def group_pairs(turn):
    ex = lax.axis_size("ex")
    tp = lax.axis_size("tp")
    pairs = []
    for place in range(ex):
        for core in range(tp):
            bit = BITS[(turn + core) % 2]
            pairs.append((place * tp + core, (place ^ bit) * tp + core))
    return pairs


def group_swap(value_rows, turn):
    return lax.ppermute(value_rows, ("ex", "tp"), group_pairs(turn))


def line_shift(value_rows, step):
    ex = lax.axis_size("ex")
    moved = 4 * step
    return lax.ppermute(value_rows, "ex", [(place, (place - moved) % ex) for place in range(ex)])


def group_gather(value_rows):
    for turn in range(2):
        value_rows = jnp.concatenate([value_rows, group_swap(value_rows, turn)], axis=-1)
    return value_rows


def group_bit(turn):
    bit = jnp.where((lax.axis_index("tp") + turn) % 2 == 0, BITS[0], BITS[1])
    return ((lax.axis_index("ex") & bit) != 0).astype(jnp.int32)


def everywhere_sum(value_rows):
    planes = lax.axis_size("ex") // 4
    for turn in (1, 0):
        half = value_rows.shape[0] // 2
        bit = group_bit(turn)
        kept = lax.dynamic_slice_in_dim(value_rows, bit * half, half, 0)
        sent = lax.dynamic_slice_in_dim(value_rows, (1 - bit) * half, half, 0)
        sent = group_swap(sent.astype(jnp.bfloat16), turn)
        value_rows = kept + sent.astype(jnp.float32)
    share = value_rows.shape[0] // planes
    plane = lax.axis_index("ex") // 4
    low = value_rows.astype(jnp.bfloat16)
    total = lax.dynamic_slice_in_dim(value_rows, plane * share, share, 0)
    for step in range(1, planes):
        target = lax.rem(plane + planes - step, planes)
        piece = lax.dynamic_slice_in_dim(low, target * share, share, 0)
        total = total + line_shift(piece, step).astype(jnp.float32)
    total = total.astype(jnp.bfloat16)
    value_rows = lax.dynamic_update_slice_in_dim(low, total, plane * share, 0)
    for step in range(1, planes):
        source = lax.rem(plane + step, planes)
        value_rows = lax.dynamic_update_slice_in_dim(
            value_rows, line_shift(total, step), source * share, 0
        )
    for turn in range(2):
        first = group_bit(turn) == 0
        other = group_swap(value_rows, turn)
        value_rows = jnp.concatenate(
            [jnp.where(first, value_rows, other), jnp.where(first, other, value_rows)], axis=0
        )
    return value_rows


def over_rows(left, right):
    return lax.dot_general(
        left, right, (((0,), (0,)), ((), ())), preferred_element_type=jnp.float32
    )


def over_last(left, right):
    return lax.dot_general(
        left, right, (((1,), (1,)), ((), ())), preferred_element_type=jnp.float32
    )


def expert_kernel(
    held,
    places,
    own_rows,
    other_rows,
    own_grads,
    other_grads,
    gates,
    weights,
    *rest,
):
    (
        rows_out,
        grads_out,
        hidden_out,
        gate_out,
        up_out,
        back_kept,
        back_sent,
        front_kept,
        front_sent,
        part_out,
        back_total,
        front_total,
        gate_columns,
        part_columns,
    ) = rest[-14:]
    slot = pl.program_id(0)
    core = places[4]
    half = own_rows.shape[0]
    length = 2 * half
    experts = gates.shape[0]
    mine = pl.multiple_of(core * half, half)
    theirs = pl.multiple_of((1 - core) * half, half)
    lanes = lax.broadcasted_iota(jnp.int32, (length, 128), 1)

    @pl.when(slot == 0)
    def begin():
        rows_out[0, pl.ds(mine, half), :] = own_rows[...]
        rows_out[0, pl.ds(theirs, half), :] = other_rows[...]
        grads_out[0, pl.ds(mine, half), :] = own_grads[...]
        grads_out[0, pl.ds(theirs, half), :] = other_grads[...]
        padded = jnp.concatenate(
            [gates[...], jnp.zeros((128 - experts, length), jnp.float32)], axis=0
        )
        gate_columns[...] = padded.T
        part_columns[...] = jnp.zeros_like(part_columns)
        back_total[...] = jnp.zeros_like(back_total)
        front_total[...] = jnp.zeros_like(front_total)

    columns = weights.shape[2]
    spot = lax.broadcasted_iota(jnp.int32, (1, columns), 1) // (columns // held)
    gate = 0.0
    for index in range(held):
        chosen = lanes == places[slot * held + index]
        column = jnp.sum(jnp.where(chosen, gate_columns[...], 0.0), axis=1, keepdims=True)
        gate = gate + (column if held == 1 else jnp.where(spot == index, column, 0.0))
    rows = rows_out[0]
    grads = grads_out[0]
    pre_gate = jnp.dot(rows, weights[0], preferred_element_type=jnp.float32)
    pre_up = jnp.dot(rows, weights[1], preferred_element_type=jnp.float32)
    grad_plain = jnp.dot(grads, weights[2], preferred_element_type=jnp.float32)
    sigmoid = jax.nn.sigmoid(pre_gate)
    activated = pre_gate * sigmoid
    hidden = activated * pre_up
    product = hidden * grad_plain
    for index in range(held):
        part = product if held == 1 else jnp.where(spot == index, product, 0.0)
        part = jnp.sum(part, axis=1, keepdims=True)
        part_columns[...] += jnp.where(lanes == places[slot * held + index], part, 0.0)
    hidden_low = (hidden * gate).astype(jnp.bfloat16)
    grad_hidden = grad_plain * gate
    gate_low = (grad_hidden * pre_up * (sigmoid * (1.0 + pre_gate * (1.0 - sigmoid)))).astype(
        jnp.bfloat16
    )
    up_low = (grad_hidden * activated).astype(jnp.bfloat16)
    hidden_out[0] = hidden_low
    gate_out[0] = gate_low
    up_out[0] = up_low
    back_total[...] += over_last(gate_low, weights[0]) + over_last(up_low, weights[1])
    front_total[...] += over_last(hidden_low, weights[2])

    @pl.when(slot == pl.num_programs(0) - 1)
    def finish():
        back_kept[...] = back_total[pl.ds(mine, half), :].astype(jnp.bfloat16)
        back_sent[...] = back_total[pl.ds(theirs, half), :].astype(jnp.bfloat16)
        front_kept[...] = front_total[pl.ds(mine, half), :].astype(jnp.bfloat16)
        front_sent[...] = front_total[pl.ds(theirs, half), :].astype(jnp.bfloat16)
        part_out[...] = part_columns[...].T[:experts]


def expert_block(places, halves, grad_halves, gates, weights, number, blocks, kept):
    half, width = halves[0].shape
    length = 2 * half
    experts = gates.shape[0]
    steps = min(4, weights.shape[2] // 128)
    units = weights.shape[2] // steps
    low = jnp.bfloat16
    whole = lambda shape: pl.BlockSpec(shape, lambda slot, places: (0, 0))
    shapes = [(length, width)] * 2 + [(length, steps * units)] * 3
    out_specs = [
        pl.BlockSpec((1, length, width), lambda slot, places: (number, 0, 0)),
        pl.BlockSpec((1, length, width), lambda slot, places: (number, 0, 0)),
    ] + [pl.BlockSpec((1, length, units), lambda slot, places: (number, 0, slot))] * 3
    out_specs = out_specs + [whole((half, width))] * 4 + [whole((experts, length))]
    out_shape = [jax.ShapeDtypeStruct((blocks,) + shape, low) for shape in shapes]
    out_shape = out_shape + [jax.ShapeDtypeStruct((half, width), low)] * 4
    out_shape = out_shape + [jax.ShapeDtypeStruct((experts, length), jnp.float32)]
    in_specs = [whole((half, width))] * 4 + [
        whole((experts, length)),
        pl.BlockSpec((3, width, units), lambda slot, places: (0, 0, slot)),
    ]
    in_specs = in_specs + [pl.BlockSpec(memory_space=pl.ANY)] * len(kept)
    return pl.pallas_call(
        functools.partial(expert_kernel, 4 // steps),
        out_shape=out_shape,
        grid_spec=pltpu.PrefetchScalarGridSpec(
            num_scalar_prefetch=1,
            grid=(steps,),
            in_specs=in_specs,
            out_specs=out_specs,
            scratch_shapes=[
                pltpu.VMEM((length, width), jnp.float32),
                pltpu.VMEM((length, width), jnp.float32),
                pltpu.VMEM((length, 128), jnp.float32),
                pltpu.VMEM((length, 128), jnp.float32),
            ],
        ),
        input_output_aliases={7 + index: index for index in range(len(kept))},
        compiler_params=pltpu.CompilerParams(vmem_limit_bytes=56 * 1024 * 1024),
        cost_estimate=pl.CostEstimate(flops=1000000, bytes_accessed=1000000, transcendentals=0),
        name="expert_block",
    )(places, *halves, *grad_halves, gates, weights, *kept)


def shards(
    tokens,
    cotangent,
    gain_one,
    w_query,
    key_weight,
    value_weight,
    w_out,
    gain_two,
    router,
    w_gate,
    w_up,
    w_down,
    expert_ids,
    leading_sequence_length,
):
    length = tokens.shape[0]
    width = tokens.shape[1]
    experts = router.shape[1]
    planes = lax.axis_size("ex") // 4
    plane = lax.axis_index("ex") // 4
    member = lax.axis_index("ex") % 4
    odd = lax.axis_index("tp") % 2
    query_group = QUERY_HEADS // KEY_VALUE_HEADS
    kv_local = key_weight.shape[1] // HEAD_SIZE
    q_width = w_query.shape[1]
    units = w_gate.shape[2]
    factor = float(HEAD_SIZE) ** (-0.5)
    low = jnp.bfloat16
    f32 = jnp.float32

    expert_weights = group_gather(jnp.stack([w_gate[0], w_up[0], w_down[0].T], axis=0))
    grad_own = own_half(cotangent)
    grad_halves = [line_shift(grad_own, step) if step else grad_own for step in range(planes)]
    grad_halves = [two_halves(half) for half in grad_halves]

    x_full = tokens.astype(f32)
    scale_one = norm_scale(x_full)
    normed_one = (x_full * scale_one * gain_one).astype(low)
    cosine_table, sine_table, second = rope_tables(length, leading_sequence_length[0], HEAD_SIZE)
    query_pre = jnp.dot(normed_one, w_query, preferred_element_type=f32).reshape(
        length, kv_local, query_group, HEAD_SIZE
    )
    query_rows = apply_rotary(query_pre, cosine_table, sine_table).astype(low)
    key_pre = jnp.dot(normed_one, key_weight, preferred_element_type=f32).reshape(
        length, kv_local, 1, HEAD_SIZE
    )
    key_rows = apply_rotary(key_pre, cosine_table, sine_table).astype(low)[:, :, 0, :]
    value_rows = (
        jnp.dot(normed_one, value_weight, preferred_element_type=f32)
        .astype(low)
        .reshape(length, kv_local, HEAD_SIZE)
    )
    scores = block_scores(query_rows, key_rows, 0, second, factor)
    largest = jnp.max(scores, axis=-1, keepdims=True)
    weights = jnp.exp(scores - largest)
    total = jnp.sum(weights, axis=-1, keepdims=True)
    probs = (weights / total).astype(low)
    log_totals = (largest + jnp.log(total))[..., 0]
    heads = (
        jnp.einsum("kgqs,skd->qkgd", probs, value_rows, preferred_element_type=f32)
        .astype(low)
        .reshape(length, q_width)
    )
    mixed = x_full + tp_sum(jnp.dot(heads, w_out, preferred_element_type=f32))
    scale_two = norm_scale(mixed)
    normed_two = mixed * scale_two * gain_two
    routed = normed_two.astype(low)
    logits = lax.dot_general(router, normed_two, (((0,), (1,)), ((), ())), precision=HIGH)
    expert_iota = jnp.arange(experts, dtype=jnp.int32)
    chosen = jnp.any(expert_ids.T[None, :, :] == expert_iota[:, None, None], axis=1)
    masked = jnp.where(chosen, logits, NEGATIVE)
    gate_weights = jnp.where(chosen, jnp.exp(masked - jnp.max(masked, axis=0, keepdims=True)), 0.0)
    gates = gate_weights / jnp.sum(gate_weights, axis=0, keepdims=True)

    gates_high = gates.astype(low)
    gates_rest = (gates - gates_high.astype(f32)).astype(low)
    extra = jnp.concatenate([gates_high, gates_rest], axis=1)
    extra = jnp.pad(extra, ((0, 0), (0, width - extra.shape[1])))
    own_routed = own_half(routed)
    payload = jnp.concatenate([own_routed, extra], axis=0)
    share = own_routed.shape[0]
    blocks = [(two_halves(own_routed), gates)]
    for step in range(1, planes):
        arrived = line_shift(payload, step)
        sent_gates = arrived[share:].astype(f32)
        blocks.append(
            (
                two_halves(arrived[:share]),
                sent_gates[:, :length] + sent_gates[:, length : 2 * length],
            )
        )

    slots = jnp.arange(4, dtype=jnp.int32)
    flipped = (slots % 2) * 2 + slots // 2
    slot_member = jnp.where(odd == 1, flipped, slots) ^ member
    core = odd if lax.axis_size("tp") == 2 else jnp.zeros_like(odd)
    places = jnp.concatenate([plane * 4 + slot_member, core[None]]).astype(jnp.int32)

    kept = ()
    backs = {}
    fronts = {}
    for step in range(planes):
        results = expert_block(
            places, blocks[step][0], grad_halves[step], blocks[step][1],
            expert_weights, step, planes, kept,
        )
        kept = results[:5]
        part = results[9]
        part_high = part.astype(low)
        part_rest = (part - part_high.astype(f32)).astype(low)
        rest = jnp.concatenate([part_high, part_rest], axis=1)
        rest = jnp.pad(rest, ((0, 0), (0, width - rest.shape[1])))
        backs[step] = jnp.concatenate([sum_halves(results[5], results[6]), rest], axis=0)
        fronts[step] = (results[7], results[8])

    def line_sum(pieces):
        total = pieces[0].astype(f32)
        for step in range(1, planes):
            total = total + line_shift(pieces[step], planes - step).astype(f32)
        return total

    back_sum = line_sum(backs)
    grad_moe = absolute_rows(back_sum[:share].astype(low)).astype(f32)
    gate_sum = back_sum[share:]
    gate_grads = tp_sum(gate_sum[:, :length] + gate_sum[:, length : 2 * length])

    grad_out = cotangent.astype(f32)
    grad_logits = gates * (gate_grads - jnp.sum(gates * gate_grads, axis=0, keepdims=True))
    grad_router = lax.dot_general(
        normed_two, grad_logits, (((0,), (1,)), ((), ())), precision=HIGH
    )
    grad_normed_two = grad_moe + lax.dot_general(
        grad_logits, router, (((0,), (1,)), ((), ())), precision=HIGH
    )
    grad_mixed_norm, grad_gain_two = norm_backward(mixed, scale_two, gain_two, grad_normed_two)
    grad_mixed = grad_out + grad_mixed_norm
    grad_attended = grad_mixed.astype(low)

    front_sum = line_sum({step: sum_halves(*fronts[step]) for step in range(planes)})
    output = (mixed + absolute_rows(front_sum.astype(low)).astype(f32)).astype(low)

    all_rows, all_grads, all_hidden, all_gate, all_up = [
        value.reshape(planes * length, value.shape[2]) for value in kept
    ]

    def expert_grad(left, right):
        half = right.shape[1] // 2
        sent = group_swap(over_rows(left, right[:, half:]).astype(low), 1)
        held = over_rows(left, right[:, :half]) + sent.astype(f32)
        half = half // 2
        sent = group_swap(held[:, half:].astype(low), 0)
        return held[:, :half] + sent.astype(f32)

    expert_grads = (
        expert_grad(all_rows, all_gate),
        expert_grad(all_rows, all_up),
        expert_grad(all_grads, all_hidden),
    )

    grad_out_proj = over_rows(heads, grad_attended)
    shared_grads = everywhere_sum(
        jnp.concatenate(
            [
                grad_out_proj,
                grad_router.T,
                grad_gain_two[None],
                jnp.zeros((127 - experts, width), f32),
            ],
            axis=0,
        )
    ).astype(f32)
    grad_out_proj = shared_grads[:q_width]
    grad_router = shared_grads[q_width : q_width + experts].T
    grad_gain_two = shared_grads[q_width + experts]
    grad_heads = jnp.einsum("td,hd->th", grad_attended, w_out, preferred_element_type=f32)
    grad_heads = grad_heads.astype(low).reshape(length, kv_local, query_group, HEAD_SIZE)
    scores = block_scores(query_rows, key_rows, 0, second, factor)
    probs = jnp.exp(scores - log_totals[..., None])
    probs_low = probs.astype(low)
    grad_probs = jnp.einsum("qkgd,skd->kgqs", grad_heads, value_rows, preferred_element_type=f32)
    inner = jnp.sum(probs * grad_probs, axis=-1, keepdims=True)
    grad_scores = (probs * (grad_probs - inner) * factor).astype(low)
    grad_queries = jnp.einsum("kgqs,skd->qkgd", grad_scores, key_rows, preferred_element_type=f32)
    grad_keys = jnp.einsum("kgqs,qkgd->skd", grad_scores, query_rows, preferred_element_type=f32)
    grad_values = jnp.einsum("kgqs,qkgd->skd", probs_low, grad_heads, preferred_element_type=f32)
    grad_queries = rotate_back(grad_queries, cosine_table, sine_table)
    grad_queries = grad_queries.astype(low).reshape(length, q_width)
    grad_keys_pre = (
        rotate_back(grad_keys[:, :, None, :], cosine_table, sine_table)
        .astype(low)
        .reshape(length, kv_local * HEAD_SIZE)
    )
    grad_values_low = grad_values.astype(low).reshape(length, kv_local * HEAD_SIZE)
    grad_three = jnp.concatenate([grad_queries, grad_keys_pre, grad_values_low], axis=1)
    three_weights = jnp.concatenate([w_query, key_weight, value_weight], axis=1)
    grad_normed_one = lax.dot_general(
        grad_three, three_weights, (((1,), (1,)), ((), ())), preferred_element_type=f32
    )
    grad_normed_one = tp_sum(grad_normed_one.astype(low)).astype(f32)
    weight_grads = everywhere_sum(over_rows(normed_one, grad_three)).astype(f32)
    grad_input_norm, unused_grad = norm_backward(x_full, scale_one, gain_one, grad_normed_one)
    grad_tokens = (grad_mixed + grad_input_norm).astype(low)
    grad_gain_one = tp_sum(jnp.sum(three_weights.astype(f32) * weight_grads, axis=1)) / gain_one
    key_end = q_width + key_weight.shape[1]
    return (
        output,
        grad_tokens,
        grad_gain_one,
        weight_grads[:, :q_width],
        weight_grads[:, q_width:key_end],
        weight_grads[:, key_end:],
        grad_out_proj,
        grad_gain_two,
        grad_router,
        expert_grads[0][None],
        expert_grads[1][None],
        expert_grads[2].T[None],
    )


def solution(mesh):
    placed = (
        P("ex", None),
        P("ex", None),
        P(),
        P(None, "tp"),
        P(None, "tp"),
        P(None, "tp"),
        P("tp", None),
        P(),
        P(),
        P("ex", None, "tp"),
        P("ex", None, "tp"),
        P("ex", "tp", None),
        P("ex", None),
        P("ex"),
    )
    return jax.shard_map(
        shards,
        mesh=mesh,
        in_specs=placed,
        out_specs=(
            P("ex", None),
            P("ex", None),
            P(),
            P(None, "tp"),
            P(None, "tp"),
            P(None, "tp"),
            P("tp", None),
            P(),
            P(),
            P("ex", None, "tp"),
            P("ex", None, "tp"),
            P("ex", "tp", None),
        ),
        check_vma=False,
    )
```

```python
import functools

import jax
import jax.numpy as jnp
from jax import lax
from jax.experimental import pallas as pl
from jax.experimental.pallas import tpu as pltpu
from jax.sharding import PartitionSpec as P

HEAD_SIZE = 64


EPS = 1e-06
THETA = 10000.0
NEGATIVE = -1e30
HIGH = lax.Precision.HIGHEST


def norm_scale(value_rows):
    return lax.rsqrt(jnp.mean(value_rows * value_rows, axis=-1, keepdims=True) + EPS)


def norm_backward(value_rows, scale, gain, grad):
    weighted = grad * gain
    inner = jnp.mean(weighted * value_rows, axis=-1, keepdims=True)
    grad_input = scale * weighted - value_rows * scale * scale * scale * inner
    grad_gain = jnp.sum(grad * value_rows * scale, axis=0)
    return (grad_input, grad_gain)


def rope_tables(length, split, width):
    index = jnp.arange(length, dtype=jnp.int32)
    place = jnp.where(index >= split, index - split, index).astype(jnp.float32)
    freq = THETA ** (-(jnp.arange(width // 2, dtype=jnp.float32) * 2.0 / width))
    angle = place[:, None] * freq[None, :]
    cosine = jnp.cos(angle)
    sine = jnp.sin(angle)
    return (
        jnp.concatenate([cosine] * 4, axis=1),
        jnp.concatenate([-sine, sine, -sine, sine], axis=1),
    )


BITS = (1, 2)


def swap(rows):
    return lax.ppermute(rows, "tp", [(0, 1), (1, 0)])


def tp_sum(part):
    if lax.axis_size("tp") == 2:
        return part + swap(part)
    return lax.psum(part, "tp")


def own_half(rows):
    share = rows.shape[0] // lax.axis_size("tp")
    return lax.dynamic_slice_in_dim(rows, lax.axis_index("tp") * share, share, 0)


def two_halves(own):
    if lax.axis_size("tp") == 2:
        return (own, swap(own))
    whole = lax.all_gather(own, "tp", axis=0, tiled=True)
    half = whole.shape[0] // 2
    return (whole[:half], whole[half:])


def sum_halves(kept, sent):
    if lax.axis_size("tp") == 2:
        return kept + swap(sent)
    whole = jnp.concatenate([kept, sent], axis=0)
    return lax.psum_scatter(whole, "tp", scatter_dimension=0, tiled=True)


def absolute_rows(own):
    if lax.axis_size("tp") == 2:
        other = swap(own)
        first = lax.axis_index("tp") == 0
        return jnp.concatenate(
            [jnp.where(first, own, other), jnp.where(first, other, own)], axis=0
        )
    return lax.all_gather(own, "tp", axis=0, tiled=True)


def group_pairs(turn):
    ex = lax.axis_size("ex")
    tp = lax.axis_size("tp")
    pairs = []
    for place in range(ex):
        for core in range(tp):
            bit = BITS[(turn + core) % 2]
            pairs.append((place * tp + core, (place ^ bit) * tp + core))
    return pairs


def group_swap(value_rows, turn):
    return lax.ppermute(value_rows, ("ex", "tp"), group_pairs(turn))


def line_shift(value_rows, step):
    ex = lax.axis_size("ex")
    moved = 4 * step
    return lax.ppermute(value_rows, "ex", [(place, (place - moved) % ex) for place in range(ex)])


def line_gather(value_rows):
    planes = lax.axis_size("ex") // 4
    if planes != 4:
        return [line_shift(value_rows, step) if step else value_rows for step in range(planes)]
    following = line_shift(value_rows, 1)
    return [value_rows, following, line_shift(following, 1), line_shift(value_rows, 3)]


def group_gather(value_rows):
    for turn in range(2):
        value_rows = jnp.concatenate([value_rows, group_swap(value_rows, turn)], axis=-1)
    return value_rows


def group_bit(turn):
    bit = jnp.where((lax.axis_index("tp") + turn) % 2 == 0, BITS[0], BITS[1])
    return ((lax.axis_index("ex") & bit) != 0).astype(jnp.int32)


def everywhere_sum(value_rows):
    planes = lax.axis_size("ex") // 4
    for turn in (1, 0):
        half = value_rows.shape[0] // 2
        bit = group_bit(turn)
        kept = lax.dynamic_slice_in_dim(value_rows, bit * half, half, 0)
        sent = lax.dynamic_slice_in_dim(value_rows, (1 - bit) * half, half, 0)
        sent = group_swap(sent.astype(jnp.bfloat16), turn)
        value_rows = kept + sent.astype(jnp.float32)
    share = value_rows.shape[0] // planes
    plane = lax.axis_index("ex") // 4
    low = value_rows.astype(jnp.bfloat16)
    total = lax.dynamic_slice_in_dim(value_rows, plane * share, share, 0)
    for step in range(1, planes):
        target = lax.rem(plane + planes - step, planes)
        piece = lax.dynamic_slice_in_dim(low, target * share, share, 0)
        total = total + line_shift(piece, step).astype(jnp.float32)
    total = total.astype(jnp.bfloat16)
    value_rows = lax.dynamic_update_slice_in_dim(low, total, plane * share, 0)
    for step in range(1, planes):
        source = lax.rem(plane + step, planes)
        value_rows = lax.dynamic_update_slice_in_dim(
            value_rows, line_shift(total, step), source * share, 0
        )
    for turn in range(2):
        first = group_bit(turn) == 0
        other = group_swap(value_rows, turn)
        value_rows = jnp.concatenate(
            [jnp.where(first, value_rows, other), jnp.where(first, other, value_rows)], axis=0
        )
    return value_rows


def over_rows(left, right):
    return lax.dot_general(
        left, right, (((0,), (0,)), ((), ())), preferred_element_type=jnp.float32
    )


def over_last(left, right):
    return lax.dot_general(
        left, right, (((1,), (1,)), ((), ())), preferred_element_type=jnp.float32
    )


def half_turn(block):
    lanes = lax.broadcasted_iota(jnp.int32, block.shape, 1)
    return jnp.where(lanes % 64 < 32, pltpu.roll(block, 96, 1), pltpu.roll(block, 32, 1))


def both_halves(block, which):
    lanes = lax.broadcasted_iota(jnp.int32, block.shape, 1)
    turned = pltpu.roll(block, 64, 1)
    return jnp.where((lanes < 64) == (which == 0), block, turned)


def set_mask(split, mask):
    keys = lax.broadcasted_iota(jnp.int32, mask.shape, 0)
    queries = lax.broadcasted_iota(jnp.int32, mask.shape, 1)
    allowed = (keys <= queries) & ((keys >= split) | (queries < split))
    mask[...] = jnp.where(allowed, 0.0, NEGATIVE)


def attention_kernel(
    split,
    tokens,
    gain,
    w_query,
    key_weight,
    value_weight,
    w_out,
    cosine,
    sine,
    normed_out,
    query_out,
    key_out,
    value_out,
    heads_out,
    totals_out,
    part_out,
    mask,
):
    length = tokens.shape[0]
    factor = float(HEAD_SIZE) ** (-0.5)
    f32 = jnp.float32
    low = jnp.bfloat16
    set_mask(split[0], mask)
    rows = tokens[...].astype(f32)
    normed = (rows * norm_scale(rows) * gain[...]).astype(low)
    normed_out[...] = normed
    query = jnp.dot(normed, w_query[...], preferred_element_type=f32)
    key = jnp.dot(normed, key_weight[...], preferred_element_type=f32)
    value = jnp.dot(normed, value_weight[...], preferred_element_type=f32)
    value_out[...] = value.astype(low)
    keys = []
    turned_values = []
    for index in range(key.shape[1] // 128):
        block = key[:, index * 128 : (index + 1) * 128]
        block = (block * cosine[...] + half_turn(block) * sine[...]).astype(low)
        key_out[:, index * 128 : (index + 1) * 128] = block
        keys.append(block.astype(f32))
        turned_values.append(value[:, index * 128 : (index + 1) * 128].T.astype(low))
    lanes = lax.broadcasted_iota(jnp.int32, (length, 128), 1)
    tile = length // 2
    for index in range(query.shape[1] // 128):
        block = query[:, index * 128 : (index + 1) * 128]
        block = block * cosine[...] + half_turn(block) * sine[...]
        query_out[:, index * 128 : (index + 1) * 128] = block.astype(low)
        shared = both_halves(keys[index // 2], index % 2).astype(low)
        turned = turned_values[index // 2][index % 2 * 64 : index % 2 * 64 + 64]
        columns = []
        for place in range(2):
            masked = jnp.where((lanes < 64) == (place == 0), block, 0.0).astype(low)
            pieces = []
            for number in range(2):
                start, end = number * tile, (number + 1) * tile
                scores = over_last(shared[:end], masked[start:end])
                scores = scores * factor + mask[:end, start:end]
                largest = jnp.max(scores, axis=0, keepdims=True)
                weights = jnp.exp(scores - largest)
                total = jnp.sum(weights, axis=0, keepdims=True)
                probs = (weights * (1.0 / total)).astype(low)
                pieces.append(jnp.dot(turned[:, :end], probs, preferred_element_type=f32))
                totals_out[2 * index + place : 2 * index + place + 1, start:end] = (
                    largest + jnp.log(total)
                )
            columns.append(jnp.concatenate(pieces, axis=1))
        heads = jnp.concatenate(columns, axis=0).T
        heads_out[:, index * 128 : (index + 1) * 128] = heads.astype(low)
    part_out[...] = jnp.dot(heads_out[...], w_out[...], preferred_element_type=f32)


def attention(split, tokens, gain, w_query, key_weight, value_weight, w_out, cosine, sine):
    length, width = tokens.shape
    q_width = w_query.shape[1]
    k_width = key_weight.shape[1]
    low = jnp.bfloat16
    whole = pl.BlockSpec(memory_space=pltpu.VMEM)
    return pl.pallas_call(
        attention_kernel,
        out_shape=[
            jax.ShapeDtypeStruct((length, width), low),
            jax.ShapeDtypeStruct((length, q_width), low),
            jax.ShapeDtypeStruct((length, k_width), low),
            jax.ShapeDtypeStruct((length, k_width), low),
            jax.ShapeDtypeStruct((length, q_width), low),
            jax.ShapeDtypeStruct((q_width // HEAD_SIZE, length), jnp.float32),
            jax.ShapeDtypeStruct((length, width), jnp.float32),
        ],
        in_specs=[pl.BlockSpec(memory_space=pltpu.SMEM)] + [whole] * 8,
        out_specs=[whole] * 7,
        scratch_shapes=[pltpu.VMEM((length, length), jnp.float32)],
        compiler_params=pltpu.CompilerParams(vmem_limit_bytes=48 * 1024 * 1024),
        cost_estimate=pl.CostEstimate(flops=1000000, bytes_accessed=1000000, transcendentals=0),
        name="attention",
    )(split, tokens, gain, w_query, key_weight, value_weight, w_out, cosine, sine)


def attention_grad_kernel(
    split,
    query,
    key,
    value,
    grad_heads,
    totals,
    cosine,
    sine,
    grad_out,
    mask,
):
    length = query.shape[0]
    factor = float(HEAD_SIZE) ** (-0.5)
    f32 = jnp.float32
    low = jnp.bfloat16
    set_mask(split[0], mask)
    lanes = lax.broadcasted_iota(jnp.int32, (length, 128), 1)
    tile = length // 2
    q_width = query.shape[1]
    k_width = key.shape[1]

    def turn_back(block):
        return (block * cosine[...] - half_turn(block) * sine[...]).astype(low)

    held = None
    for index in range(q_width // 128):
        block = query[:, index * 128 : (index + 1) * 128].astype(f32)
        grads = grad_heads[:, index * 128 : (index + 1) * 128].astype(f32)
        pair = slice(index // 2 * 128, index // 2 * 128 + 128)
        key_block = key[:, pair].astype(f32)
        keys = both_halves(key_block, index % 2).astype(low)
        values = both_halves(value[:, pair].astype(f32), index % 2).astype(low)
        turned = key_block.T[index % 2 * 64 : index % 2 * 64 + 64].astype(low)
        columns = []
        grad_key = [0.0, 0.0]
        grad_value = [0.0, 0.0]
        for place in range(2):
            mine = (lanes < 64) == (place == 0)
            masked = jnp.where(mine, block, 0.0).astype(low)
            masked_grads = jnp.where(mine, grads, 0.0).astype(low)
            pieces = []
            for number in range(2):
                start, end = number * tile, (number + 1) * tile
                part = masked[start:end]
                part_grads = masked_grads[start:end]
                scores = over_last(keys[:end], part) * factor + mask[:end, start:end]
                spot = 2 * index + place
                probs = jnp.exp(scores - totals[spot : spot + 1, start:end])
                grad_probs = over_last(values[:end], part_grads)
                inner = jnp.sum(probs * grad_probs, axis=0, keepdims=True)
                grad_scores = (probs * (grad_probs - inner) * factor).astype(low)
                pieces.append(jnp.dot(turned[:, :end], grad_scores, preferred_element_type=f32))
                some_value = jnp.dot(probs.astype(low), part_grads, preferred_element_type=f32)
                some_key = jnp.dot(grad_scores, part, preferred_element_type=f32)
                for row in range(number + 1):
                    cut = slice(row * tile, (row + 1) * tile)
                    grad_value[row] = grad_value[row] + some_value[cut]
                    grad_key[row] = grad_key[row] + some_key[cut]
            columns.append(jnp.concatenate(pieces, axis=1))
        grad_query = jnp.concatenate(columns, axis=0).T
        grad_out[:, index * 128 : (index + 1) * 128] = turn_back(grad_query)
        sums = []
        for total in (grad_key, grad_value):
            total = jnp.concatenate(total, axis=0)
            sums.append(total + pltpu.roll(total, 64, 1))
        if index % 2 == 1:
            sums = [jnp.where(lanes < 64, old, new) for old, new in zip(held, sums)]
        held = sums
        if index % 2 == 1 or index == q_width // 128 - 1:
            left = q_width + index // 2 * 128
            grad_out[:, left : left + 128] = turn_back(sums[0])
            grad_out[:, left + k_width : left + k_width + 128] = sums[1].astype(low)


def attention_grad(split, query, key, value, grad_heads, totals, cosine, sine):
    length, q_width = query.shape
    whole = pl.BlockSpec(memory_space=pltpu.VMEM)
    return pl.pallas_call(
        attention_grad_kernel,
        out_shape=jax.ShapeDtypeStruct((length, q_width + 2 * key.shape[1]), jnp.bfloat16),
        in_specs=[pl.BlockSpec(memory_space=pltpu.SMEM)] + [whole] * 7,
        out_specs=whole,
        scratch_shapes=[pltpu.VMEM((length, length), jnp.float32)],
        compiler_params=pltpu.CompilerParams(vmem_limit_bytes=48 * 1024 * 1024),
        cost_estimate=pl.CostEstimate(flops=1000000, bytes_accessed=1000000, transcendentals=0),
        name="attention_grad",
    )(split, query, key, value, grad_heads, totals, cosine, sine)


def expert_kernel(
    held,
    places,
    own_rows,
    other_rows,
    own_grads,
    other_grads,
    gates,
    weights,
    *rest,
):
    (
        rows_out,
        grads_out,
        hidden_out,
        gate_out,
        up_out,
        back_kept,
        back_sent,
        front_kept,
        front_sent,
        part_out,
        back_total,
        front_total,
        gate_columns,
        part_columns,
    ) = rest[-14:]
    slot = pl.program_id(0)
    core = places[4]
    half = own_rows.shape[0]
    length = 2 * half
    experts = gates.shape[0]
    mine = pl.multiple_of(core * half, half)
    theirs = pl.multiple_of((1 - core) * half, half)
    lanes = lax.broadcasted_iota(jnp.int32, (length, 128), 1)

    @pl.when(slot == 0)
    def begin():
        rows_out[0, pl.ds(mine, half), :] = own_rows[...]
        rows_out[0, pl.ds(theirs, half), :] = other_rows[...]
        grads_out[0, pl.ds(mine, half), :] = own_grads[...]
        grads_out[0, pl.ds(theirs, half), :] = other_grads[...]
        padded = jnp.concatenate(
            [gates[...], jnp.zeros((128 - experts, length), jnp.float32)], axis=0
        )
        gate_columns[...] = padded.T
        part_columns[...] = jnp.zeros_like(part_columns)
        back_total[...] = jnp.zeros_like(back_total)
        front_total[...] = jnp.zeros_like(front_total)

    columns = weights.shape[2]
    spot = lax.broadcasted_iota(jnp.int32, (1, columns), 1) // (columns // held)
    gate = 0.0
    for index in range(held):
        chosen = lanes == places[slot * held + index]
        column = jnp.sum(jnp.where(chosen, gate_columns[...], 0.0), axis=1, keepdims=True)
        gate = gate + (column if held == 1 else jnp.where(spot == index, column, 0.0))
    rows = rows_out[0]
    grads = grads_out[0]
    pre_gate = jnp.dot(rows, weights[0], preferred_element_type=jnp.float32)
    pre_up = jnp.dot(rows, weights[1], preferred_element_type=jnp.float32)
    grad_plain = jnp.dot(grads, weights[2], preferred_element_type=jnp.float32)
    sigmoid = jax.nn.sigmoid(pre_gate)
    activated = pre_gate * sigmoid
    hidden = activated * pre_up
    product = hidden * grad_plain
    for index in range(held):
        part = product if held == 1 else jnp.where(spot == index, product, 0.0)
        part = jnp.sum(part, axis=1, keepdims=True)
        part_columns[...] += jnp.where(lanes == places[slot * held + index], part, 0.0)
    hidden_low = (hidden * gate).astype(jnp.bfloat16)
    grad_hidden = grad_plain * gate
    gate_low = (grad_hidden * pre_up * (sigmoid * (1.0 + pre_gate * (1.0 - sigmoid)))).astype(
        jnp.bfloat16
    )
    up_low = (grad_hidden * activated).astype(jnp.bfloat16)
    hidden_out[0] = hidden_low
    gate_out[0] = gate_low
    up_out[0] = up_low
    back_total[...] += over_last(gate_low, weights[0]) + over_last(up_low, weights[1])
    front_total[...] += over_last(hidden_low, weights[2])

    @pl.when(slot == pl.num_programs(0) - 1)
    def finish():
        back_kept[...] = back_total[pl.ds(mine, half), :].astype(jnp.bfloat16)
        back_sent[...] = back_total[pl.ds(theirs, half), :].astype(jnp.bfloat16)
        front_kept[...] = front_total[pl.ds(mine, half), :].astype(jnp.bfloat16)
        front_sent[...] = front_total[pl.ds(theirs, half), :].astype(jnp.bfloat16)
        part_out[...] = part_columns[...].T[:experts]


def expert_block(places, halves, grad_halves, gates, weights, number, blocks, kept):
    half, width = halves[0].shape
    length = 2 * half
    experts = gates.shape[0]
    steps = min(4, weights.shape[2] // 128)
    units = weights.shape[2] // steps
    low = jnp.bfloat16
    whole = lambda shape: pl.BlockSpec(shape, lambda slot, places: (0, 0))
    shapes = [(length, width)] * 2 + [(length, steps * units)] * 3
    out_specs = [
        pl.BlockSpec((1, length, width), lambda slot, places: (number, 0, 0)),
        pl.BlockSpec((1, length, width), lambda slot, places: (number, 0, 0)),
    ] + [pl.BlockSpec((1, length, units), lambda slot, places: (number, 0, slot))] * 3
    out_specs = out_specs + [whole((half, width))] * 4 + [whole((experts, length))]
    out_shape = [jax.ShapeDtypeStruct((blocks,) + shape, low) for shape in shapes]
    out_shape = out_shape + [jax.ShapeDtypeStruct((half, width), low)] * 4
    out_shape = out_shape + [jax.ShapeDtypeStruct((experts, length), jnp.float32)]
    in_specs = [whole((half, width))] * 4 + [
        whole((experts, length)),
        pl.BlockSpec((3, width, units), lambda slot, places: (0, 0, slot)),
    ]
    in_specs = in_specs + [pl.BlockSpec(memory_space=pl.ANY)] * len(kept)
    return pl.pallas_call(
        functools.partial(expert_kernel, 4 // steps),
        out_shape=out_shape,
        grid_spec=pltpu.PrefetchScalarGridSpec(
            num_scalar_prefetch=1,
            grid=(steps,),
            in_specs=in_specs,
            out_specs=out_specs,
            scratch_shapes=[
                pltpu.VMEM((length, width), jnp.float32),
                pltpu.VMEM((length, width), jnp.float32),
                pltpu.VMEM((length, 128), jnp.float32),
                pltpu.VMEM((length, 128), jnp.float32),
            ],
        ),
        input_output_aliases={7 + index: index for index in range(len(kept))},
        compiler_params=pltpu.CompilerParams(vmem_limit_bytes=56 * 1024 * 1024),
        cost_estimate=pl.CostEstimate(
            flops=16000000000, bytes_accessed=16000000, transcendentals=0
        ),
        name="expert_block",
    )(places, *halves, *grad_halves, gates, weights, *kept)


def shards(
    tokens,
    cotangent,
    gain_one,
    w_query,
    key_weight,
    value_weight,
    w_out,
    gain_two,
    router,
    w_gate,
    w_up,
    w_down,
    expert_ids,
    leading_sequence_length,
):
    length = tokens.shape[0]
    width = tokens.shape[1]
    experts = router.shape[1]
    planes = lax.axis_size("ex") // 4
    plane = lax.axis_index("ex") // 4
    member = lax.axis_index("ex") % 4
    odd = lax.axis_index("tp") % 2
    q_width = w_query.shape[1]
    low = jnp.bfloat16
    f32 = jnp.float32

    expert_weights = group_gather(jnp.stack([w_gate[0], w_up[0], w_down[0].T], axis=0))
    grad_own = own_half(cotangent)
    grad_halves = line_gather(grad_own)
    grad_halves = [two_halves(half) for half in grad_halves]

    cosine, sine = rope_tables(length, leading_sequence_length[0], HEAD_SIZE)
    k_width = key_weight.shape[1]
    filler = -k_width % 128
    wide_key = jnp.pad(key_weight, ((0, 0), (0, filler)))
    wide_value = jnp.pad(value_weight, ((0, 0), (0, filler)))
    normed_one, query_rows, key_rows, value_rows, heads, log_totals, part = attention(
        leading_sequence_length, tokens, gain_one[None], w_query, wide_key, wide_value, w_out,
        cosine, sine,
    )
    x_full = tokens.astype(f32)
    scale_one = norm_scale(x_full)
    mixed = x_full + tp_sum(part)
    scale_two = norm_scale(mixed)
    normed_two = mixed * scale_two * gain_two
    routed = normed_two.astype(low)
    logits = lax.dot_general(router, normed_two, (((0,), (1,)), ((), ())), precision=HIGH)
    expert_iota = jnp.arange(experts, dtype=jnp.int32)
    chosen = jnp.any(expert_ids.T[None, :, :] == expert_iota[:, None, None], axis=1)
    masked = jnp.where(chosen, logits, NEGATIVE)
    gate_weights = jnp.where(chosen, jnp.exp(masked - jnp.max(masked, axis=0, keepdims=True)), 0.0)
    gates = gate_weights / jnp.sum(gate_weights, axis=0, keepdims=True)

    gates_high = gates.astype(low)
    gates_rest = (gates - gates_high.astype(f32)).astype(low)
    extra = jnp.concatenate([gates_high, gates_rest], axis=1)
    extra = jnp.pad(extra, ((0, 0), (0, width - extra.shape[1])))
    own_routed = own_half(routed)
    payload = jnp.concatenate([own_routed, extra], axis=0)
    share = own_routed.shape[0]
    blocks = [(two_halves(own_routed), gates)]
    for arrived in line_gather(payload)[1:]:
        sent_gates = arrived[share:].astype(f32)
        blocks.append(
            (
                two_halves(arrived[:share]),
                sent_gates[:, :length] + sent_gates[:, length : 2 * length],
            )
        )

    slots = jnp.arange(4, dtype=jnp.int32)
    flipped = (slots % 2) * 2 + slots // 2
    slot_member = jnp.where(odd == 1, flipped, slots) ^ member
    core = odd if lax.axis_size("tp") == 2 else jnp.zeros_like(odd)
    places = jnp.concatenate([plane * 4 + slot_member, core[None]]).astype(jnp.int32)

    kept = ()
    backs = {}
    fronts = {}
    for step in range(planes):
        results = expert_block(
            places, blocks[step][0], grad_halves[step], blocks[step][1],
            expert_weights, step, planes, kept,
        )
        kept = results[:5]
        part = results[9]
        part_high = part.astype(low)
        part_rest = (part - part_high.astype(f32)).astype(low)
        rest = jnp.concatenate([part_high, part_rest], axis=1)
        rest = jnp.pad(rest, ((0, 0), (0, width - rest.shape[1])))
        backs[step] = jnp.concatenate([sum_halves(results[5], results[6]), rest], axis=0)
        fronts[step] = (results[7], results[8])

    def line_sum(pieces):
        total = pieces[0].astype(f32)
        for step in range(1, planes):
            total = total + line_shift(pieces[step], planes - step).astype(f32)
        return total

    back_sum = line_sum(backs)
    grad_moe = absolute_rows(back_sum[:share].astype(low)).astype(f32)
    gate_sum = back_sum[share:]
    gate_grads = tp_sum(gate_sum[:, :length] + gate_sum[:, length : 2 * length])

    grad_out = cotangent.astype(f32)
    grad_logits = gates * (gate_grads - jnp.sum(gates * gate_grads, axis=0, keepdims=True))
    grad_router = lax.dot_general(
        normed_two, grad_logits, (((0,), (1,)), ((), ())), precision=HIGH
    )
    grad_normed_two = grad_moe + lax.dot_general(
        grad_logits, router, (((0,), (1,)), ((), ())), precision=HIGH
    )
    grad_mixed_norm, grad_gain_two = norm_backward(mixed, scale_two, gain_two, grad_normed_two)
    grad_mixed = grad_out + grad_mixed_norm
    grad_attended = grad_mixed.astype(low)

    front_sum = line_sum({step: sum_halves(*fronts[step]) for step in range(planes)})
    output = (mixed + absolute_rows(front_sum.astype(low)).astype(f32)).astype(low)

    all_rows, all_grads, all_hidden, all_gate, all_up = [
        value.reshape(planes * length, value.shape[2]) for value in kept
    ]

    def expert_grad(left, right):
        half = right.shape[1] // 2
        sent = group_swap(over_rows(left, right[:, half:]).astype(low), 1)
        held = over_rows(left, right[:, :half]) + sent.astype(f32)
        half = half // 2
        sent = group_swap(held[:, half:].astype(low), 0)
        return held[:, :half] + sent.astype(f32)

    expert_grads = (
        expert_grad(all_rows, all_gate),
        expert_grad(all_rows, all_up),
        expert_grad(all_grads, all_hidden),
    )

    grad_out_proj = over_rows(heads, grad_attended)
    shared_grads = everywhere_sum(
        jnp.concatenate(
            [
                grad_out_proj,
                grad_router.T,
                grad_gain_two[None],
                jnp.zeros((127 - experts, width), f32),
            ],
            axis=0,
        )
    ).astype(f32)
    grad_out_proj = shared_grads[:q_width]
    grad_router = shared_grads[q_width : q_width + experts].T
    grad_gain_two = shared_grads[q_width + experts]
    grad_heads = jnp.einsum("td,hd->th", grad_attended, w_out, preferred_element_type=f32)
    grad_three = attention_grad(
        leading_sequence_length, query_rows, key_rows, value_rows, grad_heads.astype(low),
        log_totals, cosine, sine,
    )
    three_weights = jnp.concatenate([w_query, wide_key, wide_value], axis=1)
    grad_normed_one = lax.dot_general(
        grad_three, three_weights, (((1,), (1,)), ((), ())), preferred_element_type=f32
    )
    grad_normed_one = tp_sum(grad_normed_one.astype(low)).astype(f32)
    weight_grads = over_rows(normed_one, grad_three)
    middle = width // 2
    weight_grads = jnp.concatenate(
        [everywhere_sum(weight_grads[:middle]), everywhere_sum(weight_grads[middle:])], axis=0
    ).astype(f32)
    grad_input_norm, unused_grad = norm_backward(x_full, scale_one, gain_one, grad_normed_one)
    grad_tokens = (grad_mixed + grad_input_norm).astype(low)
    grad_gain_one = tp_sum(jnp.sum(three_weights.astype(f32) * weight_grads, axis=1)) / gain_one
    key_start = q_width
    value_start = q_width + k_width + filler
    return (
        output,
        grad_tokens,
        grad_gain_one,
        weight_grads[:, :q_width],
        weight_grads[:, key_start : key_start + k_width],
        weight_grads[:, value_start : value_start + k_width],
        grad_out_proj,
        grad_gain_two,
        grad_router,
        expert_grads[0][None],
        expert_grads[1][None],
        expert_grads[2].T[None],
    )


def solution(mesh):
    placed = (
        P("ex", None),
        P("ex", None),
        P(),
        P(None, "tp"),
        P(None, "tp"),
        P(None, "tp"),
        P("tp", None),
        P(),
        P(),
        P("ex", None, "tp"),
        P("ex", None, "tp"),
        P("ex", "tp", None),
        P("ex", None),
        P("ex"),
    )
    return jax.shard_map(
        shards,
        mesh=mesh,
        in_specs=placed,
        out_specs=(
            P("ex", None),
            P("ex", None),
            P(),
            P(None, "tp"),
            P(None, "tp"),
            P(None, "tp"),
            P("tp", None),
            P(),
            P(),
            P("ex", None, "tp"),
            P("ex", None, "tp"),
            P("ex", "tp", None),
        ),
        check_vma=False,
    )
```

```python
import functools

import jax
import jax.numpy as jnp
from jax import lax
from jax.experimental import pallas as pl
from jax.experimental.pallas import tpu as pltpu
from jax.sharding import PartitionSpec as P

HEAD_SIZE = 64


EPS = 1e-06
THETA = 10000.0
NEGATIVE = -1e30
HIGH = lax.Precision.HIGHEST


def norm_scale(value_rows):
    return lax.rsqrt(jnp.mean(value_rows * value_rows, axis=-1, keepdims=True) + EPS)


def norm_backward(value_rows, scale, gain, grad):
    weighted = grad * gain
    inner = jnp.mean(weighted * value_rows, axis=-1, keepdims=True)
    grad_input = scale * weighted - value_rows * scale * scale * scale * inner
    grad_gain = jnp.sum(grad * value_rows * scale, axis=0)
    return (grad_input, grad_gain)


def rope_tables(length, split, width):
    index = jnp.arange(length, dtype=jnp.int32)
    place = jnp.where(index >= split, index - split, index).astype(jnp.float32)
    freq = THETA ** (-(jnp.arange(width // 2, dtype=jnp.float32) * 2.0 / width))
    angle = place[:, None] * freq[None, :]
    cosine = jnp.cos(angle)
    sine = jnp.sin(angle)
    return (
        jnp.concatenate([cosine] * 4, axis=1),
        jnp.concatenate([-sine, sine, -sine, sine], axis=1),
    )


BITS = (1, 2)


def swap(rows):
    return lax.ppermute(rows, "tp", [(0, 1), (1, 0)])


def tp_sum(part):
    if lax.axis_size("tp") == 2:
        return part + swap(part)
    return lax.psum(part, "tp")


def two_halves(own):
    if lax.axis_size("tp") == 2:
        return (own, swap(own))
    whole = lax.all_gather(own, "tp", axis=0, tiled=True)
    half = whole.shape[0] // 2
    return (whole[:half], whole[half:])


def sum_halves(kept, sent):
    if lax.axis_size("tp") == 2:
        return kept + swap(sent)
    whole = jnp.concatenate([kept, sent], axis=0)
    return lax.psum_scatter(whole, "tp", scatter_dimension=0, tiled=True)


def sum_payload(kept, sent, half):
    if lax.axis_size("tp") == 2:
        return kept + swap(sent)
    total = sum_halves(kept[:half], sent[:half])
    return jnp.concatenate([total, kept[half:]], axis=0)


def absolute_rows(own):
    if lax.axis_size("tp") == 2:
        other = swap(own)
        first = lax.axis_index("tp") == 0
        return jnp.concatenate(
            [jnp.where(first, own, other), jnp.where(first, other, own)], axis=0
        )
    return lax.all_gather(own, "tp", axis=0, tiled=True)


def group_pairs(turn):
    ex = lax.axis_size("ex")
    tp = lax.axis_size("tp")
    pairs = []
    for place in range(ex):
        for core in range(tp):
            bit = BITS[(turn + core) % 2]
            pairs.append((place * tp + core, (place ^ bit) * tp + core))
    return pairs


def group_swap(value_rows, turn):
    return lax.ppermute(value_rows, ("ex", "tp"), group_pairs(turn))


def line_shift(value_rows, step):
    ex = lax.axis_size("ex")
    moved = 4 * step
    return lax.ppermute(value_rows, "ex", [(place, (place - moved) % ex) for place in range(ex)])


def group_bit(turn):
    bit = jnp.where((lax.axis_index("tp") + turn) % 2 == 0, BITS[0], BITS[1])
    return ((lax.axis_index("ex") & bit) != 0).astype(jnp.int32)


def cut_rows(array, place, size):
    return lax.dynamic_slice_in_dim(array, place * size, size, 0)


def group_sum(arrays):
    for turn in (1, 0):
        halves = [array.shape[0] // 2 for array in arrays]
        bit = group_bit(turn)
        sent = [
            cut_rows(array, 1 - bit, half).astype(jnp.bfloat16)
            for array, half in zip(arrays, halves)
        ]
        sent = group_swap(jnp.concatenate(sent, axis=0), turn)
        start = 0
        totals = []
        for array, half in zip(arrays, halves):
            arrived = sent[start : start + half].astype(jnp.float32)
            totals.append(cut_rows(array, bit, half) + arrived)
            start += half
        arrays = totals
    return arrays


def line_total(arrays):
    planes = lax.axis_size("ex") // 4
    plane = lax.axis_index("ex") // 4
    shares = [array.shape[0] // planes for array in arrays]
    lows = [array.astype(jnp.bfloat16) for array in arrays]

    def piece(place):
        return jnp.concatenate(
            [cut_rows(low, place, share) for low, share in zip(lows, shares)], axis=0
        )

    total = jnp.concatenate(
        [cut_rows(array, plane, share) for array, share in zip(arrays, shares)], axis=0
    )
    for step in range(1, planes):
        arrived = line_shift(piece(lax.rem(plane + planes - step, planes)), step)
        total = total + arrived.astype(jnp.float32)
    return total.astype(jnp.bfloat16)


def everywhere(total, shares):
    planes = lax.axis_size("ex") // 4
    plane = lax.axis_index("ex") // 4
    share = total.shape[0]
    rows = jnp.zeros((planes * share, total.shape[1]), total.dtype)
    rows = lax.dynamic_update_slice_in_dim(rows, total, plane * share, 0)
    for step in range(1, planes):
        source = lax.rem(plane + step, planes)
        rows = lax.dynamic_update_slice_in_dim(rows, line_shift(total, step), source * share, 0)
    for turn in range(2):
        first = group_bit(turn) == 0
        other = group_swap(rows, turn)
        rows = jnp.concatenate(
            [jnp.where(first, rows, other), jnp.where(first, other, rows)], axis=0
        )
    rows = rows.reshape(4 * planes, share, total.shape[1])
    results = []
    start = 0
    for size in shares:
        part = rows[:, start : start + size].astype(jnp.float32)
        results.append(part.reshape(4 * planes * size, total.shape[1]))
        start += size
    return results


def over_rows(left, right):
    return lax.dot_general(
        left, right, (((0,), (0,)), ((), ())), preferred_element_type=jnp.float32
    )


def over_last(left, right):
    return lax.dot_general(
        left, right, (((1,), (1,)), ((), ())), preferred_element_type=jnp.float32
    )


def half_turn(block):
    lanes = lax.broadcasted_iota(jnp.int32, block.shape, 1)
    return jnp.where(lanes % 64 < 32, pltpu.roll(block, 96, 1), pltpu.roll(block, 32, 1))


def both_halves(block, which):
    lanes = lax.broadcasted_iota(jnp.int32, block.shape, 1)
    turned = pltpu.roll(block, 64, 1)
    return jnp.where((lanes < 64) == (which == 0), block, turned)


def set_mask(split, mask):
    keys = lax.broadcasted_iota(jnp.int32, mask.shape, 0)
    queries = lax.broadcasted_iota(jnp.int32, mask.shape, 1)
    allowed = (keys <= queries) & ((keys >= split) | (queries < split))
    mask[...] = jnp.where(allowed, 0.0, NEGATIVE)


def attention_kernel(
    split,
    tokens,
    gain,
    w_query,
    key_weight,
    value_weight,
    w_out,
    cosine,
    sine,
    normed_out,
    query_out,
    key_out,
    value_out,
    heads_out,
    totals_out,
    part_out,
    mask,
):
    length = tokens.shape[0]
    factor = float(HEAD_SIZE) ** (-0.5)
    f32 = jnp.float32
    low = jnp.bfloat16
    set_mask(split[0], mask)
    rows = tokens[...].astype(f32)
    normed = (rows * norm_scale(rows) * gain[...]).astype(low)
    normed_out[...] = normed
    query = jnp.dot(normed, w_query[...], preferred_element_type=f32)
    key = jnp.dot(normed, key_weight[...], preferred_element_type=f32)
    value = jnp.dot(normed, value_weight[...], preferred_element_type=f32)
    value_out[...] = value.astype(low)
    keys = []
    turned_values = []
    for index in range(key.shape[1] // 128):
        block = key[:, index * 128 : (index + 1) * 128]
        block = (block * cosine[...] + half_turn(block) * sine[...]).astype(low)
        key_out[:, index * 128 : (index + 1) * 128] = block
        keys.append(block.astype(f32))
        turned_values.append(value[:, index * 128 : (index + 1) * 128].T.astype(low))
    lanes = lax.broadcasted_iota(jnp.int32, (length, 128), 1)
    tile = length // 2
    for index in range(query.shape[1] // 128):
        block = query[:, index * 128 : (index + 1) * 128]
        block = block * cosine[...] + half_turn(block) * sine[...]
        query_out[:, index * 128 : (index + 1) * 128] = block.astype(low)
        shared = both_halves(keys[index // 2], index % 2).astype(low)
        turned = turned_values[index // 2][index % 2 * 64 : index % 2 * 64 + 64]
        columns = []
        for place in range(2):
            masked = jnp.where((lanes < 64) == (place == 0), block, 0.0).astype(low)
            pieces = []
            for number in range(2):
                start, end = number * tile, (number + 1) * tile
                scores = over_last(shared[:end], masked[start:end])
                scores = scores * factor + mask[:end, start:end]
                largest = jnp.max(scores, axis=0, keepdims=True)
                weights = jnp.exp(scores - largest)
                total = jnp.sum(weights, axis=0, keepdims=True)
                probs = (weights * (1.0 / total)).astype(low)
                pieces.append(jnp.dot(turned[:, :end], probs, preferred_element_type=f32))
                totals_out[2 * index + place : 2 * index + place + 1, start:end] = (
                    largest + jnp.log(total)
                )
            columns.append(jnp.concatenate(pieces, axis=1))
        heads = jnp.concatenate(columns, axis=0).T
        heads_out[:, index * 128 : (index + 1) * 128] = heads.astype(low)
    part = jnp.dot(heads_out[...], w_out[...], preferred_element_type=f32)
    part_out[...] = part.astype(low)


def attention(split, tokens, gain, w_query, key_weight, value_weight, w_out, cosine, sine):
    length, width = tokens.shape
    q_width = w_query.shape[1]
    k_width = key_weight.shape[1]
    low = jnp.bfloat16
    whole = pl.BlockSpec(memory_space=pltpu.VMEM)
    return pl.pallas_call(
        attention_kernel,
        out_shape=[
            jax.ShapeDtypeStruct((length, width), low),
            jax.ShapeDtypeStruct((length, q_width), low),
            jax.ShapeDtypeStruct((length, k_width), low),
            jax.ShapeDtypeStruct((length, k_width), low),
            jax.ShapeDtypeStruct((length, q_width), low),
            jax.ShapeDtypeStruct((q_width // HEAD_SIZE, length), jnp.float32),
            jax.ShapeDtypeStruct((length, width), low),
        ],
        in_specs=[pl.BlockSpec(memory_space=pltpu.SMEM)] + [whole] * 8,
        out_specs=[whole] * 7,
        scratch_shapes=[pltpu.VMEM((length, length), jnp.float32)],
        compiler_params=pltpu.CompilerParams(vmem_limit_bytes=48 * 1024 * 1024),
        cost_estimate=pl.CostEstimate(flops=1000000, bytes_accessed=1000000, transcendentals=0),
        name="attention",
    )(split, tokens, gain, w_query, key_weight, value_weight, w_out, cosine, sine)


def attention_grad_kernel(
    split,
    query,
    key,
    value,
    grad_attended,
    w_out,
    totals,
    cosine,
    sine,
    grad_out,
    mask,
):
    length = query.shape[0]
    grad_heads = over_last(grad_attended[...], w_out[...]).astype(jnp.bfloat16)
    factor = float(HEAD_SIZE) ** (-0.5)
    f32 = jnp.float32
    low = jnp.bfloat16
    set_mask(split[0], mask)
    lanes = lax.broadcasted_iota(jnp.int32, (length, 128), 1)
    tile = length // 2
    q_width = query.shape[1]
    k_width = key.shape[1]

    def turn_back(block):
        return (block * cosine[...] - half_turn(block) * sine[...]).astype(low)

    held = None
    for index in range(q_width // 128):
        block = query[:, index * 128 : (index + 1) * 128].astype(f32)
        grads = grad_heads[:, index * 128 : (index + 1) * 128].astype(f32)
        pair = slice(index // 2 * 128, index // 2 * 128 + 128)
        key_block = key[:, pair].astype(f32)
        keys = both_halves(key_block, index % 2).astype(low)
        values = both_halves(value[:, pair].astype(f32), index % 2).astype(low)
        turned = key_block.T[index % 2 * 64 : index % 2 * 64 + 64].astype(low)
        columns = []
        grad_key = [0.0, 0.0]
        grad_value = [0.0, 0.0]
        for place in range(2):
            mine = (lanes < 64) == (place == 0)
            masked = jnp.where(mine, block, 0.0).astype(low)
            masked_grads = jnp.where(mine, grads, 0.0).astype(low)
            pieces = []
            for number in range(2):
                start, end = number * tile, (number + 1) * tile
                part = masked[start:end]
                part_grads = masked_grads[start:end]
                scores = over_last(keys[:end], part) * factor + mask[:end, start:end]
                spot = 2 * index + place
                probs = jnp.exp(scores - totals[spot : spot + 1, start:end])
                grad_probs = over_last(values[:end], part_grads)
                inner = jnp.sum(probs * grad_probs, axis=0, keepdims=True)
                grad_scores = (probs * (grad_probs - inner) * factor).astype(low)
                pieces.append(jnp.dot(turned[:, :end], grad_scores, preferred_element_type=f32))
                some_value = jnp.dot(probs.astype(low), part_grads, preferred_element_type=f32)
                some_key = jnp.dot(grad_scores, part, preferred_element_type=f32)
                for row in range(number + 1):
                    cut = slice(row * tile, (row + 1) * tile)
                    grad_value[row] = grad_value[row] + some_value[cut]
                    grad_key[row] = grad_key[row] + some_key[cut]
            columns.append(jnp.concatenate(pieces, axis=1))
        grad_query = jnp.concatenate(columns, axis=0).T
        grad_out[:, index * 128 : (index + 1) * 128] = turn_back(grad_query)
        sums = []
        for total in (grad_key, grad_value):
            total = jnp.concatenate(total, axis=0)
            sums.append(total + pltpu.roll(total, 64, 1))
        if index % 2 == 1:
            sums = [jnp.where(lanes < 64, old, new) for old, new in zip(held, sums)]
        held = sums
        if index % 2 == 1 or index == q_width // 128 - 1:
            left = q_width + index // 2 * 128
            grad_out[:, left : left + 128] = turn_back(sums[0])
            grad_out[:, left + k_width : left + k_width + 128] = sums[1].astype(low)


def attention_grad(split, query, key, value, grad_attended, w_out, totals, cosine, sine):
    length, q_width = query.shape
    whole = pl.BlockSpec(memory_space=pltpu.VMEM)
    return pl.pallas_call(
        attention_grad_kernel,
        out_shape=jax.ShapeDtypeStruct((length, q_width + 2 * key.shape[1]), jnp.bfloat16),
        in_specs=[pl.BlockSpec(memory_space=pltpu.SMEM)] + [whole] * 8,
        out_specs=whole,
        scratch_shapes=[pltpu.VMEM((length, length), jnp.float32)],
        compiler_params=pltpu.CompilerParams(vmem_limit_bytes=48 * 1024 * 1024),
        cost_estimate=pl.CostEstimate(flops=1000000, bytes_accessed=1000000, transcendentals=0),
        name="attention_grad",
    )(split, query, key, value, grad_attended, w_out, totals, cosine, sine)


def high_low(values):
    high = values.astype(jnp.bfloat16)
    rest = (values - high.astype(jnp.float32)).astype(jnp.bfloat16)
    return (high, rest)


def join_high_low(rows, length):
    wide = rows.astype(jnp.float32)
    return wide[:, :length] + wide[:, length : 2 * length]


def middle_kernel(share, place, tokens, part, other, gain, router, ids, *rest):
    mixed_out, gates_out, routed_out, payload_out, routed = rest[-5:]
    length = tokens.shape[0]
    experts = router.shape[0]
    mixed = tokens[...].astype(jnp.float32) + (
        part[...].astype(jnp.float32) + other[...].astype(jnp.float32)
    )
    mixed_out[...] = mixed
    normed = mixed * norm_scale(mixed) * gain[...]
    routed[...] = normed.astype(jnp.bfloat16)
    routed_out[...] = routed[...]
    logits = lax.dot_general(
        router[...], normed, (((1,), (1,)), ((), ())), precision=HIGH,
        preferred_element_type=jnp.float32,
    )
    names = lax.broadcasted_iota(jnp.int32, (experts, length), 0)
    chosen = names == ids[0:1, :]
    for index in range(1, ids.shape[0]):
        chosen = chosen | (names == ids[index : index + 1, :])
    masked = jnp.where(chosen, logits, NEGATIVE)
    weights = jnp.exp(masked - jnp.max(masked, axis=0, keepdims=True))
    weights = jnp.where(chosen, weights, 0.0)
    gates = weights / jnp.sum(weights, axis=0, keepdims=True)
    gates_out[...] = gates
    payload_out[:share, :] = routed[pl.ds(pl.multiple_of(place[0] * share, share), share), :]
    high, low = high_low(gates)
    payload_out[share:, :length] = high
    payload_out[share:, length : 2 * length] = low


def middle(share, place, tokens, part, other, gain, router, ids, waited):
    length, width = tokens.shape
    experts = router.shape[0]
    whole = pl.BlockSpec(memory_space=pltpu.VMEM)
    anywhere = pl.BlockSpec(memory_space=pl.ANY)
    return pl.pallas_call(
        functools.partial(middle_kernel, share),
        out_shape=[
            jax.ShapeDtypeStruct((length, width), jnp.float32),
            jax.ShapeDtypeStruct((experts, length), jnp.float32),
            jax.ShapeDtypeStruct((length, width), jnp.bfloat16),
            jax.ShapeDtypeStruct((share + experts, width), jnp.bfloat16),
        ],
        in_specs=[pl.BlockSpec(memory_space=pltpu.SMEM)] + [whole] * 6 + [anywhere] * len(waited),
        out_specs=[whole] * 4,
        scratch_shapes=[pltpu.VMEM((length, width), jnp.bfloat16)],
        compiler_params=pltpu.CompilerParams(vmem_limit_bytes=32 * 1024 * 1024),
        cost_estimate=pl.CostEstimate(flops=1000000, bytes_accessed=1000000, transcendentals=0),
        name="middle",
    )(place, tokens, part, other, gain, router, ids, *waited)


def turn_kernel(
    place,
    moe,
    other_moe,
    part_rows,
    other_part_rows,
    mixed_ref,
    gain,
    gates_ref,
    router,
    cotangent,
    heads,
    mixed_out,
    attended_out,
    shared_out,
    grad_normed,
):
    half, width = moe.shape
    length = 2 * half
    experts = router.shape[0]
    q_width = heads.shape[1]
    f32 = jnp.float32
    grad_normed[pl.ds(pl.multiple_of(place[0] * half, half), half), :] = moe[...].astype(f32)
    grad_normed[pl.ds(pl.multiple_of((1 - place[0]) * half, half), half), :] = other_moe[
        ...
    ].astype(f32)
    gate_grads = join_high_low(part_rows[...], length) + join_high_low(
        other_part_rows[...], length
    )
    gates = gates_ref[...]
    grad_logits = gates * (gate_grads - jnp.sum(gates * gate_grads, axis=0, keepdims=True))
    mixed = mixed_ref[...]
    scale = norm_scale(mixed)
    scaled = mixed * scale
    normed = scaled * gain[...]
    grad_router = jnp.dot(grad_logits, normed, precision=HIGH, preferred_element_type=f32)
    padded = jnp.concatenate([grad_logits, jnp.zeros((128 - experts, length), f32)], axis=0)
    wide_router = jnp.concatenate([router[...], jnp.zeros((128 - experts, width), f32)], axis=0)
    grad = grad_normed[...] + jnp.dot(
        padded.T, wide_router, precision=HIGH, preferred_element_type=f32
    )
    weighted = grad * gain[...]
    inner = jnp.mean(weighted * mixed, axis=-1, keepdims=True)
    grad_mixed = (
        cotangent[...].astype(f32) + scale * weighted - scaled * (scale * scale) * inner
    )
    mixed_out[...] = grad_mixed
    attended = grad_mixed.astype(jnp.bfloat16)
    attended_out[...] = attended
    shared_out[:q_width, :] = jnp.dot(
        heads[...].astype(f32).T.astype(jnp.bfloat16), attended, preferred_element_type=f32
    )
    shared_out[q_width : q_width + experts, :] = grad_router
    lines = lax.broadcasted_iota(jnp.int32, (128 - experts, 1), 0)
    gain_grad = jnp.sum(grad * scaled, axis=0, keepdims=True)
    shared_out[q_width + experts :, :] = jnp.where(lines == 0, gain_grad, 0.0)


def turn(place, moe, other_moe, part_rows, other_part_rows, mixed, gain, gates, router, cotangent,
         heads):
    length, width = mixed.shape
    q_width = heads.shape[1]
    whole = pl.BlockSpec(memory_space=pltpu.VMEM)
    return pl.pallas_call(
        turn_kernel,
        out_shape=[
            jax.ShapeDtypeStruct((length, width), jnp.float32),
            jax.ShapeDtypeStruct((length, width), jnp.bfloat16),
            jax.ShapeDtypeStruct((q_width + 128, width), jnp.float32),
        ],
        in_specs=[pl.BlockSpec(memory_space=pltpu.SMEM)] + [whole] * 10,
        out_specs=[whole] * 3,
        scratch_shapes=[pltpu.VMEM((length, width), jnp.float32)],
        compiler_params=pltpu.CompilerParams(vmem_limit_bytes=40 * 1024 * 1024),
        cost_estimate=pl.CostEstimate(flops=1000000, bytes_accessed=1000000, transcendentals=0),
        name="turn",
    )(place, moe, other_moe, part_rows, other_part_rows, mixed, gain, gates, router, cotangent,
      heads)


def expert_kernel(places, own_rows, other_rows, own_grads, other_grads, gate_rows, *rest):
    weights = rest[:4]
    (
        rows_out,
        grads_out,
        hidden_out,
        gate_out,
        up_out,
        back_kept,
        back_sent,
        front_kept,
        front_sent,
        back_total,
        front_total,
        gate_columns,
    ) = rest[-12:]
    core = places[4]
    half = own_rows.shape[0]
    length = 2 * half
    experts = gate_rows.shape[0]
    units = weights[0].shape[1]
    low = jnp.bfloat16
    f32 = jnp.float32
    mine = pl.multiple_of(core * half, half)
    theirs = pl.multiple_of((1 - core) * half, half)
    rows_out[0, pl.ds(mine, half), :] = own_rows[...]
    rows_out[0, pl.ds(theirs, half), :] = other_rows[...]
    grads_out[0, pl.ds(mine, half), :] = own_grads[...]
    grads_out[0, pl.ds(theirs, half), :] = other_grads[...]
    gates = join_high_low(gate_rows[...], length)
    filler = jnp.zeros((128 - experts, length), f32)
    gate_columns[...] = jnp.concatenate([gates, filler], axis=0).T
    rows = rows_out[0]
    grads = grads_out[0]
    lanes = lax.broadcasted_iota(jnp.int32, (length, 128), 1)
    parts = jnp.zeros((length, 128), f32)
    for slot in range(4):
        packed = weights[slot]
        width = rows.shape[1]
        gate_w = packed.at[:width]
        up_w = packed.at[width : 2 * width]
        down_w = jnp.concatenate(
            [packed[start : start + units, :] for start in range(2 * width, 3 * width, units)],
            axis=1,
        )
        chosen = lanes == places[slot]
        gate = jnp.sum(jnp.where(chosen, gate_columns[...], 0.0), axis=1, keepdims=True)
        pre_gate = jnp.dot(rows, gate_w[...], preferred_element_type=f32)
        pre_up = jnp.dot(rows, up_w[...], preferred_element_type=f32)
        grad_plain = over_last(grads, down_w)
        sigmoid = jax.nn.sigmoid(pre_gate)
        activated = pre_gate * sigmoid
        hidden = activated * pre_up
        part = jnp.sum(hidden * grad_plain, axis=1, keepdims=True)
        parts = parts + jnp.where(chosen, part, 0.0)
        hidden_low = (hidden * gate).astype(low)
        grad_hidden = grad_plain * gate
        gate_low = (
            grad_hidden * pre_up * (sigmoid * (1.0 + pre_gate * (1.0 - sigmoid)))
        ).astype(low)
        up_low = (grad_hidden * activated).astype(low)
        columns = slice(slot * units, (slot + 1) * units)
        hidden_out[0, :, columns] = hidden_low
        gate_out[0, :, columns] = gate_low
        up_out[0, :, columns] = up_low
        back = over_last(gate_low, gate_w[...]) + over_last(up_low, up_w[...])
        front = jnp.dot(hidden_low, down_w, preferred_element_type=f32)
        if slot == 0:
            back_total[...] = back
            front_total[...] = front
        else:
            back_total[...] += back
            front_total[...] += front
    back_kept[:half, :] = back_total[pl.ds(mine, half), :].astype(low)
    back_sent[:half, :] = back_total[pl.ds(theirs, half), :].astype(low)
    front_kept[...] = front_total[pl.ds(mine, half), :].astype(low)
    front_sent[...] = front_total[pl.ds(theirs, half), :].astype(low)
    high, rest = high_low(parts.T[:experts])
    back_kept[half:, :length] = high
    back_kept[half:, length : 2 * length] = rest
    back_sent[half:, :] = jnp.zeros((experts, back_sent.shape[1]), low)


def expert_block(places, halves, grad_halves, gate_rows, weights, number, blocks, kept, waited):
    width = halves[0][0].shape[1]
    length = blocks[1]
    half = length // 2
    experts = blocks[2]
    hidden_width = 4 * weights[0].shape[1]
    low = jnp.bfloat16

    def fixed(shape):
        return pl.BlockSpec(shape, lambda step, places: (0, 0))

    def chosen(shape, spot):
        return pl.BlockSpec(shape, lambda step, places: (spot(places), 0))

    def numbered(columns):
        return pl.BlockSpec((1, length, columns), lambda step, places: (number, 0, 0))

    pairs = list(halves) + list(grad_halves)
    in_specs = [chosen((half, width), spot) for unused_array, spot in pairs]
    in_specs = in_specs + [chosen((experts, width), gate_rows[1])]
    in_specs = in_specs + [fixed(weight.shape) for weight in weights]
    loose = list(waited) + list(kept)
    in_specs = in_specs + [pl.BlockSpec(memory_space=pl.ANY)] * len(loose)
    columns = [width] * 2 + [hidden_width] * 3
    first = 1 + 5 + len(weights) + len(waited)
    return pl.pallas_call(
        expert_kernel,
        out_shape=[jax.ShapeDtypeStruct((blocks[0], length, wide), low) for wide in columns]
        + [jax.ShapeDtypeStruct((half + experts, width), low)] * 2
        + [jax.ShapeDtypeStruct((half, width), low)] * 2,
        grid_spec=pltpu.PrefetchScalarGridSpec(
            num_scalar_prefetch=1,
            grid=(1,),
            in_specs=in_specs,
            out_specs=[numbered(wide) for wide in columns]
            + [fixed((half + experts, width))] * 2
            + [fixed((half, width))] * 2,
            scratch_shapes=[
                pltpu.VMEM((length, width), jnp.float32),
                pltpu.VMEM((length, width), jnp.float32),
                pltpu.VMEM((length, 128), jnp.float32),
            ],
        ),
        input_output_aliases={first + index: index for index in range(len(kept))},
        compiler_params=pltpu.CompilerParams(vmem_limit_bytes=48 * 1024 * 1024),
        cost_estimate=pl.CostEstimate(flops=1000000, bytes_accessed=1000000, transcendentals=0),
        name="expert_block",
    )(
        places,
        *[array for array, unused_spot in pairs],
        gate_rows[0],
        *weights,
        *loose,
    )


def product_kernel(steps, rows, hidden, gate, up, grads, wide_kept, wide_sent, down_kept, down_sent,
                   turned_rows, turned_hidden):
    step = pl.program_id(0)
    blocks, length, unused = rows.shape
    low = jnp.bfloat16

    @pl.when(step == 0)
    def begin():
        for block in range(blocks):
            part = slice(block * length, (block + 1) * length)
            turned_rows[:, part] = rows[block].T
            turned_hidden[:, part] = hidden[block].T

    def product(turned, ref):
        flat = ref[...].reshape(blocks * length, ref.shape[2])
        return jnp.dot(turned[...], flat, preferred_element_type=jnp.float32)

    both = (product(turned_rows, gate), product(turned_rows, up))

    @pl.when(step < steps // 2)
    def keep():
        wide_kept[0], wide_kept[1] = both

    @pl.when(step >= steps // 2)
    def send():
        wide_sent[0], wide_sent[1] = both[0].astype(low), both[1].astype(low)

    down = product(turned_hidden, grads)
    half = down.shape[0] // 2
    down_kept[...] = down[:half]
    down_sent[...] = down[half:].astype(low)


def products(rows, grads, hidden, gate, up):
    blocks, length, width = rows.shape
    units = hidden.shape[2]
    steps = 4 if units >= 512 else 2
    half = steps // 2
    low = jnp.bfloat16
    whole = lambda columns: pl.BlockSpec((blocks, length, columns), lambda step: (0, 0, 0))
    tiled = lambda columns: pl.BlockSpec((blocks, length, columns), lambda step: (0, 0, step))
    return pl.pallas_call(
        functools.partial(product_kernel, steps),
        out_shape=[
            jax.ShapeDtypeStruct((2, width, units // 2), jnp.float32),
            jax.ShapeDtypeStruct((2, width, units // 2), low),
            jax.ShapeDtypeStruct((units // 2, width), jnp.float32),
            jax.ShapeDtypeStruct((units // 2, width), low),
        ],
        grid=(steps,),
        in_specs=[whole(width), whole(units), tiled(units // steps), tiled(units // steps),
                  tiled(width // steps)],
        out_specs=[
            pl.BlockSpec(
                (2, width, units // steps), lambda step: (0, 0, jnp.minimum(step, half - 1))
            ),
            pl.BlockSpec(
                (2, width, units // steps), lambda step: (0, 0, jnp.maximum(step - half, 0))
            ),
            pl.BlockSpec((units // 2, width // steps), lambda step: (0, step)),
            pl.BlockSpec((units // 2, width // steps), lambda step: (0, step)),
        ],
        scratch_shapes=[
            pltpu.VMEM((width, blocks * length), low),
            pltpu.VMEM((units, blocks * length), low),
        ],
        compiler_params=pltpu.CompilerParams(vmem_limit_bytes=56 * 1024 * 1024),
        cost_estimate=pl.CostEstimate(flops=1000000, bytes_accessed=1000000, transcendentals=0),
        name="products",
    )(rows, hidden, gate, up, grads)


def shards(
    tokens,
    cotangent,
    gain_one,
    w_query,
    key_weight,
    value_weight,
    w_out,
    gain_two,
    router,
    w_gate,
    w_up,
    w_down,
    expert_ids,
    leading_sequence_length,
):
    length = tokens.shape[0]
    width = tokens.shape[1]
    experts = router.shape[1]
    planes = lax.axis_size("ex") // 4
    plane = lax.axis_index("ex") // 4
    member = lax.axis_index("ex") % 4
    pair = lax.axis_size("tp") == 2
    tp_place = lax.axis_index("tp").astype(jnp.int32)
    odd = tp_place % 2
    core = odd if pair else jnp.zeros_like(odd)
    share = length // lax.axis_size("tp")
    half = length // 2
    q_width = w_query.shape[1]
    low = jnp.bfloat16
    f32 = jnp.float32

    units = w_gate.shape[2]
    own_weights = jnp.concatenate(
        [w_gate[0], w_up[0]]
        + [w_down[0][:, start : start + units] for start in range(0, width, units)],
        axis=0,
    )
    near = group_swap(own_weights, 0)
    far = group_swap(own_weights, 1)
    if pair:
        own_grads = lax.dynamic_slice_in_dim(cotangent, core * half, half, 0)
    else:
        own_grads = lax.dynamic_slice_in_dim(cotangent, tp_place * share, share, 0)
    grads_next = line_shift(own_grads, 1)
    grads_last = line_shift(own_grads, planes - 1)

    cosine, sine = rope_tables(length, leading_sequence_length[0], HEAD_SIZE)
    k_width = key_weight.shape[1]
    filler = -k_width % 128
    wide_key = jnp.pad(key_weight, ((0, 0), (0, filler)))
    wide_value = jnp.pad(value_weight, ((0, 0), (0, filler)))
    normed_one, query_rows, key_rows, value_rows, heads, log_totals, part = attention(
        leading_sequence_length, tokens, gain_one[None], w_query, wide_key, wide_value, w_out,
        cosine, sine,
    )
    part, grads_next, grads_last, near = lax.optimization_barrier(
        (part, grads_next, grads_last, near)
    )
    if pair:
        other_part = swap(part)
    else:
        other_part = (lax.psum(part.astype(f32), "tp") - part.astype(f32)).astype(low)
    turned_router = router.T
    mixed, gates, routed, payload = middle(
        share, tp_place[None], tokens, part, other_part, gain_two[None], turned_router,
        expert_ids.T, [],
    )
    weights = [own_weights, near, far, group_swap(near, 1)]

    slots = jnp.arange(4, dtype=jnp.int32)
    flipped = (slots % 2) * 2 + slots // 2
    slot_member = jnp.where(odd == 1, flipped, slots) ^ member
    places = jnp.concatenate([plane * 4 + slot_member, core[None]]).astype(jnp.int32)

    def gathered(value_rows, following, last):
        held = {0: value_rows, 1: following, planes - 1: last}
        if planes == 4:
            held[2] = line_shift(following, 1)
        else:
            for step in range(2, planes - 1):
                held[step] = line_shift(value_rows, step)
        return held

    def first_block(places):
        return 0

    def own_place(places):
        return places[4]

    def other_place(places):
        return 1 - places[4]

    held_grads = gathered(own_grads, grads_next, grads_last)
    held_rows = gathered(payload, line_shift(payload, 1), line_shift(payload, planes - 1))

    def both(array):
        if pair:
            return ((array, first_block), (swap(array[:half]), first_block))
        own, other = two_halves(array[:share])
        return ((own, first_block), (other, first_block))

    order = [1, 3, 2, 0] if planes == 4 else list(range(1, planes)) + [0]
    kept = ()
    backs = {}
    fronts = {}
    received = []
    results = None
    finished = []
    for number, step in enumerate(order):
        if step == 0:
            halves = ((routed, own_place), (routed, other_place))
            grad_pair = ((cotangent, own_place), (cotangent, other_place))
        else:
            rows, grads = held_rows[step], held_grads[step]
            if number >= 2:
                rows, grads, unused = lax.optimization_barrier((rows, grads, finished[-1]))
            halves, grad_pair = both(rows), both(grads)
        if step == 0 or not pair:
            source = payload if step == 0 else rows
            gate_rows = (source[share:], first_block)
        else:
            gate_rows = (rows, lambda places: half // experts)
        waited = []
        finished.append(None if results is None else results[5])
        results = expert_block(
            places, halves, grad_pair, gate_rows, weights, number, (planes, length, experts),
            kept, waited,
        )
        kept = results[:5]
        backs[step] = sum_payload(results[5], results[6], half)
        fronts[step] = (results[7], results[8])
        if step:
            received.append(line_shift(backs[step], planes - step))

    back_sum = backs[0].astype(f32)
    for arrived in received:
        back_sum = back_sum + arrived.astype(f32)
    back_sum = back_sum.astype(low)
    front_parts = [sum_halves(*fronts[step]) for step in range(planes)]
    weight_products = products(*kept)
    *tied, back_sum = lax.optimization_barrier((*weight_products, *front_parts, back_sum))
    wide_kept, wide_sent, down_kept, down_sent = tied[:4]
    front_parts = tied[4:]
    front_arrived = [
        line_shift(front_parts[step], planes - step) for step in range(1, planes)
    ]
    wide_sent = group_swap(wide_sent, 1)
    down_sent = group_swap(down_sent, 1)
    if pair:
        other_sum = swap(back_sum)
        moe, other_moe = back_sum[:half], other_sum[:half]
        part_rows, other_part_rows = back_sum[half:], other_sum[half:]
    else:
        moe, other_moe = two_halves(back_sum[:share])
        part_sum = lax.psum(join_high_low(back_sum[share:], length), "tp")
        part_rows = jnp.concatenate(high_low(part_sum), axis=1)
        other_part_rows = jnp.zeros_like(part_rows)
    grad_mixed, grad_attended, shared_grads = turn(
        core[None], moe, other_moe, part_rows, other_part_rows, mixed, gain_two[None], gates,
        turned_router, cotangent, heads,
    )
    grad_three = attention_grad(
        leading_sequence_length, query_rows, key_rows, value_rows, grad_attended, w_out,
        log_totals, cosine, sine,
    )

    wide_sent, down_sent, grad_three, shared_grads = lax.optimization_barrier(
        (wide_sent, down_sent, grad_three, shared_grads)
    )
    weight_grads = over_rows(normed_one, grad_three)
    groups = [[weight_grads, shared_grads]]
    if weight_grads.shape[1] != width:
        groups = [[weight_grads], [shared_grads]]
    sums = [group_sum(group) for group in groups]
    tied, front_arrived = lax.optimization_barrier((sums, front_arrived))
    totals = [line_total(group) for group in tied]
    front_sum = front_parts[0].astype(f32)
    for arrived in front_arrived:
        front_sum = front_sum + arrived.astype(f32)
    output = (mixed + absolute_rows(front_sum.astype(low)).astype(f32)).astype(low)

    def expert_grad(held, sent, axis):
        quarter = held.shape[axis] // 2
        late = lax.slice_in_dim(held, quarter, 2 * quarter, axis=axis) + lax.slice_in_dim(
            sent, quarter, 2 * quarter, axis=axis
        ).astype(f32)
        late = group_swap(late.astype(low), 0)
        return (
            lax.slice_in_dim(held, 0, quarter, axis=axis)
            + lax.slice_in_dim(sent, 0, quarter, axis=axis).astype(f32)
            + late.astype(f32)
        )

    wide_grads = expert_grad(wide_kept, wide_sent, 2)
    down_grads = expert_grad(down_kept, down_sent, 0)

    results = []
    for group, total in zip(groups, totals):
        results += everywhere(total, [array.shape[0] // (4 * planes) for array in group])
    weight_grads, shared_grads = results
    grad_out_proj = shared_grads[:q_width]
    grad_router = shared_grads[q_width : q_width + experts].T
    grad_gain_two = shared_grads[q_width + experts]
    three_weights = jnp.concatenate([w_query, wide_key, wide_value], axis=1)
    grad_normed_one = over_last(grad_three, three_weights)
    grad_normed_one = tp_sum(grad_normed_one.astype(low)).astype(f32)
    x_full = tokens.astype(f32)
    scale_one = norm_scale(x_full)
    grad_input_norm, unused_grad = norm_backward(x_full, scale_one, gain_one, grad_normed_one)
    grad_tokens = (grad_mixed + grad_input_norm).astype(low)
    grad_gain_one = tp_sum(jnp.sum(three_weights.astype(f32) * weight_grads, axis=1)) / gain_one
    key_start = q_width
    value_start = q_width + k_width + filler
    return (
        output,
        grad_tokens,
        grad_gain_one,
        weight_grads[:, :q_width],
        weight_grads[:, key_start : key_start + k_width],
        weight_grads[:, value_start : value_start + k_width],
        grad_out_proj,
        grad_gain_two,
        grad_router,
        wide_grads[0][None],
        wide_grads[1][None],
        down_grads[None],
    )


def solution(mesh):
    placed = (
        P("ex", None),
        P("ex", None),
        P(),
        P(None, "tp"),
        P(None, "tp"),
        P(None, "tp"),
        P("tp", None),
        P(),
        P(),
        P("ex", None, "tp"),
        P("ex", None, "tp"),
        P("ex", "tp", None),
        P("ex", None),
        P("ex"),
    )
    return jax.shard_map(
        shards,
        mesh=mesh,
        in_specs=placed,
        out_specs=(
            P("ex", None),
            P("ex", None),
            P(),
            P(None, "tp"),
            P(None, "tp"),
            P(None, "tp"),
            P("tp", None),
            P(),
            P(),
            P("ex", None, "tp"),
            P("ex", None, "tp"),
            P("ex", "tp", None),
        ),
        check_vma=False,
    )
```

```python
import functools

import jax
import jax.numpy as jnp
from jax import lax
from jax.experimental import pallas as pl
from jax.experimental.pallas import tpu as pltpu
from jax.sharding import PartitionSpec as P

HEAD_SIZE = 64


EPS = 1e-06
THETA = 10000.0
NEGATIVE = -1e30
HIGH = lax.Precision.HIGHEST


def norm_scale(value_rows):
    return lax.rsqrt(jnp.mean(value_rows * value_rows, axis=-1, keepdims=True) + EPS)


def norm_backward(value_rows, scale, gain, grad):
    weighted = grad * gain
    inner = jnp.mean(weighted * value_rows, axis=-1, keepdims=True)
    grad_input = scale * weighted - value_rows * scale * scale * scale * inner
    grad_gain = jnp.sum(grad * value_rows * scale, axis=0)
    return (grad_input, grad_gain)


def rope_tables(length, split, width):
    index = jnp.arange(length, dtype=jnp.int32)
    place = jnp.where(index >= split, index - split, index).astype(jnp.float32)
    freq = THETA ** (-(jnp.arange(width // 2, dtype=jnp.float32) * 2.0 / width))
    angle = place[:, None] * freq[None, :]
    cosine = jnp.cos(angle)
    sine = jnp.sin(angle)
    return (
        jnp.concatenate([cosine] * 4, axis=1),
        jnp.concatenate([-sine, sine, -sine, sine], axis=1),
    )


BITS = (1, 2)


def swap(rows):
    return lax.ppermute(rows, "tp", [(0, 1), (1, 0)])


def tp_sum(part):
    if lax.axis_size("tp") == 2:
        return part + swap(part)
    return lax.psum(part, "tp")


def two_halves(own):
    if lax.axis_size("tp") == 2:
        return (own, swap(own))
    whole = lax.all_gather(own, "tp", axis=0, tiled=True)
    half = whole.shape[0] // 2
    return (whole[:half], whole[half:])


def sum_halves(kept, sent):
    if lax.axis_size("tp") == 2:
        return kept + swap(sent)
    whole = jnp.concatenate([kept, sent], axis=0)
    return lax.psum_scatter(whole, "tp", scatter_dimension=0, tiled=True)


def sum_payload(kept, sent, half):
    if lax.axis_size("tp") == 2:
        return kept + swap(sent)
    total = sum_halves(kept[:half], sent[:half])
    return jnp.concatenate([total, kept[half:]], axis=0)


def absolute_rows(own):
    if lax.axis_size("tp") == 2:
        other = swap(own)
        first = lax.axis_index("tp") == 0
        return jnp.concatenate(
            [jnp.where(first, own, other), jnp.where(first, other, own)], axis=0
        )
    return lax.all_gather(own, "tp", axis=0, tiled=True)


def group_pairs(turn):
    ex = lax.axis_size("ex")
    tp = lax.axis_size("tp")
    pairs = []
    for place in range(ex):
        for core in range(tp):
            bit = BITS[(turn + core) % 2]
            pairs.append((place * tp + core, (place ^ bit) * tp + core))
    return pairs


def group_swap(value_rows, turn):
    return lax.ppermute(value_rows, ("ex", "tp"), group_pairs(turn))


def line_shift(value_rows, step):
    ex = lax.axis_size("ex")
    moved = 4 * step
    return lax.ppermute(value_rows, "ex", [(place, (place - moved) % ex) for place in range(ex)])


def group_bit(turn):
    bit = jnp.where((lax.axis_index("tp") + turn) % 2 == 0, BITS[0], BITS[1])
    return ((lax.axis_index("ex") & bit) != 0).astype(jnp.int32)


def cut_rows(array, place, size):
    return lax.dynamic_slice_in_dim(array, place * size, size, 0)


def group_sum(arrays):
    for turn in (1, 0):
        halves = [array.shape[0] // 2 for array in arrays]
        bit = group_bit(turn)
        sent = [
            cut_rows(array, 1 - bit, half).astype(jnp.bfloat16)
            for array, half in zip(arrays, halves)
        ]
        sent = group_swap(jnp.concatenate(sent, axis=0), turn)
        start = 0
        totals = []
        for array, half in zip(arrays, halves):
            arrived = sent[start : start + half].astype(jnp.float32)
            totals.append(cut_rows(array, bit, half) + arrived)
            start += half
        arrays = totals
    return arrays


def line_total(arrays):
    planes = lax.axis_size("ex") // 4
    plane = lax.axis_index("ex") // 4
    shares = [array.shape[0] // planes for array in arrays]
    lows = [array.astype(jnp.bfloat16) for array in arrays]

    def piece(place):
        return jnp.concatenate(
            [cut_rows(low, place, share) for low, share in zip(lows, shares)], axis=0
        )

    total = jnp.concatenate(
        [cut_rows(array, plane, share) for array, share in zip(arrays, shares)], axis=0
    )
    for step in range(1, planes):
        arrived = line_shift(piece(lax.rem(plane + planes - step, planes)), step)
        total = total + arrived.astype(jnp.float32)
    return total.astype(jnp.bfloat16)


def everywhere(total, shares):
    planes = lax.axis_size("ex") // 4
    plane = lax.axis_index("ex") // 4
    share = total.shape[0]
    rows = jnp.zeros((planes * share, total.shape[1]), total.dtype)
    rows = lax.dynamic_update_slice_in_dim(rows, total, plane * share, 0)
    for step in range(1, planes):
        source = lax.rem(plane + step, planes)
        rows = lax.dynamic_update_slice_in_dim(rows, line_shift(total, step), source * share, 0)
    for turn in range(2):
        first = group_bit(turn) == 0
        other = group_swap(rows, turn)
        rows = jnp.concatenate(
            [jnp.where(first, rows, other), jnp.where(first, other, rows)], axis=0
        )
    rows = rows.reshape(4 * planes, share, total.shape[1])
    results = []
    start = 0
    for size in shares:
        part = rows[:, start : start + size].astype(jnp.float32)
        results.append(part.reshape(4 * planes * size, total.shape[1]))
        start += size
    return results


def over_rows(left, right):
    return lax.dot_general(
        left, right, (((0,), (0,)), ((), ())), preferred_element_type=jnp.float32
    )


def over_last(left, right):
    return lax.dot_general(
        left, right, (((1,), (1,)), ((), ())), preferred_element_type=jnp.float32
    )


def half_turn(block):
    lanes = lax.broadcasted_iota(jnp.int32, block.shape, 1)
    return jnp.where(lanes % 64 < 32, pltpu.roll(block, 96, 1), pltpu.roll(block, 32, 1))


def both_halves(block, which):
    lanes = lax.broadcasted_iota(jnp.int32, block.shape, 1)
    turned = pltpu.roll(block, 64, 1)
    return jnp.where((lanes < 64) == (which == 0), block, turned)


def set_mask(split, mask):
    keys = lax.broadcasted_iota(jnp.int32, mask.shape, 0)
    queries = lax.broadcasted_iota(jnp.int32, mask.shape, 1)
    allowed = (keys <= queries) & ((keys >= split) | (queries < split))
    mask[...] = jnp.where(allowed, 0.0, NEGATIVE)


def attention_kernel(
    split,
    tokens,
    gain,
    w_query,
    key_weight,
    value_weight,
    w_out,
    cosine,
    sine,
    normed_out,
    query_out,
    key_out,
    value_out,
    heads_out,
    totals_out,
    part_out,
    mask,
):
    length = tokens.shape[0]
    factor = float(HEAD_SIZE) ** (-0.5)
    f32 = jnp.float32
    low = jnp.bfloat16
    set_mask(split[0], mask)
    rows = tokens[...].astype(f32)
    normed = (rows * norm_scale(rows) * gain[...]).astype(low)
    normed_out[...] = normed
    query = jnp.dot(normed, w_query[...], preferred_element_type=f32)
    key = jnp.dot(normed, key_weight[...], preferred_element_type=f32)
    value = jnp.dot(normed, value_weight[...], preferred_element_type=f32)
    value_out[...] = value.astype(low)
    keys = []
    turned_values = []
    for index in range(key.shape[1] // 128):
        block = key[:, index * 128 : (index + 1) * 128]
        block = (block * cosine[...] + half_turn(block) * sine[...]).astype(low)
        key_out[:, index * 128 : (index + 1) * 128] = block
        keys.append(block.astype(f32))
        turned_values.append(value[:, index * 128 : (index + 1) * 128].T.astype(low))
    lanes = lax.broadcasted_iota(jnp.int32, (length, 128), 1)
    tile = length // 2
    for index in range(query.shape[1] // 128):
        block = query[:, index * 128 : (index + 1) * 128]
        block = block * cosine[...] + half_turn(block) * sine[...]
        query_out[:, index * 128 : (index + 1) * 128] = block.astype(low)
        shared = both_halves(keys[index // 2], index % 2).astype(low)
        turned = turned_values[index // 2][index % 2 * 64 : index % 2 * 64 + 64]
        columns = []
        for place in range(2):
            masked = jnp.where((lanes < 64) == (place == 0), block, 0.0).astype(low)
            pieces = []
            for number in range(2):
                start, end = number * tile, (number + 1) * tile
                scores = over_last(shared[:end], masked[start:end])
                scores = scores * factor + mask[:end, start:end]
                largest = jnp.max(scores, axis=0, keepdims=True)
                weights = jnp.exp(scores - largest)
                total = jnp.sum(weights, axis=0, keepdims=True)
                probs = (weights * (1.0 / total)).astype(low)
                pieces.append(jnp.dot(turned[:, :end], probs, preferred_element_type=f32))
                totals_out[2 * index + place : 2 * index + place + 1, start:end] = (
                    largest + jnp.log(total)
                )
            columns.append(jnp.concatenate(pieces, axis=1))
        heads = jnp.concatenate(columns, axis=0).T
        heads_out[:, index * 128 : (index + 1) * 128] = heads.astype(low)
    part = jnp.dot(heads_out[...], w_out[...], preferred_element_type=f32)
    part_out[...] = part.astype(low)


def attention(split, tokens, gain, w_query, key_weight, value_weight, w_out, cosine, sine):
    length, width = tokens.shape
    q_width = w_query.shape[1]
    k_width = key_weight.shape[1]
    low = jnp.bfloat16
    whole = pl.BlockSpec(memory_space=pltpu.VMEM)
    return pl.pallas_call(
        attention_kernel,
        out_shape=[
            jax.ShapeDtypeStruct((length, width), low),
            jax.ShapeDtypeStruct((length, q_width), low),
            jax.ShapeDtypeStruct((length, k_width), low),
            jax.ShapeDtypeStruct((length, k_width), low),
            jax.ShapeDtypeStruct((length, q_width), low),
            jax.ShapeDtypeStruct((q_width // HEAD_SIZE, length), jnp.float32),
            jax.ShapeDtypeStruct((length, width), low),
        ],
        in_specs=[pl.BlockSpec(memory_space=pltpu.SMEM)] + [whole] * 8,
        out_specs=[whole] * 7,
        scratch_shapes=[pltpu.VMEM((length, length), jnp.float32)],
        compiler_params=pltpu.CompilerParams(vmem_limit_bytes=48 * 1024 * 1024),
        cost_estimate=pl.CostEstimate(flops=1000000, bytes_accessed=1000000, transcendentals=0),
        name="attention",
    )(split, tokens, gain, w_query, key_weight, value_weight, w_out, cosine, sine)


def attention_grad_kernel(
    split,
    query,
    key,
    value,
    grad_attended,
    w_out,
    totals,
    cosine,
    sine,
    grad_out,
    mask,
):
    length = query.shape[0]
    grad_heads = over_last(grad_attended[...], w_out[...]).astype(jnp.bfloat16)
    factor = float(HEAD_SIZE) ** (-0.5)
    f32 = jnp.float32
    low = jnp.bfloat16
    set_mask(split[0], mask)
    lanes = lax.broadcasted_iota(jnp.int32, (length, 128), 1)
    tile = length // 2
    q_width = query.shape[1]
    k_width = key.shape[1]

    def turn_back(block):
        return (block * cosine[...] - half_turn(block) * sine[...]).astype(low)

    held = None
    for index in range(q_width // 128):
        block = query[:, index * 128 : (index + 1) * 128].astype(f32)
        grads = grad_heads[:, index * 128 : (index + 1) * 128].astype(f32)
        pair = slice(index // 2 * 128, index // 2 * 128 + 128)
        key_block = key[:, pair].astype(f32)
        keys = both_halves(key_block, index % 2).astype(low)
        values = both_halves(value[:, pair].astype(f32), index % 2).astype(low)
        turned = key_block.T[index % 2 * 64 : index % 2 * 64 + 64].astype(low)
        columns = []
        grad_key = [0.0, 0.0]
        grad_value = [0.0, 0.0]
        for place in range(2):
            mine = (lanes < 64) == (place == 0)
            masked = jnp.where(mine, block, 0.0).astype(low)
            masked_grads = jnp.where(mine, grads, 0.0).astype(low)
            pieces = []
            for number in range(2):
                start, end = number * tile, (number + 1) * tile
                part = masked[start:end]
                part_grads = masked_grads[start:end]
                scores = over_last(keys[:end], part) * factor + mask[:end, start:end]
                spot = 2 * index + place
                probs = jnp.exp(scores - totals[spot : spot + 1, start:end])
                grad_probs = over_last(values[:end], part_grads)
                inner = jnp.sum(probs * grad_probs, axis=0, keepdims=True)
                grad_scores = (probs * (grad_probs - inner) * factor).astype(low)
                pieces.append(jnp.dot(turned[:, :end], grad_scores, preferred_element_type=f32))
                some_value = jnp.dot(probs.astype(low), part_grads, preferred_element_type=f32)
                some_key = jnp.dot(grad_scores, part, preferred_element_type=f32)
                for row in range(number + 1):
                    cut = slice(row * tile, (row + 1) * tile)
                    grad_value[row] = grad_value[row] + some_value[cut]
                    grad_key[row] = grad_key[row] + some_key[cut]
            columns.append(jnp.concatenate(pieces, axis=1))
        grad_query = jnp.concatenate(columns, axis=0).T
        grad_out[:, index * 128 : (index + 1) * 128] = turn_back(grad_query)
        sums = []
        for total in (grad_key, grad_value):
            total = jnp.concatenate(total, axis=0)
            sums.append(total + pltpu.roll(total, 64, 1))
        if index % 2 == 1:
            sums = [jnp.where(lanes < 64, old, new) for old, new in zip(held, sums)]
        held = sums
        if index % 2 == 1 or index == q_width // 128 - 1:
            left = q_width + index // 2 * 128
            grad_out[:, left : left + 128] = turn_back(sums[0])
            grad_out[:, left + k_width : left + k_width + 128] = sums[1].astype(low)


def attention_grad(split, query, key, value, grad_attended, w_out, totals, cosine, sine):
    length, q_width = query.shape
    whole = pl.BlockSpec(memory_space=pltpu.VMEM)
    return pl.pallas_call(
        attention_grad_kernel,
        out_shape=jax.ShapeDtypeStruct((length, q_width + 2 * key.shape[1]), jnp.bfloat16),
        in_specs=[pl.BlockSpec(memory_space=pltpu.SMEM)] + [whole] * 8,
        out_specs=whole,
        scratch_shapes=[pltpu.VMEM((length, length), jnp.float32)],
        compiler_params=pltpu.CompilerParams(vmem_limit_bytes=48 * 1024 * 1024),
        cost_estimate=pl.CostEstimate(flops=1000000, bytes_accessed=1000000, transcendentals=0),
        name="attention_grad",
    )(split, query, key, value, grad_attended, w_out, totals, cosine, sine)


def high_low(values):
    high = values.astype(jnp.bfloat16)
    rest = (values - high.astype(jnp.float32)).astype(jnp.bfloat16)
    return (high, rest)


def join_high_low(rows, length):
    wide = rows.astype(jnp.float32)
    return wide[:, :length] + wide[:, length : 2 * length]


def middle_kernel(share, place, tokens, part, other, gain, router, ids, *rest):
    mixed_out, gates_out, routed_out, payload_out, routed = rest[-5:]
    length = tokens.shape[0]
    experts = router.shape[0]
    mixed = tokens[...].astype(jnp.float32) + (
        part[...].astype(jnp.float32) + other[...].astype(jnp.float32)
    )
    mixed_out[...] = mixed
    normed = mixed * norm_scale(mixed) * gain[...]
    routed[...] = normed.astype(jnp.bfloat16)
    routed_out[...] = routed[...]
    logits = lax.dot_general(
        router[...], normed, (((1,), (1,)), ((), ())), precision=HIGH,
        preferred_element_type=jnp.float32,
    )
    names = lax.broadcasted_iota(jnp.int32, (experts, length), 0)
    chosen = names == ids[0:1, :]
    for index in range(1, ids.shape[0]):
        chosen = chosen | (names == ids[index : index + 1, :])
    masked = jnp.where(chosen, logits, NEGATIVE)
    weights = jnp.exp(masked - jnp.max(masked, axis=0, keepdims=True))
    weights = jnp.where(chosen, weights, 0.0)
    gates = weights / jnp.sum(weights, axis=0, keepdims=True)
    gates_out[...] = gates
    payload_out[:share, :] = routed[pl.ds(pl.multiple_of(place[0] * share, share), share), :]
    high, low = high_low(gates)
    payload_out[share:, :length] = high
    payload_out[share:, length : 2 * length] = low


def middle(share, place, tokens, part, other, gain, router, ids, waited):
    length, width = tokens.shape
    experts = router.shape[0]
    whole = pl.BlockSpec(memory_space=pltpu.VMEM)
    anywhere = pl.BlockSpec(memory_space=pl.ANY)
    return pl.pallas_call(
        functools.partial(middle_kernel, share),
        out_shape=[
            jax.ShapeDtypeStruct((length, width), jnp.float32),
            jax.ShapeDtypeStruct((experts, length), jnp.float32),
            jax.ShapeDtypeStruct((length, width), jnp.bfloat16),
            jax.ShapeDtypeStruct((share + experts, width), jnp.bfloat16),
        ],
        in_specs=[pl.BlockSpec(memory_space=pltpu.SMEM)] + [whole] * 6 + [anywhere] * len(waited),
        out_specs=[whole] * 4,
        scratch_shapes=[pltpu.VMEM((length, width), jnp.bfloat16)],
        compiler_params=pltpu.CompilerParams(vmem_limit_bytes=32 * 1024 * 1024),
        cost_estimate=pl.CostEstimate(flops=1000000, bytes_accessed=1000000, transcendentals=0),
        name="middle",
    )(place, tokens, part, other, gain, router, ids, *waited)


def turn_kernel(
    place,
    moe,
    other_moe,
    part_rows,
    other_part_rows,
    mixed_ref,
    gain,
    gates_ref,
    router,
    cotangent,
    heads,
    mixed_out,
    attended_out,
    shared_out,
    grad_normed,
):
    half, width = moe.shape
    length = 2 * half
    experts = router.shape[0]
    q_width = heads.shape[1]
    f32 = jnp.float32
    grad_normed[pl.ds(pl.multiple_of(place[0] * half, half), half), :] = moe[...].astype(f32)
    grad_normed[pl.ds(pl.multiple_of((1 - place[0]) * half, half), half), :] = other_moe[
        ...
    ].astype(f32)
    gate_grads = join_high_low(part_rows[...], length) + join_high_low(
        other_part_rows[...], length
    )
    gates = gates_ref[...]
    grad_logits = gates * (gate_grads - jnp.sum(gates * gate_grads, axis=0, keepdims=True))
    mixed = mixed_ref[...]
    scale = norm_scale(mixed)
    scaled = mixed * scale
    normed = scaled * gain[...]
    grad_router = jnp.dot(grad_logits, normed, precision=HIGH, preferred_element_type=f32)
    padded = jnp.concatenate([grad_logits, jnp.zeros((128 - experts, length), f32)], axis=0)
    wide_router = jnp.concatenate([router[...], jnp.zeros((128 - experts, width), f32)], axis=0)
    grad = grad_normed[...] + jnp.dot(
        padded.T, wide_router, precision=HIGH, preferred_element_type=f32
    )
    weighted = grad * gain[...]
    inner = jnp.mean(weighted * mixed, axis=-1, keepdims=True)
    grad_mixed = (
        cotangent[...].astype(f32) + scale * weighted - scaled * (scale * scale) * inner
    )
    mixed_out[...] = grad_mixed
    attended = grad_mixed.astype(jnp.bfloat16)
    attended_out[...] = attended
    shared_out[:q_width, :] = jnp.dot(
        heads[...].astype(f32).T.astype(jnp.bfloat16), attended, preferred_element_type=f32
    )
    shared_out[q_width : q_width + experts, :] = grad_router
    lines = lax.broadcasted_iota(jnp.int32, (128 - experts, 1), 0)
    gain_grad = jnp.sum(grad * scaled, axis=0, keepdims=True)
    shared_out[q_width + experts :, :] = jnp.where(lines == 0, gain_grad, 0.0)


def turn(place, moe, other_moe, part_rows, other_part_rows, mixed, gain, gates, router, cotangent,
         heads):
    length, width = mixed.shape
    q_width = heads.shape[1]
    whole = pl.BlockSpec(memory_space=pltpu.VMEM)
    return pl.pallas_call(
        turn_kernel,
        out_shape=[
            jax.ShapeDtypeStruct((length, width), jnp.float32),
            jax.ShapeDtypeStruct((length, width), jnp.bfloat16),
            jax.ShapeDtypeStruct((q_width + 128, width), jnp.float32),
        ],
        in_specs=[pl.BlockSpec(memory_space=pltpu.SMEM)] + [whole] * 10,
        out_specs=[whole] * 3,
        scratch_shapes=[pltpu.VMEM((length, width), jnp.float32)],
        compiler_params=pltpu.CompilerParams(vmem_limit_bytes=40 * 1024 * 1024),
        cost_estimate=pl.CostEstimate(flops=1000000, bytes_accessed=1000000, transcendentals=0),
        name="turn",
    )(place, moe, other_moe, part_rows, other_part_rows, mixed, gain, gates, router, cotangent,
      heads)


def expert_kernel(places, own_rows, other_rows, own_grads, other_grads, gate_rows, *rest):
    weights = rest[:4]
    (
        rows_out,
        grads_out,
        hidden_out,
        gate_out,
        up_out,
        back_kept,
        back_sent,
        front_kept,
        front_sent,
        back_total,
        front_total,
        gate_columns,
    ) = rest[-12:]
    core = places[4]
    half = own_rows.shape[0]
    length = 2 * half
    experts = gate_rows.shape[0]
    units = weights[0].shape[1]
    low = jnp.bfloat16
    f32 = jnp.float32
    mine = pl.multiple_of(core * half, half)
    theirs = pl.multiple_of((1 - core) * half, half)
    rows_out[0, pl.ds(mine, half), :] = own_rows[...]
    rows_out[0, pl.ds(theirs, half), :] = other_rows[...]
    grads_out[0, pl.ds(mine, half), :] = own_grads[...]
    grads_out[0, pl.ds(theirs, half), :] = other_grads[...]
    gates = join_high_low(gate_rows[...], length)
    filler = jnp.zeros((128 - experts, length), f32)
    gate_columns[...] = jnp.concatenate([gates, filler], axis=0).T
    rows = rows_out[0]
    grads = grads_out[0]
    lanes = lax.broadcasted_iota(jnp.int32, (length, 128), 1)
    parts = jnp.zeros((length, 128), f32)
    for slot in range(4):
        packed = weights[slot]
        width = rows.shape[1]
        gate_w = packed.at[:width]
        up_w = packed.at[width : 2 * width]
        down_w = jnp.concatenate(
            [packed[start : start + units, :] for start in range(2 * width, 3 * width, units)],
            axis=1,
        )
        chosen = lanes == places[slot]
        gate = jnp.sum(jnp.where(chosen, gate_columns[...], 0.0), axis=1, keepdims=True)
        pre_gate = jnp.dot(rows, gate_w[...], preferred_element_type=f32)
        pre_up = jnp.dot(rows, up_w[...], preferred_element_type=f32)
        grad_plain = over_last(grads, down_w)
        sigmoid = jax.nn.sigmoid(pre_gate)
        activated = pre_gate * sigmoid
        hidden = activated * pre_up
        part = jnp.sum(hidden * grad_plain, axis=1, keepdims=True)
        parts = parts + jnp.where(chosen, part, 0.0)
        hidden_low = (hidden * gate).astype(low)
        grad_hidden = grad_plain * gate
        gate_low = (
            grad_hidden * pre_up * (sigmoid * (1.0 + pre_gate * (1.0 - sigmoid)))
        ).astype(low)
        up_low = (grad_hidden * activated).astype(low)
        columns = slice(slot * units, (slot + 1) * units)
        hidden_out[0, :, columns] = hidden_low
        gate_out[0, :, columns] = gate_low
        up_out[0, :, columns] = up_low
        back = over_last(gate_low, gate_w[...]) + over_last(up_low, up_w[...])
        front = jnp.dot(hidden_low, down_w, preferred_element_type=f32)
        if slot == 0:
            back_total[...] = back
            front_total[...] = front
        else:
            back_total[...] += back
            front_total[...] += front
    back_kept[:half, :] = back_total[pl.ds(mine, half), :].astype(low)
    back_sent[:half, :] = back_total[pl.ds(theirs, half), :].astype(low)
    front_kept[...] = front_total[pl.ds(mine, half), :].astype(low)
    front_sent[...] = front_total[pl.ds(theirs, half), :].astype(low)
    high, rest = high_low(parts.T[:experts])
    back_kept[half:, :length] = high
    back_kept[half:, length : 2 * length] = rest
    back_sent[half:, :] = jnp.zeros((experts, back_sent.shape[1]), low)


def expert_block(places, halves, grad_halves, gate_rows, weights, number, blocks, kept, waited):
    width = halves[0][0].shape[1]
    length = blocks[1]
    half = length // 2
    experts = blocks[2]
    hidden_width = 4 * weights[0].shape[1]
    low = jnp.bfloat16

    def fixed(shape):
        return pl.BlockSpec(shape, lambda step, places: (0, 0))

    def chosen(shape, spot):
        return pl.BlockSpec(shape, lambda step, places: (spot(places), 0))

    def numbered(columns):
        return pl.BlockSpec((1, length, columns), lambda step, places: (number, 0, 0))

    pairs = list(halves) + list(grad_halves)
    in_specs = [chosen((half, width), spot) for unused_array, spot in pairs]
    in_specs = in_specs + [chosen((experts, width), gate_rows[1])]
    in_specs = in_specs + [fixed(weight.shape) for weight in weights]
    loose = list(waited) + list(kept)
    in_specs = in_specs + [pl.BlockSpec(memory_space=pl.ANY)] * len(loose)
    columns = [width] * 2 + [hidden_width] * 3
    first = 1 + 5 + len(weights) + len(waited)
    return pl.pallas_call(
        expert_kernel,
        out_shape=[jax.ShapeDtypeStruct((blocks[0], length, wide), low) for wide in columns]
        + [jax.ShapeDtypeStruct((half + experts, width), low)] * 2
        + [jax.ShapeDtypeStruct((half, width), low)] * 2,
        grid_spec=pltpu.PrefetchScalarGridSpec(
            num_scalar_prefetch=1,
            grid=(1,),
            in_specs=in_specs,
            out_specs=[numbered(wide) for wide in columns]
            + [fixed((half + experts, width))] * 2
            + [fixed((half, width))] * 2,
            scratch_shapes=[
                pltpu.VMEM((length, width), jnp.float32),
                pltpu.VMEM((length, width), jnp.float32),
                pltpu.VMEM((length, 128), jnp.float32),
            ],
        ),
        input_output_aliases={first + index: index for index in range(len(kept))},
        compiler_params=pltpu.CompilerParams(vmem_limit_bytes=48 * 1024 * 1024),
        cost_estimate=pl.CostEstimate(flops=1000000, bytes_accessed=1000000, transcendentals=0),
        name="expert_block",
    )(
        places,
        *[array for array, unused_spot in pairs],
        gate_rows[0],
        *weights,
        *loose,
    )


def product_kernel(steps, rows, hidden, gate, up, grads, wide_kept, wide_sent, down_kept, down_sent,
                   turned_rows, turned_hidden):
    step = pl.program_id(0)
    blocks, length, unused = rows.shape
    low = jnp.bfloat16

    @pl.when(step == 0)
    def begin():
        for block in range(blocks):
            part = slice(block * length, (block + 1) * length)
            turned_rows[:, part] = rows[block].T
            turned_hidden[:, part] = hidden[block].T

    def product(turned, ref):
        flat = ref[...].reshape(blocks * length, ref.shape[2])
        return jnp.dot(turned[...], flat, preferred_element_type=jnp.float32)

    both = (product(turned_rows, gate), product(turned_rows, up))

    @pl.when(step < steps // 2)
    def keep():
        wide_kept[0], wide_kept[1] = both

    @pl.when(step >= steps // 2)
    def send():
        wide_sent[0], wide_sent[1] = both[0].astype(low), both[1].astype(low)

    down = product(turned_hidden, grads)
    half = down.shape[0] // 2
    down_kept[...] = down[:half]
    down_sent[...] = down[half:].astype(low)


def products(rows, grads, hidden, gate, up):
    blocks, length, width = rows.shape
    units = hidden.shape[2]
    steps = 4 if units >= 512 else 2
    half = steps // 2
    low = jnp.bfloat16
    whole = lambda columns: pl.BlockSpec((blocks, length, columns), lambda step: (0, 0, 0))
    tiled = lambda columns: pl.BlockSpec((blocks, length, columns), lambda step: (0, 0, step))
    return pl.pallas_call(
        functools.partial(product_kernel, steps),
        out_shape=[
            jax.ShapeDtypeStruct((2, width, units // 2), jnp.float32),
            jax.ShapeDtypeStruct((2, width, units // 2), low),
            jax.ShapeDtypeStruct((units // 2, width), jnp.float32),
            jax.ShapeDtypeStruct((units // 2, width), low),
        ],
        grid=(steps,),
        in_specs=[whole(width), whole(units), tiled(units // steps), tiled(units // steps),
                  tiled(width // steps)],
        out_specs=[
            pl.BlockSpec(
                (2, width, units // steps), lambda step: (0, 0, jnp.minimum(step, half - 1))
            ),
            pl.BlockSpec(
                (2, width, units // steps), lambda step: (0, 0, jnp.maximum(step - half, 0))
            ),
            pl.BlockSpec((units // 2, width // steps), lambda step: (0, step)),
            pl.BlockSpec((units // 2, width // steps), lambda step: (0, step)),
        ],
        scratch_shapes=[
            pltpu.VMEM((width, blocks * length), low),
            pltpu.VMEM((units, blocks * length), low),
        ],
        compiler_params=pltpu.CompilerParams(vmem_limit_bytes=56 * 1024 * 1024),
        cost_estimate=pl.CostEstimate(flops=1000000, bytes_accessed=1000000, transcendentals=0),
        name="products",
    )(rows, hidden, gate, up, grads)


def shards(
    tokens,
    cotangent,
    gain_one,
    w_query,
    key_weight,
    value_weight,
    w_out,
    gain_two,
    router,
    w_gate,
    w_up,
    w_down,
    expert_ids,
    leading_sequence_length,
):
    length = tokens.shape[0]
    width = tokens.shape[1]
    experts = router.shape[1]
    planes = lax.axis_size("ex") // 4
    plane = lax.axis_index("ex") // 4
    member = lax.axis_index("ex") % 4
    pair = lax.axis_size("tp") == 2
    tp_place = lax.axis_index("tp").astype(jnp.int32)
    odd = tp_place % 2
    core = odd if pair else jnp.zeros_like(odd)
    share = length // lax.axis_size("tp")
    half = length // 2
    q_width = w_query.shape[1]
    low = jnp.bfloat16
    f32 = jnp.float32

    units = w_gate.shape[2]
    own_weights = jnp.concatenate(
        [w_gate[0], w_up[0]]
        + [w_down[0][:, start : start + units] for start in range(0, width, units)],
        axis=0,
    )
    near = group_swap(own_weights, 0)
    far = group_swap(own_weights, 1)
    if pair:
        own_grads = lax.dynamic_slice_in_dim(cotangent, core * half, half, 0)
    else:
        own_grads = lax.dynamic_slice_in_dim(cotangent, tp_place * share, share, 0)
    grads_next = line_shift(own_grads, 1)
    grads_last = line_shift(own_grads, planes - 1)

    cosine, sine = rope_tables(length, leading_sequence_length[0], HEAD_SIZE)
    k_width = key_weight.shape[1]
    filler = -k_width % 128
    wide_key = jnp.pad(key_weight, ((0, 0), (0, filler)))
    wide_value = jnp.pad(value_weight, ((0, 0), (0, filler)))
    normed_one, query_rows, key_rows, value_rows, heads, log_totals, part = attention(
        leading_sequence_length, tokens, gain_one[None], w_query, wide_key, wide_value, w_out,
        cosine, sine,
    )
    part, grads_next, grads_last, near = lax.optimization_barrier(
        (part, grads_next, grads_last, near)
    )
    if pair:
        other_part = swap(part)
    else:
        other_part = (lax.psum(part.astype(f32), "tp") - part.astype(f32)).astype(low)
    turned_router = router.T
    mixed, gates, routed, payload = middle(
        share, tp_place[None], tokens, part, other_part, gain_two[None], turned_router,
        expert_ids.T, [],
    )
    weights = [own_weights, near, far, group_swap(near, 1)]

    slots = jnp.arange(4, dtype=jnp.int32)
    flipped = (slots % 2) * 2 + slots // 2
    slot_member = jnp.where(odd == 1, flipped, slots) ^ member
    places = jnp.concatenate([plane * 4 + slot_member, core[None]]).astype(jnp.int32)

    def gathered(value_rows, following, last):
        held = {0: value_rows, 1: following, planes - 1: last}
        if planes == 4:
            held[2] = line_shift(following, 1)
        else:
            for step in range(2, planes - 1):
                held[step] = line_shift(value_rows, step)
        return held

    def first_block(places):
        return 0

    def own_place(places):
        return places[4]

    def other_place(places):
        return 1 - places[4]

    held_grads = gathered(own_grads, grads_next, grads_last)
    held_rows = gathered(payload, line_shift(payload, 1), line_shift(payload, planes - 1))

    def both(array):
        if pair:
            return ((array, first_block), (swap(array[:half]), first_block))
        own, other = two_halves(array[:share])
        return ((own, first_block), (other, first_block))

    order = [1, 3, 2, 0] if planes == 4 else list(range(1, planes)) + [0]
    kept = ()
    backs = {}
    fronts = {}
    received = []
    results = None
    finished = []
    for number, step in enumerate(order):
        if step == 0:
            halves = ((routed, own_place), (routed, other_place))
            grad_pair = ((cotangent, own_place), (cotangent, other_place))
        else:
            rows, grads = held_rows[step], held_grads[step]
            if number >= 2:
                rows, grads, unused = lax.optimization_barrier((rows, grads, finished[-1]))
            halves, grad_pair = both(rows), both(grads)
        if step == 0 or not pair:
            source = payload if step == 0 else rows
            gate_rows = (source[share:], first_block)
        else:
            gate_rows = (rows, lambda places: half // experts)
        waited = []
        finished.append(None if results is None else results[5])
        results = expert_block(
            places, halves, grad_pair, gate_rows, weights, number, (planes, length, experts),
            kept, waited,
        )
        kept = results[:5]
        backs[step] = sum_payload(results[5], results[6], half)
        fronts[step] = (results[7], results[8])
        if step:
            received.append(line_shift(backs[step], planes - step))

    back_sum = backs[0].astype(f32)
    for arrived in received:
        back_sum = back_sum + arrived.astype(f32)
    back_sum = back_sum.astype(low)
    front_parts = [sum_halves(*fronts[step]) for step in range(planes)]
    weight_products = products(*kept)
    *tied, back_sum = lax.optimization_barrier((*weight_products, *front_parts, back_sum))
    wide_kept, wide_sent, down_kept, down_sent = tied[:4]
    front_parts = tied[4:]
    front_arrived = [
        line_shift(front_parts[step], planes - step) for step in range(1, planes)
    ]
    wide_sent = group_swap(wide_sent, 1)
    down_sent = group_swap(down_sent, 1)
    if pair:
        other_sum = swap(back_sum)
        moe, other_moe = back_sum[:half], other_sum[:half]
        part_rows, other_part_rows = back_sum[half:], other_sum[half:]
    else:
        moe, other_moe = two_halves(back_sum[:share])
        part_sum = lax.psum(join_high_low(back_sum[share:], length), "tp")
        part_rows = jnp.concatenate(high_low(part_sum), axis=1)
        other_part_rows = jnp.zeros_like(part_rows)
    grad_mixed, grad_attended, shared_grads = turn(
        core[None], moe, other_moe, part_rows, other_part_rows, mixed, gain_two[None], gates,
        turned_router, cotangent, heads,
    )
    grad_three = attention_grad(
        leading_sequence_length, query_rows, key_rows, value_rows, grad_attended, w_out,
        log_totals, cosine, sine,
    )

    front_first, front_last = front_arrived[0], front_arrived[-1]
    wide_sent, down_sent, grad_three, shared_grads, front_first, front_last = (
        lax.optimization_barrier(
            (wide_sent, down_sent, grad_three, shared_grads, front_first, front_last)
        )
    )
    front_arrived = [front_first] + front_arrived[1:-1] + [front_last]
    weight_grads = over_rows(normed_one, grad_three)
    groups = [[weight_grads, shared_grads]]
    if weight_grads.shape[1] != width:
        groups = [[weight_grads], [shared_grads]]
    sums = [group_sum(group) for group in groups]
    tied, front_arrived = lax.optimization_barrier((sums, front_arrived))
    totals = [line_total(group) for group in tied]
    front_sum = front_parts[0].astype(f32)
    for arrived in front_arrived:
        front_sum = front_sum + arrived.astype(f32)
    output = (mixed + absolute_rows(front_sum.astype(low)).astype(f32)).astype(low)

    def expert_grad(held, sent, axis):
        quarter = held.shape[axis] // 2
        late = lax.slice_in_dim(held, quarter, 2 * quarter, axis=axis) + lax.slice_in_dim(
            sent, quarter, 2 * quarter, axis=axis
        ).astype(f32)
        late = group_swap(late.astype(low), 0)
        return (
            lax.slice_in_dim(held, 0, quarter, axis=axis)
            + lax.slice_in_dim(sent, 0, quarter, axis=axis).astype(f32)
            + late.astype(f32)
        )

    wide_grads = expert_grad(wide_kept, wide_sent, 2)
    down_grads = expert_grad(down_kept, down_sent, 0)

    results = []
    for group, total in zip(groups, totals):
        results += everywhere(total, [array.shape[0] // (4 * planes) for array in group])
    weight_grads, shared_grads = results
    grad_out_proj = shared_grads[:q_width]
    grad_router = shared_grads[q_width : q_width + experts].T
    grad_gain_two = shared_grads[q_width + experts]
    three_weights = jnp.concatenate([w_query, wide_key, wide_value], axis=1)
    grad_normed_one = over_last(grad_three, three_weights)
    grad_normed_one = tp_sum(grad_normed_one.astype(low)).astype(f32)
    x_full = tokens.astype(f32)
    scale_one = norm_scale(x_full)
    grad_input_norm, unused_grad = norm_backward(x_full, scale_one, gain_one, grad_normed_one)
    grad_tokens = (grad_mixed + grad_input_norm).astype(low)
    grad_gain_one = tp_sum(jnp.sum(three_weights.astype(f32) * weight_grads, axis=1)) / gain_one
    key_start = q_width
    value_start = q_width + k_width + filler
    return (
        output,
        grad_tokens,
        grad_gain_one,
        weight_grads[:, :q_width],
        weight_grads[:, key_start : key_start + k_width],
        weight_grads[:, value_start : value_start + k_width],
        grad_out_proj,
        grad_gain_two,
        grad_router,
        wide_grads[0][None],
        wide_grads[1][None],
        down_grads[None],
    )


def solution(mesh):
    placed = (
        P("ex", None),
        P("ex", None),
        P(),
        P(None, "tp"),
        P(None, "tp"),
        P(None, "tp"),
        P("tp", None),
        P(),
        P(),
        P("ex", None, "tp"),
        P("ex", None, "tp"),
        P("ex", "tp", None),
        P("ex", None),
        P("ex"),
    )
    return jax.shard_map(
        shards,
        mesh=mesh,
        in_specs=placed,
        out_specs=(
            P("ex", None),
            P("ex", None),
            P(),
            P(None, "tp"),
            P(None, "tp"),
            P(None, "tp"),
            P("tp", None),
            P(),
            P(),
            P("ex", None, "tp"),
            P("ex", None, "tp"),
            P("ex", "tp", None),
        ),
        check_vma=False,
    )
```

```python
import functools

import jax
import jax.numpy as jnp
from jax import lax
from jax.experimental import pallas as pl
from jax.experimental.pallas import tpu as pltpu
from jax.sharding import PartitionSpec as P

HEAD_SIZE = 64


EPS = 1e-06
THETA = 10000.0
NEGATIVE = -1e30
HIGH = lax.Precision.HIGHEST


def norm_scale(value_rows):
    return lax.rsqrt(jnp.mean(value_rows * value_rows, axis=-1, keepdims=True) + EPS)


def norm_backward(value_rows, scale, gain, grad):
    weighted = grad * gain
    inner = jnp.mean(weighted * value_rows, axis=-1, keepdims=True)
    grad_input = scale * weighted - value_rows * scale * scale * scale * inner
    grad_gain = jnp.sum(grad * value_rows * scale, axis=0)
    return (grad_input, grad_gain)


def rope_tables(length, split, width):
    index = jnp.arange(length, dtype=jnp.int32)
    place = jnp.where(index >= split, index - split, index).astype(jnp.float32)
    freq = THETA ** (-(jnp.arange(width // 2, dtype=jnp.float32) * 2.0 / width))
    angle = place[:, None] * freq[None, :]
    cosine = jnp.cos(angle)
    sine = jnp.sin(angle)
    return (
        jnp.concatenate([cosine] * 4, axis=1),
        jnp.concatenate([-sine, sine, -sine, sine], axis=1),
    )


BITS = (1, 2)


def swap(rows):
    return lax.ppermute(rows, "tp", [(0, 1), (1, 0)])


def tp_sum(part):
    if lax.axis_size("tp") == 2:
        return part + swap(part)
    return lax.psum(part, "tp")


def two_halves(own):
    if lax.axis_size("tp") == 2:
        return (own, swap(own))
    whole = lax.all_gather(own, "tp", axis=0, tiled=True)
    half = whole.shape[0] // 2
    return (whole[:half], whole[half:])


def sum_halves(kept, sent):
    if lax.axis_size("tp") == 2:
        return kept + swap(sent)
    whole = jnp.concatenate([kept, sent], axis=0)
    return lax.psum_scatter(whole, "tp", scatter_dimension=0, tiled=True)


def sum_payload(kept, sent, half):
    if lax.axis_size("tp") == 2:
        return kept + swap(sent)
    total = sum_halves(kept[:half], sent[:half])
    return jnp.concatenate([total, kept[half:]], axis=0)


def absolute_rows(own):
    if lax.axis_size("tp") == 2:
        other = swap(own)
        first = lax.axis_index("tp") == 0
        return jnp.concatenate(
            [jnp.where(first, own, other), jnp.where(first, other, own)], axis=0
        )
    return lax.all_gather(own, "tp", axis=0, tiled=True)


def group_pairs(turn):
    ex = lax.axis_size("ex")
    tp = lax.axis_size("tp")
    pairs = []
    for place in range(ex):
        for core in range(tp):
            bit = BITS[(turn + core) % 2]
            pairs.append((place * tp + core, (place ^ bit) * tp + core))
    return pairs


def group_swap(value_rows, turn):
    return lax.ppermute(value_rows, ("ex", "tp"), group_pairs(turn))


def line_shift(value_rows, step):
    ex = lax.axis_size("ex")
    moved = 4 * step
    return lax.ppermute(value_rows, "ex", [(place, (place - moved) % ex) for place in range(ex)])


def group_bit(turn):
    bit = jnp.where((lax.axis_index("tp") + turn) % 2 == 0, BITS[0], BITS[1])
    return ((lax.axis_index("ex") & bit) != 0).astype(jnp.int32)


def cut_rows(array, place, size):
    return lax.dynamic_slice_in_dim(array, place * size, size, 0)


def group_sum(arrays):
    for turn in (1, 0):
        halves = [array.shape[0] // 2 for array in arrays]
        bit = group_bit(turn)
        sent = [
            cut_rows(array, 1 - bit, half).astype(jnp.bfloat16)
            for array, half in zip(arrays, halves)
        ]
        sent = group_swap(jnp.concatenate(sent, axis=0), turn)
        start = 0
        totals = []
        for array, half in zip(arrays, halves):
            arrived = sent[start : start + half].astype(jnp.float32)
            totals.append(cut_rows(array, bit, half) + arrived)
            start += half
        arrays = totals
    return arrays


def line_total(arrays):
    planes = lax.axis_size("ex") // 4
    plane = lax.axis_index("ex") // 4
    shares = [array.shape[0] // planes for array in arrays]
    lows = [array.astype(jnp.bfloat16) for array in arrays]

    def piece(place):
        return jnp.concatenate(
            [cut_rows(low, place, share) for low, share in zip(lows, shares)], axis=0
        )

    total = jnp.concatenate(
        [cut_rows(array, plane, share) for array, share in zip(arrays, shares)], axis=0
    )
    for step in range(1, planes):
        arrived = line_shift(piece(lax.rem(plane + planes - step, planes)), step)
        total = total + arrived.astype(jnp.float32)
    return total.astype(jnp.bfloat16)


def everywhere(total, shares):
    planes = lax.axis_size("ex") // 4
    plane = lax.axis_index("ex") // 4
    share = total.shape[0]
    rows = jnp.zeros((planes * share, total.shape[1]), total.dtype)
    rows = lax.dynamic_update_slice_in_dim(rows, total, plane * share, 0)
    for step in range(1, planes):
        source = lax.rem(plane + step, planes)
        rows = lax.dynamic_update_slice_in_dim(rows, line_shift(total, step), source * share, 0)
    for turn in range(2):
        first = group_bit(turn) == 0
        other = group_swap(rows, turn)
        rows = jnp.concatenate(
            [jnp.where(first, rows, other), jnp.where(first, other, rows)], axis=0
        )
    rows = rows.reshape(4 * planes, share, total.shape[1])
    results = []
    start = 0
    for size in shares:
        part = rows[:, start : start + size].astype(jnp.float32)
        results.append(part.reshape(4 * planes * size, total.shape[1]))
        start += size
    return results


def over_rows(left, right):
    return lax.dot_general(
        left, right, (((0,), (0,)), ((), ())), preferred_element_type=jnp.float32
    )


def over_last(left, right):
    return lax.dot_general(
        left, right, (((1,), (1,)), ((), ())), preferred_element_type=jnp.float32
    )


def half_turn(block):
    lanes = lax.broadcasted_iota(jnp.int32, block.shape, 1)
    return jnp.where(lanes % 64 < 32, pltpu.roll(block, 96, 1), pltpu.roll(block, 32, 1))


def both_halves(block, which):
    lanes = lax.broadcasted_iota(jnp.int32, block.shape, 1)
    turned = pltpu.roll(block, 64, 1)
    return jnp.where((lanes < 64) == (which == 0), block, turned)


def set_mask(split, mask):
    keys = lax.broadcasted_iota(jnp.int32, mask.shape, 0)
    queries = lax.broadcasted_iota(jnp.int32, mask.shape, 1)
    allowed = (keys <= queries) & ((keys >= split) | (queries < split))
    mask[...] = jnp.where(allowed, 0.0, NEGATIVE)


def attention_kernel(
    split,
    tokens,
    gain,
    w_query,
    key_weight,
    value_weight,
    w_out,
    cosine,
    sine,
    normed_out,
    query_out,
    key_out,
    value_out,
    heads_out,
    totals_out,
    part_out,
    mask,
):
    length = tokens.shape[0]
    factor = float(HEAD_SIZE) ** (-0.5)
    f32 = jnp.float32
    low = jnp.bfloat16
    set_mask(split[0], mask)
    rows = tokens[...].astype(f32)
    normed = (rows * norm_scale(rows) * gain[...]).astype(low)
    normed_out[...] = normed
    query = jnp.dot(normed, w_query[...], preferred_element_type=f32)
    key = jnp.dot(normed, key_weight[...], preferred_element_type=f32)
    value = jnp.dot(normed, value_weight[...], preferred_element_type=f32)
    value_out[...] = value.astype(low)
    keys = []
    turned_values = []
    for index in range(key.shape[1] // 128):
        block = key[:, index * 128 : (index + 1) * 128]
        block = (block * cosine[...] + half_turn(block) * sine[...]).astype(low)
        key_out[:, index * 128 : (index + 1) * 128] = block
        keys.append(block.astype(f32))
        turned_values.append(value[:, index * 128 : (index + 1) * 128].T.astype(low))
    lanes = lax.broadcasted_iota(jnp.int32, (length, 128), 1)
    tile = length // 2
    for index in range(query.shape[1] // 128):
        block = query[:, index * 128 : (index + 1) * 128]
        block = block * cosine[...] + half_turn(block) * sine[...]
        query_out[:, index * 128 : (index + 1) * 128] = block.astype(low)
        shared = both_halves(keys[index // 2], index % 2).astype(low)
        turned = turned_values[index // 2][index % 2 * 64 : index % 2 * 64 + 64]
        columns = []
        for place in range(2):
            masked = jnp.where((lanes < 64) == (place == 0), block, 0.0).astype(low)
            pieces = []
            for number in range(2):
                start, end = number * tile, (number + 1) * tile
                scores = over_last(shared[:end], masked[start:end])
                scores = scores * factor + mask[:end, start:end]
                largest = jnp.max(scores, axis=0, keepdims=True)
                weights = jnp.exp(scores - largest)
                total = jnp.sum(weights, axis=0, keepdims=True)
                probs = (weights * (1.0 / total)).astype(low)
                pieces.append(jnp.dot(turned[:, :end], probs, preferred_element_type=f32))
                totals_out[2 * index + place : 2 * index + place + 1, start:end] = (
                    largest + jnp.log(total)
                )
            columns.append(jnp.concatenate(pieces, axis=1))
        heads = jnp.concatenate(columns, axis=0).T
        heads_out[:, index * 128 : (index + 1) * 128] = heads.astype(low)
    part = jnp.dot(heads_out[...], w_out[...], preferred_element_type=f32)
    part_out[...] = part.astype(low)


def attention(split, tokens, gain, w_query, key_weight, value_weight, w_out, cosine, sine):
    length, width = tokens.shape
    q_width = w_query.shape[1]
    k_width = key_weight.shape[1]
    low = jnp.bfloat16
    whole = pl.BlockSpec(memory_space=pltpu.VMEM)
    return pl.pallas_call(
        attention_kernel,
        out_shape=[
            jax.ShapeDtypeStruct((length, width), low),
            jax.ShapeDtypeStruct((length, q_width), low),
            jax.ShapeDtypeStruct((length, k_width), low),
            jax.ShapeDtypeStruct((length, k_width), low),
            jax.ShapeDtypeStruct((length, q_width), low),
            jax.ShapeDtypeStruct((q_width // HEAD_SIZE, length), jnp.float32),
            jax.ShapeDtypeStruct((length, width), low),
        ],
        in_specs=[pl.BlockSpec(memory_space=pltpu.SMEM)] + [whole] * 8,
        out_specs=[whole] * 7,
        scratch_shapes=[pltpu.VMEM((length, length), jnp.float32)],
        compiler_params=pltpu.CompilerParams(vmem_limit_bytes=48 * 1024 * 1024),
        cost_estimate=pl.CostEstimate(flops=1000000, bytes_accessed=1000000, transcendentals=0),
        name="attention",
    )(split, tokens, gain, w_query, key_weight, value_weight, w_out, cosine, sine)


def attention_grad_kernel(
    split,
    query,
    key,
    value,
    grad_attended,
    w_out,
    totals,
    cosine,
    sine,
    grad_out,
    mask,
):
    length = query.shape[0]
    grad_heads = over_last(grad_attended[...], w_out[...]).astype(jnp.bfloat16)
    factor = float(HEAD_SIZE) ** (-0.5)
    f32 = jnp.float32
    low = jnp.bfloat16
    set_mask(split[0], mask)
    lanes = lax.broadcasted_iota(jnp.int32, (length, 128), 1)
    tile = length // 2
    q_width = query.shape[1]
    k_width = key.shape[1]

    def turn_back(block):
        return (block * cosine[...] - half_turn(block) * sine[...]).astype(low)

    held = None
    for index in range(q_width // 128):
        block = query[:, index * 128 : (index + 1) * 128].astype(f32)
        grads = grad_heads[:, index * 128 : (index + 1) * 128].astype(f32)
        pair = slice(index // 2 * 128, index // 2 * 128 + 128)
        key_block = key[:, pair].astype(f32)
        keys = both_halves(key_block, index % 2).astype(low)
        values = both_halves(value[:, pair].astype(f32), index % 2).astype(low)
        turned = key_block.T[index % 2 * 64 : index % 2 * 64 + 64].astype(low)
        columns = []
        grad_key = [0.0, 0.0]
        grad_value = [0.0, 0.0]
        for place in range(2):
            mine = (lanes < 64) == (place == 0)
            masked = jnp.where(mine, block, 0.0).astype(low)
            masked_grads = jnp.where(mine, grads, 0.0).astype(low)
            pieces = []
            for number in range(2):
                start, end = number * tile, (number + 1) * tile
                part = masked[start:end]
                part_grads = masked_grads[start:end]
                scores = over_last(keys[:end], part) * factor + mask[:end, start:end]
                spot = 2 * index + place
                probs = jnp.exp(scores - totals[spot : spot + 1, start:end])
                grad_probs = over_last(values[:end], part_grads)
                inner = jnp.sum(probs * grad_probs, axis=0, keepdims=True)
                grad_scores = (probs * (grad_probs - inner) * factor).astype(low)
                pieces.append(jnp.dot(turned[:, :end], grad_scores, preferred_element_type=f32))
                some_value = jnp.dot(probs.astype(low), part_grads, preferred_element_type=f32)
                some_key = jnp.dot(grad_scores, part, preferred_element_type=f32)
                for row in range(number + 1):
                    cut = slice(row * tile, (row + 1) * tile)
                    grad_value[row] = grad_value[row] + some_value[cut]
                    grad_key[row] = grad_key[row] + some_key[cut]
            columns.append(jnp.concatenate(pieces, axis=1))
        grad_query = jnp.concatenate(columns, axis=0).T
        grad_out[:, index * 128 : (index + 1) * 128] = turn_back(grad_query)
        sums = []
        for total in (grad_key, grad_value):
            total = jnp.concatenate(total, axis=0)
            sums.append(total + pltpu.roll(total, 64, 1))
        if index % 2 == 1:
            sums = [jnp.where(lanes < 64, old, new) for old, new in zip(held, sums)]
        held = sums
        if index % 2 == 1 or index == q_width // 128 - 1:
            left = q_width + index // 2 * 128
            grad_out[:, left : left + 128] = turn_back(sums[0])
            grad_out[:, left + k_width : left + k_width + 128] = sums[1].astype(low)


def attention_grad(split, query, key, value, grad_attended, w_out, totals, cosine, sine):
    length, q_width = query.shape
    whole = pl.BlockSpec(memory_space=pltpu.VMEM)
    return pl.pallas_call(
        attention_grad_kernel,
        out_shape=jax.ShapeDtypeStruct((length, q_width + 2 * key.shape[1]), jnp.bfloat16),
        in_specs=[pl.BlockSpec(memory_space=pltpu.SMEM)] + [whole] * 8,
        out_specs=whole,
        scratch_shapes=[pltpu.VMEM((length, length), jnp.float32)],
        compiler_params=pltpu.CompilerParams(vmem_limit_bytes=48 * 1024 * 1024),
        cost_estimate=pl.CostEstimate(flops=1000000, bytes_accessed=1000000, transcendentals=0),
        name="attention_grad",
    )(split, query, key, value, grad_attended, w_out, totals, cosine, sine)


def high_low(values):
    high = values.astype(jnp.bfloat16)
    rest = (values - high.astype(jnp.float32)).astype(jnp.bfloat16)
    return (high, rest)


def join_high_low(rows, length):
    wide = rows.astype(jnp.float32)
    return wide[:, :length] + wide[:, length : 2 * length]


def middle_kernel(share, place, tokens, part, other, gain, router, ids, *rest):
    mixed_out, gates_out, routed_out, payload_out, routed = rest[-5:]
    length = tokens.shape[0]
    experts = router.shape[0]
    mixed = tokens[...].astype(jnp.float32) + (
        part[...].astype(jnp.float32) + other[...].astype(jnp.float32)
    )
    mixed_out[...] = mixed
    normed = mixed * norm_scale(mixed) * gain[...]
    routed[...] = normed.astype(jnp.bfloat16)
    routed_out[...] = routed[...]
    logits = lax.dot_general(
        router[...], normed, (((1,), (1,)), ((), ())), precision=HIGH,
        preferred_element_type=jnp.float32,
    )
    names = lax.broadcasted_iota(jnp.int32, (experts, length), 0)
    chosen = names == ids[0:1, :]
    for index in range(1, ids.shape[0]):
        chosen = chosen | (names == ids[index : index + 1, :])
    masked = jnp.where(chosen, logits, NEGATIVE)
    weights = jnp.exp(masked - jnp.max(masked, axis=0, keepdims=True))
    weights = jnp.where(chosen, weights, 0.0)
    gates = weights / jnp.sum(weights, axis=0, keepdims=True)
    gates_out[...] = gates
    payload_out[:share, :] = routed[pl.ds(pl.multiple_of(place[0] * share, share), share), :]
    high, low = high_low(gates)
    payload_out[share:, :length] = high
    payload_out[share:, length : 2 * length] = low


def middle(share, place, tokens, part, other, gain, router, ids, waited):
    length, width = tokens.shape
    experts = router.shape[0]
    whole = pl.BlockSpec(memory_space=pltpu.VMEM)
    anywhere = pl.BlockSpec(memory_space=pl.ANY)
    return pl.pallas_call(
        functools.partial(middle_kernel, share),
        out_shape=[
            jax.ShapeDtypeStruct((length, width), jnp.float32),
            jax.ShapeDtypeStruct((experts, length), jnp.float32),
            jax.ShapeDtypeStruct((length, width), jnp.bfloat16),
            jax.ShapeDtypeStruct((share + experts, width), jnp.bfloat16),
        ],
        in_specs=[pl.BlockSpec(memory_space=pltpu.SMEM)] + [whole] * 6 + [anywhere] * len(waited),
        out_specs=[whole] * 4,
        scratch_shapes=[pltpu.VMEM((length, width), jnp.bfloat16)],
        compiler_params=pltpu.CompilerParams(vmem_limit_bytes=32 * 1024 * 1024),
        cost_estimate=pl.CostEstimate(flops=1000000, bytes_accessed=1000000, transcendentals=0),
        name="middle",
    )(place, tokens, part, other, gain, router, ids, *waited)


def turn_kernel(
    place,
    moe,
    other_moe,
    part_rows,
    other_part_rows,
    mixed_ref,
    gain,
    gates_ref,
    router,
    cotangent,
    heads,
    mixed_out,
    attended_out,
    shared_out,
    grad_normed,
):
    half, width = moe.shape
    length = 2 * half
    experts = router.shape[0]
    q_width = heads.shape[1]
    f32 = jnp.float32
    grad_normed[pl.ds(pl.multiple_of(place[0] * half, half), half), :] = moe[...].astype(f32)
    grad_normed[pl.ds(pl.multiple_of((1 - place[0]) * half, half), half), :] = other_moe[
        ...
    ].astype(f32)
    gate_grads = join_high_low(part_rows[...], length) + join_high_low(
        other_part_rows[...], length
    )
    gates = gates_ref[...]
    grad_logits = gates * (gate_grads - jnp.sum(gates * gate_grads, axis=0, keepdims=True))
    mixed = mixed_ref[...]
    scale = norm_scale(mixed)
    scaled = mixed * scale
    normed = scaled * gain[...]
    grad_router = jnp.dot(grad_logits, normed, precision=HIGH, preferred_element_type=f32)
    padded = jnp.concatenate([grad_logits, jnp.zeros((128 - experts, length), f32)], axis=0)
    wide_router = jnp.concatenate([router[...], jnp.zeros((128 - experts, width), f32)], axis=0)
    grad = grad_normed[...] + jnp.dot(
        padded.T, wide_router, precision=HIGH, preferred_element_type=f32
    )
    weighted = grad * gain[...]
    inner = jnp.mean(weighted * mixed, axis=-1, keepdims=True)
    grad_mixed = (
        cotangent[...].astype(f32) + scale * weighted - scaled * (scale * scale) * inner
    )
    mixed_out[...] = grad_mixed
    attended = grad_mixed.astype(jnp.bfloat16)
    attended_out[...] = attended
    shared_out[:q_width, :] = jnp.dot(
        heads[...].astype(f32).T.astype(jnp.bfloat16), attended, preferred_element_type=f32
    )
    shared_out[q_width : q_width + experts, :] = grad_router
    lines = lax.broadcasted_iota(jnp.int32, (64 - experts, 1), 0)
    gain_grad = jnp.sum(grad * scaled, axis=0, keepdims=True)
    shared_out[q_width + experts :, :] = jnp.where(lines == 0, gain_grad, 0.0)


def turn(place, moe, other_moe, part_rows, other_part_rows, mixed, gain, gates, router, cotangent,
         heads):
    length, width = mixed.shape
    q_width = heads.shape[1]
    whole = pl.BlockSpec(memory_space=pltpu.VMEM)
    return pl.pallas_call(
        turn_kernel,
        out_shape=[
            jax.ShapeDtypeStruct((length, width), jnp.float32),
            jax.ShapeDtypeStruct((length, width), jnp.bfloat16),
            jax.ShapeDtypeStruct((q_width + 64, width), jnp.float32),
        ],
        in_specs=[pl.BlockSpec(memory_space=pltpu.SMEM)] + [whole] * 10,
        out_specs=[whole] * 3,
        scratch_shapes=[pltpu.VMEM((length, width), jnp.float32)],
        compiler_params=pltpu.CompilerParams(vmem_limit_bytes=40 * 1024 * 1024),
        cost_estimate=pl.CostEstimate(flops=1000000, bytes_accessed=1000000, transcendentals=0),
        name="turn",
    )(place, moe, other_moe, part_rows, other_part_rows, mixed, gain, gates, router, cotangent,
      heads)


def expert_kernel(places, own_rows, other_rows, own_grads, other_grads, gate_rows, *rest):
    weights = rest[:4]
    (
        rows_out,
        grads_out,
        hidden_out,
        gate_out,
        up_out,
        back_kept,
        back_sent,
        front_kept,
        front_sent,
        back_total,
        front_total,
        gate_columns,
    ) = rest[-12:]
    core = places[4]
    half = own_rows.shape[0]
    length = 2 * half
    experts = gate_rows.shape[0]
    units = weights[0].shape[1]
    low = jnp.bfloat16
    f32 = jnp.float32
    mine = pl.multiple_of(core * half, half)
    theirs = pl.multiple_of((1 - core) * half, half)
    rows_out[0, pl.ds(mine, half), :] = own_rows[...]
    rows_out[0, pl.ds(theirs, half), :] = other_rows[...]
    grads_out[0, pl.ds(mine, half), :] = own_grads[...]
    grads_out[0, pl.ds(theirs, half), :] = other_grads[...]
    gates = join_high_low(gate_rows[...], length)
    filler = jnp.zeros((128 - experts, length), f32)
    gate_columns[...] = jnp.concatenate([gates, filler], axis=0).T
    rows = rows_out[0]
    grads = grads_out[0]
    lanes = lax.broadcasted_iota(jnp.int32, (length, 128), 1)
    parts = jnp.zeros((length, 128), f32)
    for slot in range(4):
        packed = weights[slot]
        width = rows.shape[1]
        gate_w = packed.at[:width]
        up_w = packed.at[width : 2 * width]
        down_w = jnp.concatenate(
            [packed[start : start + units, :] for start in range(2 * width, 3 * width, units)],
            axis=1,
        )
        chosen = lanes == places[slot]
        gate = jnp.sum(jnp.where(chosen, gate_columns[...], 0.0), axis=1, keepdims=True)
        pre_gate = jnp.dot(rows, gate_w[...], preferred_element_type=f32)
        pre_up = jnp.dot(rows, up_w[...], preferred_element_type=f32)
        grad_plain = over_last(grads, down_w)
        sigmoid = jax.nn.sigmoid(pre_gate)
        activated = pre_gate * sigmoid
        hidden = activated * pre_up
        part = jnp.sum(hidden * grad_plain, axis=1, keepdims=True)
        parts = parts + jnp.where(chosen, part, 0.0)
        hidden_low = (hidden * gate).astype(low)
        grad_hidden = grad_plain * gate
        gate_low = (
            grad_hidden * pre_up * (sigmoid * (1.0 + pre_gate * (1.0 - sigmoid)))
        ).astype(low)
        up_low = (grad_hidden * activated).astype(low)
        columns = slice(slot * units, (slot + 1) * units)
        hidden_out[0, :, columns] = hidden_low
        gate_out[0, :, columns] = gate_low
        up_out[0, :, columns] = up_low
        back = over_last(gate_low, gate_w[...]) + over_last(up_low, up_w[...])
        front = jnp.dot(hidden_low, down_w, preferred_element_type=f32)
        if slot == 0:
            back_total[...] = back
            front_total[...] = front
        else:
            back_total[...] += back
            front_total[...] += front
    back_kept[:half, :] = back_total[pl.ds(mine, half), :].astype(low)
    back_sent[:half, :] = back_total[pl.ds(theirs, half), :].astype(low)
    front_kept[...] = front_total[pl.ds(mine, half), :].astype(low)
    front_sent[...] = front_total[pl.ds(theirs, half), :].astype(low)
    high, rest = high_low(parts.T[:experts])
    back_kept[half:, :length] = high
    back_kept[half:, length : 2 * length] = rest
    back_sent[half:, :] = jnp.zeros((experts, back_sent.shape[1]), low)


def expert_block(places, halves, grad_halves, gate_rows, weights, number, blocks, kept, waited):
    width = halves[0][0].shape[1]
    length = blocks[1]
    half = length // 2
    experts = blocks[2]
    hidden_width = 4 * weights[0].shape[1]
    low = jnp.bfloat16

    def fixed(shape):
        return pl.BlockSpec(shape, lambda step, places: (0, 0))

    def chosen(shape, spot):
        return pl.BlockSpec(shape, lambda step, places: (spot(places), 0))

    def numbered(columns):
        return pl.BlockSpec((1, length, columns), lambda step, places: (number, 0, 0))

    pairs = list(halves) + list(grad_halves)
    in_specs = [chosen((half, width), spot) for unused_array, spot in pairs]
    in_specs = in_specs + [chosen((experts, width), gate_rows[1])]
    in_specs = in_specs + [fixed(weight.shape) for weight in weights]
    loose = list(waited) + list(kept)
    in_specs = in_specs + [pl.BlockSpec(memory_space=pl.ANY)] * len(loose)
    columns = [width] * 2 + [hidden_width] * 3
    first = 1 + 5 + len(weights) + len(waited)
    return pl.pallas_call(
        expert_kernel,
        out_shape=[jax.ShapeDtypeStruct((blocks[0], length, wide), low) for wide in columns]
        + [jax.ShapeDtypeStruct((half + experts, width), low)] * 2
        + [jax.ShapeDtypeStruct((half, width), low)] * 2,
        grid_spec=pltpu.PrefetchScalarGridSpec(
            num_scalar_prefetch=1,
            grid=(1,),
            in_specs=in_specs,
            out_specs=[numbered(wide) for wide in columns]
            + [fixed((half + experts, width))] * 2
            + [fixed((half, width))] * 2,
            scratch_shapes=[
                pltpu.VMEM((length, width), jnp.float32),
                pltpu.VMEM((length, width), jnp.float32),
                pltpu.VMEM((length, 128), jnp.float32),
            ],
        ),
        input_output_aliases={first + index: index for index in range(len(kept))},
        compiler_params=pltpu.CompilerParams(vmem_limit_bytes=48 * 1024 * 1024),
        cost_estimate=pl.CostEstimate(flops=1000000, bytes_accessed=1000000, transcendentals=0),
        name="expert_block",
    )(
        places,
        *[array for array, unused_spot in pairs],
        gate_rows[0],
        *weights,
        *loose,
    )


def product_kernel(steps, rows, hidden, gate, up, grads, wide_kept, wide_sent, down_kept, down_sent,
                   turned_rows, turned_hidden):
    step = pl.program_id(0)
    blocks, length, unused = rows.shape
    low = jnp.bfloat16

    @pl.when(step == 0)
    def begin():
        for block in range(blocks):
            part = slice(block * length, (block + 1) * length)
            turned_rows[:, part] = rows[block].T
            turned_hidden[:, part] = hidden[block].T

    def product(turned, ref):
        flat = ref[...].reshape(blocks * length, ref.shape[2])
        return jnp.dot(turned[...], flat, preferred_element_type=jnp.float32)

    both = (product(turned_rows, gate), product(turned_rows, up))

    @pl.when(step < steps // 2)
    def keep():
        wide_kept[0], wide_kept[1] = both

    @pl.when(step >= steps // 2)
    def send():
        wide_sent[0], wide_sent[1] = both[0].astype(low), both[1].astype(low)

    down = product(turned_hidden, grads)
    half = down.shape[0] // 2
    down_kept[...] = down[:half]
    down_sent[...] = down[half:].astype(low)


def products(rows, grads, hidden, gate, up):
    blocks, length, width = rows.shape
    units = hidden.shape[2]
    steps = 4 if units >= 512 else 2
    half = steps // 2
    low = jnp.bfloat16
    whole = lambda columns: pl.BlockSpec((blocks, length, columns), lambda step: (0, 0, 0))
    tiled = lambda columns: pl.BlockSpec((blocks, length, columns), lambda step: (0, 0, step))
    return pl.pallas_call(
        functools.partial(product_kernel, steps),
        out_shape=[
            jax.ShapeDtypeStruct((2, width, units // 2), jnp.float32),
            jax.ShapeDtypeStruct((2, width, units // 2), low),
            jax.ShapeDtypeStruct((units // 2, width), jnp.float32),
            jax.ShapeDtypeStruct((units // 2, width), low),
        ],
        grid=(steps,),
        in_specs=[whole(width), whole(units), tiled(units // steps), tiled(units // steps),
                  tiled(width // steps)],
        out_specs=[
            pl.BlockSpec(
                (2, width, units // steps), lambda step: (0, 0, jnp.minimum(step, half - 1))
            ),
            pl.BlockSpec(
                (2, width, units // steps), lambda step: (0, 0, jnp.maximum(step - half, 0))
            ),
            pl.BlockSpec((units // 2, width // steps), lambda step: (0, step)),
            pl.BlockSpec((units // 2, width // steps), lambda step: (0, step)),
        ],
        scratch_shapes=[
            pltpu.VMEM((width, blocks * length), low),
            pltpu.VMEM((units, blocks * length), low),
        ],
        compiler_params=pltpu.CompilerParams(vmem_limit_bytes=56 * 1024 * 1024),
        cost_estimate=pl.CostEstimate(flops=1000000, bytes_accessed=1000000, transcendentals=0),
        name="products",
    )(rows, hidden, gate, up, grads)


def shards(
    tokens,
    cotangent,
    gain_one,
    w_query,
    key_weight,
    value_weight,
    w_out,
    gain_two,
    router,
    w_gate,
    w_up,
    w_down,
    expert_ids,
    leading_sequence_length,
):
    length = tokens.shape[0]
    width = tokens.shape[1]
    experts = router.shape[1]
    planes = lax.axis_size("ex") // 4
    plane = lax.axis_index("ex") // 4
    member = lax.axis_index("ex") % 4
    pair = lax.axis_size("tp") == 2
    tp_place = lax.axis_index("tp").astype(jnp.int32)
    odd = tp_place % 2
    core = odd if pair else jnp.zeros_like(odd)
    share = length // lax.axis_size("tp")
    half = length // 2
    q_width = w_query.shape[1]
    low = jnp.bfloat16
    f32 = jnp.float32

    units = w_gate.shape[2]
    own_weights = jnp.concatenate(
        [w_gate[0], w_up[0]]
        + [w_down[0][:, start : start + units] for start in range(0, width, units)],
        axis=0,
    )
    near = group_swap(own_weights, 0)
    far = group_swap(own_weights, 1)
    if pair:
        own_grads = lax.dynamic_slice_in_dim(cotangent, core * half, half, 0)
    else:
        own_grads = lax.dynamic_slice_in_dim(cotangent, tp_place * share, share, 0)
    grads_next = line_shift(own_grads, 1)
    grads_last = line_shift(own_grads, planes - 1)

    cosine, sine = rope_tables(length, leading_sequence_length[0], HEAD_SIZE)
    k_width = key_weight.shape[1]
    filler = -k_width % 128
    wide_key = jnp.pad(key_weight, ((0, 0), (0, filler)))
    wide_value = jnp.pad(value_weight, ((0, 0), (0, filler)))
    normed_one, query_rows, key_rows, value_rows, heads, log_totals, part = attention(
        leading_sequence_length, tokens, gain_one[None], w_query, wide_key, wide_value, w_out,
        cosine, sine,
    )
    part, grads_next, grads_last, near = lax.optimization_barrier(
        (part, grads_next, grads_last, near)
    )
    if pair:
        other_part = swap(part)
    else:
        other_part = (lax.psum(part.astype(f32), "tp") - part.astype(f32)).astype(low)
    turned_router = router.T
    mixed, gates, routed, payload = middle(
        share, tp_place[None], tokens, part, other_part, gain_two[None], turned_router,
        expert_ids.T, [],
    )
    weights = [own_weights, near, far, group_swap(near, 1)]

    slots = jnp.arange(4, dtype=jnp.int32)
    flipped = (slots % 2) * 2 + slots // 2
    slot_member = jnp.where(odd == 1, flipped, slots) ^ member
    places = jnp.concatenate([plane * 4 + slot_member, core[None]]).astype(jnp.int32)

    def gathered(value_rows, following, last):
        held = {0: value_rows, 1: following, planes - 1: last}
        if planes == 4:
            held[2] = line_shift(following, 1)
        else:
            for step in range(2, planes - 1):
                held[step] = line_shift(value_rows, step)
        return held

    def first_block(places):
        return 0

    def own_place(places):
        return places[4]

    def other_place(places):
        return 1 - places[4]

    held_grads = gathered(own_grads, grads_next, grads_last)
    held_rows = gathered(payload, line_shift(payload, 1), line_shift(payload, planes - 1))

    def both(array):
        if pair:
            return ((array, first_block), (swap(array[:half]), first_block))
        own, other = two_halves(array[:share])
        return ((own, first_block), (other, first_block))

    order = [1, 3, 2, 0] if planes == 4 else list(range(1, planes)) + [0]
    kept = ()
    backs = {}
    fronts = {}
    received = []
    results = None
    finished = []
    for number, step in enumerate(order):
        if step == 0:
            halves = ((routed, own_place), (routed, other_place))
            grad_pair = ((cotangent, own_place), (cotangent, other_place))
        else:
            rows, grads = held_rows[step], held_grads[step]
            if number >= 2:
                rows, grads, unused = lax.optimization_barrier((rows, grads, finished[-1]))
            halves, grad_pair = both(rows), both(grads)
        if step == 0 or not pair:
            source = payload if step == 0 else rows
            gate_rows = (source[share:], first_block)
        else:
            gate_rows = (rows, lambda places: half // experts)
        waited = []
        finished.append(None if results is None else results[5])
        results = expert_block(
            places, halves, grad_pair, gate_rows, weights, number, (planes, length, experts),
            kept, waited,
        )
        kept = results[:5]
        backs[step] = sum_payload(results[5], results[6], half)
        fronts[step] = (results[7], results[8])
        if step:
            received.append(line_shift(backs[step], planes - step))

    back_sum = backs[0].astype(f32)
    for arrived in received:
        back_sum = back_sum + arrived.astype(f32)
    back_sum = back_sum.astype(low)
    front_parts = [sum_halves(*fronts[step]) for step in range(planes)]
    weight_products = products(*kept)
    *tied, back_sum = lax.optimization_barrier((*weight_products, *front_parts, back_sum))
    wide_kept, wide_sent, down_kept, down_sent = tied[:4]
    front_parts = tied[4:]
    front_arrived = [
        line_shift(front_parts[step], planes - step) for step in range(1, planes)
    ]
    wide_sent = group_swap(wide_sent, 1)
    down_sent = group_swap(down_sent, 1)
    if pair:
        other_sum = swap(back_sum)
        moe, other_moe = back_sum[:half], other_sum[:half]
        part_rows, other_part_rows = back_sum[half:], other_sum[half:]
    else:
        moe, other_moe = two_halves(back_sum[:share])
        part_sum = lax.psum(join_high_low(back_sum[share:], length), "tp")
        part_rows = jnp.concatenate(high_low(part_sum), axis=1)
        other_part_rows = jnp.zeros_like(part_rows)
    grad_mixed, grad_attended, shared_grads = turn(
        core[None], moe, other_moe, part_rows, other_part_rows, mixed, gain_two[None], gates,
        turned_router, cotangent, heads,
    )
    grad_three = attention_grad(
        leading_sequence_length, query_rows, key_rows, value_rows, grad_attended, w_out,
        log_totals, cosine, sine,
    )

    front_first, front_last = front_arrived[0], front_arrived[-1]
    wide_sent, down_sent, grad_three, shared_grads, front_first, front_last = (
        lax.optimization_barrier(
            (wide_sent, down_sent, grad_three, shared_grads, front_first, front_last)
        )
    )
    front_arrived = [front_first] + front_arrived[1:-1] + [front_last]
    weight_grads = over_rows(normed_one, grad_three)
    groups = [[weight_grads, shared_grads]]
    if weight_grads.shape[1] != width:
        groups = [[weight_grads], [shared_grads]]
    sums = [group_sum(group) for group in groups]
    tied, front_arrived = lax.optimization_barrier((sums, front_arrived))
    totals = [line_total(group) for group in tied]
    front_sum = front_parts[0].astype(f32)
    for arrived in front_arrived:
        front_sum = front_sum + arrived.astype(f32)
    output = (mixed + absolute_rows(front_sum.astype(low)).astype(f32)).astype(low)

    def expert_grad(held, sent, axis):
        quarter = held.shape[axis] // 2
        late = lax.slice_in_dim(held, quarter, 2 * quarter, axis=axis) + lax.slice_in_dim(
            sent, quarter, 2 * quarter, axis=axis
        ).astype(f32)
        late = group_swap(late.astype(low), 0)
        return (
            lax.slice_in_dim(held, 0, quarter, axis=axis)
            + lax.slice_in_dim(sent, 0, quarter, axis=axis).astype(f32)
            + late.astype(f32)
        )

    wide_grads = expert_grad(wide_kept, wide_sent, 2)
    down_grads = expert_grad(down_kept, down_sent, 0)

    results = []
    for group, total in zip(groups, totals):
        results += everywhere(total, [array.shape[0] // (4 * planes) for array in group])
    weight_grads, shared_grads = results
    grad_out_proj = shared_grads[:q_width]
    grad_router = shared_grads[q_width : q_width + experts].T
    grad_gain_two = shared_grads[q_width + experts]
    three_weights = jnp.concatenate([w_query, wide_key, wide_value], axis=1)
    grad_normed_one = over_last(grad_three, three_weights)
    grad_normed_one = tp_sum(grad_normed_one.astype(low)).astype(f32)
    x_full = tokens.astype(f32)
    scale_one = norm_scale(x_full)
    grad_input_norm, unused_grad = norm_backward(x_full, scale_one, gain_one, grad_normed_one)
    grad_tokens = (grad_mixed + grad_input_norm).astype(low)
    grad_gain_one = tp_sum(jnp.sum(three_weights.astype(f32) * weight_grads, axis=1)) / gain_one
    key_start = q_width
    value_start = q_width + k_width + filler
    return (
        output,
        grad_tokens,
        grad_gain_one,
        weight_grads[:, :q_width],
        weight_grads[:, key_start : key_start + k_width],
        weight_grads[:, value_start : value_start + k_width],
        grad_out_proj,
        grad_gain_two,
        grad_router,
        wide_grads[0][None],
        wide_grads[1][None],
        down_grads[None],
    )


def solution(mesh):
    placed = (
        P("ex", None),
        P("ex", None),
        P(),
        P(None, "tp"),
        P(None, "tp"),
        P(None, "tp"),
        P("tp", None),
        P(),
        P(),
        P("ex", None, "tp"),
        P("ex", None, "tp"),
        P("ex", "tp", None),
        P("ex", None),
        P("ex"),
    )
    return jax.shard_map(
        shards,
        mesh=mesh,
        in_specs=placed,
        out_specs=(
            P("ex", None),
            P("ex", None),
            P(),
            P(None, "tp"),
            P(None, "tp"),
            P(None, "tp"),
            P("tp", None),
            P(),
            P(),
            P("ex", None, "tp"),
            P("ex", None, "tp"),
            P("ex", "tp", None),
        ),
        check_vma=False,
    )
```
